32 devices in a mesh: dp: 2 (over x), tile: 16 (over z, y, core).
Axes of the slice: x: 2, y: 2, z: 4, core: 2. Of those that a mesh axis runs over, the one named last changes fastest.
Arguments:
- inputs: bfloat16 [2, 256, 8, 8, 128], P('dp', 'tile'), may hold values from -6 to 6
- cotangent: bfloat16 [2, 256, 4, 4, 128], P('dp', 'tile'), may hold values from -6 to 6
- w_first: bfloat16 [1152, 128], replicated, may hold values from -0.1875 to 0.1875
- w_second: bfloat16 [1152, 128], replicated, may hold values from -0.1875 to 0.1875
- w_down: bfloat16 [512, 128], replicated, may hold values from -0.25 to 0.25
- edge_owner: int32 [256, 4], replicated, may hold values from 0 to 15, all different within a row; in each aligned block of 16 rows (0 to 15, 16 to 31, ...) at most 5 rows name the same one
- corner_owner: int32 [256, 4], replicated, may hold values from 0 to 15, all different within a row; in each aligned block of 16 rows (0 to 15, 16 to 31, ...) at most 5 rows name the same one
- neighbour_tile: int32 [256, 8], replicated, may hold values from 0 to 15
- seam_rotation: int32 [256, 8], replicated, may hold values from 0 to 3
Outputs:
- features: bfloat16 [2, 256, 4, 4, 128], P('dp', 'tile')
- input_grad: float32 [2, 256, 8, 8, 128], P('dp', 'tile')
- grad_first: float32 [1152, 128], P('dp')
- grad_second: float32 [1152, 128], P('dp')
- grad_down: float32 [512, 128], P('dp')
The draws below stay inside these ranges and needn't reach their ends.
Inputs may be any that keep to these rules, and one draw needn't show every extreme that they name: `edge_owner`: the four devices of a row differ. Among the rows of the 16 tiles of one device no device is named more than 5 times, and some device exactly 5 times. `corner_owner`: as for edge_owner.
All inputs are finite; a program needn't handle non-finite values.
Results may differ from the reference program's by a relative error of at most 0.0085.
Values may be sent and summed in bfloat16 or wider, within the bound.
No kernel may reach another device: no remote copies, remote signals or barrier semaphores. Data moves between devices by JAX's collectives and lax.ppermute only.
A program may use at most 64 MiB of HBM per device.

```python
import math
import jax
import jax.numpy as jnp
import numpy as np
from jax import lax

C = 128
S = 8
TILE_DEV = 16
TILES = 256
SAMPLES = 2
CAP = 5
N_TILE = 16


def set_ends(array, own_key, low, top_value):
    index_at = [jax.random.randint(jax.random.fold_in(own_key, axis), (), 0, length) for axis, length in enumerate(array.shape)]
    main_axis = array.shape.index(max(array.shape))
    beside = index_at[:main_axis] + [(index_at[main_axis] + 1) % array.shape[main_axis]] + index_at[main_axis + 1:]
    return array.at[tuple(index_at)].set(low).at[tuple(beside)].set(top_value)


def block_scale(key, shape, cuts, low, largest):
    def one(axis_at, blocks):
        draws = jax.random.uniform(jax.random.fold_in(jax.random.fold_in(key, 6), axis_at), (blocks,), jnp.float32, low / len(cuts), largest / len(cuts))
        return jnp.repeat(jnp.exp(draws), shape[axis_at] // blocks).reshape((-1,) + (1,) * (len(shape) - axis_at - 1))

    loudness = one(*cuts[0])
    for cut in cuts[1:]:
        loudness = loudness * one(*cut)
    return loudness


def deal_out(key, own, number, rows, number_of, top, reach, skew):
    sequence = jax.random.permutation(key, number_of)
    crowded, common = load_shares(number_of, rows * top, reach, skew, True), load_shares(number_of, rows * top, reach, skew, False)
    places = jnp.arange(number_of)

    def named(lengths, offset_by):
        used = int((lengths > 0).sum())
        fixed = max(1, used // 4)
        moved = fixed + (places - fixed + offset_by * (used - fixed)) % max(1, number_of - fixed)
        return jnp.zeros((number_of,), jnp.int32).at[sequence[jnp.where(places < fixed, places, moved)]].set(jnp.asarray(lengths, jnp.int32))

    lengths = jnp.where(number % 4 == 0, named(crowded, number // 4), named(common, number - number // 4 - 1))
    mixed = jax.random.permutation(jax.random.fold_in(own, 3), number_of)
    giver, sink = mixed[0:number_of // 2 * 2:2], mixed[1:number_of // 2 * 2:2]
    room = jnp.minimum(lengths[giver] - 1, reach - lengths[sink]) // 2
    room = jnp.where((giver == sequence[0]) | (sink == sequence[0]) | (lengths[sink] == 0), 0, jnp.maximum(room, 0))
    moved = jax.random.randint(jax.random.fold_in(own, 4), (number_of // 2,), 0, 1 << 20) % (room + 1)
    lengths = lengths.at[giver].add(-moved).at[sink].add(moved)
    items = jnp.searchsorted(jnp.cumsum(lengths), jnp.arange(rows * top), side="right").astype(jnp.int32)
    grid = items.reshape(top, rows).T
    grid = grid[jax.random.permutation(jax.random.fold_in(own, 1), rows)]
    offset_by = jax.random.randint(jax.random.fold_in(own, 2), (rows, 1), 0, top)
    return jnp.take_along_axis(grid, (jnp.arange(top)[None, :] + offset_by) % top, axis=1)


def load_shares(number_of, total, reach, lean, full):
    portions = [(1 << 20) // math.isqrt(rank ** lean) + 1 for rank in range(1, number_of + 1)]
    largest = reach if full else min(reach, max(-(-total // number_of), total * portions[0] // sum(portions)))
    least = 1 if total - largest >= number_of - 1 else 0
    counts, rest = [largest] + [least] * (number_of - 1), total - largest - least * (number_of - 1)
    while rest > 0:
        free = [i for i in range(1, number_of) if counts[i] < largest] or [i for i in range(1, number_of) if counts[i] < reach]
        whole, remaining = sum([portions[i] for i in free]), rest
        for i in free:
            more = min(reach - counts[i], max(1, remaining * portions[i] // whole), rest)
            counts[i] = counts[i] + more
            rest = rest - more
    return np.array(counts)


def centred(own_key, shape, spread, most, shards=(), kind=jnp.bfloat16):
    values = spread * jax.random.normal(own_key, shape, jnp.float32)
    if shards:
        values = values * block_scale(own_key, shape, shards, -0.22, 0.18)
    return jnp.clip(values, -most, most).astype(kind)


def setup_inputs(seed: int = 0) -> dict:
    splits = jax.random.split(jax.random.key(seed), 10)
    inputs = centred(splits[0], (SAMPLES, TILES, S, S, C), 1.0, 6.0, ((0, 2), (1, 16)))
    cotangent = centred(splits[1], (SAMPLES, TILES, S // 2, S // 2, C), 1.0, 6.0, ((0, 2), (1, 16)))
    w_first = centred(splits[2], (9 * C, C), (9 * C) ** -0.5, 0.1875)
    w_second = centred(splits[3], (9 * C, C), (9 * C) ** -0.5, 0.1875)
    w_down = centred(splits[4], (4 * C, C), (4 * C) ** -0.5, 0.25)
    edge_owner_keys = jax.random.split(jax.random.fold_in(splits[5], 1), TILES // TILE_DEV)
    edge_owner_turns = jax.random.permutation(jax.random.fold_in(splits[5], 3), TILES // TILE_DEV)
    edge_owner = jax.vmap(lambda own, number: deal_out(jax.random.fold_in(splits[5], 2), own, number, TILE_DEV, N_TILE, 4, CAP, 2))(edge_owner_keys, edge_owner_turns).reshape((TILES, 4))
    corner_owner_keys = jax.random.split(jax.random.fold_in(splits[6], 1), TILES // TILE_DEV)
    corner_owner_turns = jax.random.permutation(jax.random.fold_in(splits[6], 3), TILES // TILE_DEV)
    corner_owner = jax.vmap(lambda own, number: deal_out(jax.random.fold_in(splits[6], 2), own, number, TILE_DEV, N_TILE, 4, CAP, 2))(corner_owner_keys, corner_owner_turns).reshape((TILES, 4))
    neighbour_tile = set_ends(jax.random.randint(splits[7], (TILES, 8), 0, TILE_DEV), jax.random.fold_in(splits[7], 1), 0, TILE_DEV - 1).astype(jnp.int32)
    seam_rotation = set_ends(jax.random.randint(splits[8], (TILES, 8), 0, 4), jax.random.fold_in(splits[8], 1), 0, 3).astype(jnp.int32)
    return dict(inputs=inputs, cotangent=cotangent, w_first=w_first, w_second=w_second, w_down=w_down, edge_owner=edge_owner, corner_owner=corner_owner, neighbour_tile=neighbour_tile, seam_rotation=seam_rotation)


def rotations(tile_data):
    return jnp.stack([jnp.rot90(tile_data, quarter, axes=(0, 1)) for quarter in range(4)])

def pad_field(field, neighbour_ids, seam_rotation):

    def build(packed):
        own_tile, id_row, turn_row = packed
        turned = [rotations(field[id_row[slot]])[turn_row[slot]] for slot in range(8)]
        north_rim = turned[0][-1:, :]
        east_rim = turned[1][:, :1]
        south_rim = turned[2][:1, :]
        west_rim = turned[3][:, -1:]
        top_row = jnp.concatenate([turned[7][-1:, -1:], north_rim, turned[4][-1:, :1]], axis=1)
        middle_band = jnp.concatenate([west_rim, own_tile, east_rim], axis=1)
        bottom_row = jnp.concatenate([turned[6][:1, -1:], south_rim, turned[5][:1, :1]], axis=1)
        return jnp.concatenate([top_row, middle_band, bottom_row], axis=0)
    return lax.map(build, (field, neighbour_ids, seam_rotation))

def pad_adjoint(back_pad, neighbour_ids, seam_rotation):
    zeros_field = jnp.zeros((TILES, S, S, C), jnp.float32)
    _, pull_back = jax.vjp(lambda values: pad_field(values, neighbour_ids, seam_rotation), zeros_field)
    return pull_back(back_pad)[0]

def conv_three(padded, weight):
    running = jnp.zeros((TILES * S * S, C), jnp.float32)
    for row_off in range(3):
        for col_off in range(3):
            tap_rows = padded[:, row_off:row_off + S, col_off:col_off + S].reshape(-1, C)
            tap_start = (3 * row_off + col_off) * C
            running = running + jnp.dot(tap_rows, weight[tap_start:tap_start + C], preferred_element_type=jnp.float32)
    return running.reshape(TILES, S, S, C)

def conv_weight_grad(padded, slope):
    slope_rows = slope.reshape(-1, C)
    pieces = []
    for row_off in range(3):
        for col_off in range(3):
            tap_rows = padded[:, row_off:row_off + S, col_off:col_off + S].reshape(-1, C)
            pieces.append(jnp.dot(tap_rows.T, slope_rows, preferred_element_type=jnp.float32))
    return jnp.concatenate(pieces, axis=0)

def conv_adjoint(slope, weight):
    slope_rows = slope.reshape(-1, C)
    back_pad = jnp.zeros((TILES, S + 2, S + 2, C), jnp.float32)
    for row_off in range(3):
        for col_off in range(3):
            tap_start = (3 * row_off + col_off) * C
            contrib = jnp.dot(slope_rows, weight[tap_start:tap_start + C].T, preferred_element_type=jnp.float32)
            back_pad = back_pad.at[:, row_off:row_off + S, col_off:col_off + S].add(contrib.reshape(TILES, S, S, C))
    return back_pad

def down_blocks(hidden):
    return hidden.reshape(TILES, S // 2, 2, S // 2, 2, C)

def down_forward(hidden, w_down):
    blocks = down_blocks(hidden)
    running = jnp.zeros((TILES * (S // 2) * (S // 2), C), jnp.float32)
    for row_off in range(2):
        for col_off in range(2):
            tap_rows = blocks[:, :, row_off, :, col_off].reshape(-1, C)
            tap_start = (2 * row_off + col_off) * C
            running = running + jnp.dot(tap_rows, w_down[tap_start:tap_start + C], preferred_element_type=jnp.float32)
    return running.reshape(TILES, S // 2, S // 2, C)

def down_adjoint(cot, w_down):
    cot_rows = cot.reshape(-1, C)
    outer_list = []
    for row_off in range(2):
        inner_list = []
        for col_off in range(2):
            tap_start = (2 * row_off + col_off) * C
            contrib = jnp.dot(cot_rows, w_down[tap_start:tap_start + C].T, preferred_element_type=jnp.float32)
            inner_list.append(contrib.reshape(TILES, S // 2, S // 2, C))
        outer_list.append(jnp.stack(inner_list, axis=3))
    return jnp.stack(outer_list, axis=2).reshape(TILES, S, S, C)

def down_weight_grad(hidden, cot):
    blocks = down_blocks(hidden)
    cot_rows = cot.reshape(-1, C)
    pieces = []
    for row_off in range(2):
        for col_off in range(2):
            tap_rows = blocks[:, :, row_off, :, col_off].reshape(-1, C)
            pieces.append(jnp.dot(tap_rows.T, cot_rows, preferred_element_type=jnp.float32))
    return jnp.concatenate(pieces, axis=0)

def silu_slope(values):
    logistic = jax.nn.sigmoid(values)
    return logistic * (1.0 + values * (1.0 - logistic))

def reference(inputs, cotangent, w_first, w_second, w_down, edge_owner, corner_owner, neighbour_tile, seam_rotation):
    neighbour_ids = jnp.concatenate([edge_owner * TILE_DEV + neighbour_tile[:, :4], corner_owner * TILE_DEV + neighbour_tile[:, 4:]], axis=1).astype(jnp.int32)
    grad_scale = float(SAMPLES * TILES * S * S) ** (-0.5)
    feature_list = []
    input_list = []
    grad_one = jnp.zeros((9 * C, C), jnp.float32)
    grad_two = jnp.zeros((9 * C, C), jnp.float32)
    grad_low = jnp.zeros((4 * C, C), jnp.float32)
    for sample in range(SAMPLES):
        pad_inputs = pad_field(inputs[sample], neighbour_ids, seam_rotation)
        pre_first = conv_three(pad_inputs, w_first)
        hidden_first = jax.nn.silu(pre_first).astype(jnp.bfloat16)
        pad_hidden = pad_field(hidden_first, neighbour_ids, seam_rotation)
        pre_second = conv_three(pad_hidden, w_second)
        hidden_second = jax.nn.silu(pre_second).astype(jnp.bfloat16)
        feature_list.append(down_forward(hidden_second, w_down).astype(jnp.bfloat16))
        cot = cotangent[sample]
        grad_low = grad_low + down_weight_grad(hidden_second, cot) * grad_scale
        back_second = down_adjoint(cot, w_down)
        slope_second = (back_second * silu_slope(pre_second)).astype(jnp.bfloat16)
        grad_two = grad_two + conv_weight_grad(pad_hidden, slope_second) * grad_scale
        back_first = pad_adjoint(conv_adjoint(slope_second, w_second), neighbour_ids, seam_rotation)
        slope_first = (back_first * silu_slope(pre_first)).astype(jnp.bfloat16)
        grad_one = grad_one + conv_weight_grad(pad_inputs, slope_first) * grad_scale
        input_list.append(pad_adjoint(conv_adjoint(slope_first, w_first), neighbour_ids, seam_rotation))
    return (jnp.stack(feature_list), jnp.stack(input_list), grad_one, grad_two, grad_low)
```

```python
import functools
import jax
import jax.numpy as jnp
from jax import lax
from jax.experimental import pallas as pl
from jax.experimental.pallas import tpu as pltpu
from jax.sharding import PartitionSpec as P

F32, BF16, I32 = jnp.float32, jnp.bfloat16, jnp.int32
LANES = 128


class Sizes:
    def __init__(self, tiles, side, chan, devices, samples):
        self.tiles, self.side, self.chan = tiles, side, chan
        self.devices, self.samples = devices, samples
        self.slots = max(2, 4 * tiles // devices + 1)
        self.pair = -(-self.slots * (side + 1) // 16) * 16
        self.sent = devices * self.pair
        self.line = tiles * side
        self.pixels = side * self.line
        self.column = (side + 2) * tiles
        self.cells = 2 * self.line + 2 * self.column
        self.cells_up = -(-self.cells // LANES) * LANES
        self.tap_rows = 9 * chan // samples
        self.down_rows = 4 * chan // samples
        self.late = self.tap_rows
        self.early = self.tap_rows + self.down_rows
        self.chunk = -(-(self.early + self.late) // (16 * devices)) * 16


def iota(shape, dim):
    return lax.broadcasted_iota(I32, shape, dim)


def mm(a, b):
    return jnp.dot(a.astype(BF16), b.astype(BF16), preferred_element_type=F32)


def mm_t(a, b):
    return lax.dot_general(a, b, (((0,), (0,)), ((), ())), preferred_element_type=F32)


def flag(cond):
    return jnp.where(cond, 1.0, 0.0).astype(BF16)


def pick_rows(index, width):
    rows = index.shape[0]
    lane = iota((rows, LANES), 1)
    return jnp.concatenate([flag(index == lane + at) for at in range(0, width, LANES)], axis=1)


def pick_columns(index, height):
    shape = (height, index.shape[1])
    return flag(jnp.broadcast_to(index, shape) == iota(shape, 0))


def row_first(x):
    tiles, side, _, chan = x.shape
    x = x.astype(F32)
    return jnp.stack([x[:, r].reshape(tiles * side, chan) for r in range(side)], axis=0)


def sender_index(me, owners, local_ids, turns, z):
    requests = z.devices * z.tiles
    lane8 = iota((requests, 8), 1)
    matched = owners == me
    code = jnp.where(matched, local_ids * 16 + turns * 4 + (lane8 & 3) + 1, 0).astype(F32)
    found = jnp.where(matched, 1.0, 0.0)
    edge = lane8 < 4
    has_e = jnp.sum(jnp.where(edge, found, 0.0), axis=1, keepdims=True)
    has_c = jnp.sum(jnp.where(edge, 0.0, found), axis=1, keepdims=True)
    code_e = jnp.sum(jnp.where(edge, code, 0.0), axis=1, keepdims=True)
    code_c = jnp.sum(jnp.where(edge, 0.0, code), axis=1, keepdims=True)
    lane = iota((requests, LANES), 1)
    half = LANES // 2
    first = lane < half
    has = jnp.where(first, has_e, has_c)
    code = jnp.where(first, code_e, code_c)
    block = (z.devices, z.tiles, requests)
    own_block = (iota(block, 2) >= iota(block, 0) * z.tiles) & (
        iota(block, 2) < iota(block, 0) * z.tiles + iota(block, 1)
    )
    rank = mm(flag(own_block).reshape(requests, requests), has)
    placed = jnp.where((lane & (half - 1)).astype(F32) == rank, code, 0.0)
    group = (z.devices, requests)
    low = iota(group, 0) * z.tiles
    per_device = mm(flag((iota(group, 1) >= low) & (iota(group, 1) < low + z.tiles)), placed)
    spread = (z.devices, z.pair, z.devices)
    rows = mm(flag(iota(spread, 0) == iota(spread, 2)).reshape(z.sent, z.devices), per_device)
    cube = (z.devices, z.pair, LANES)
    at = iota(cube, 1).reshape(z.sent, LANES)
    lane = iota((z.sent, LANES), 1)
    edges = z.slots * z.side
    is_edge = at < edges
    slot = jnp.where(is_edge, lax.div(at, z.side), at - edges + half)
    wanted = (slot == lane) & (at < edges + z.slots)
    code = mm(jnp.where(wanted, rows, 0.0), jnp.ones((LANES, LANES), BF16)).astype(I32) - 1
    along = lax.rem(at, z.side)
    source, turn, towards = code >> 4, (code >> 2) & 3, code & 3
    end = z.side - 1
    i_edge = jnp.where(towards == 0, end, jnp.where(towards == 2, 0, along))
    j_edge = jnp.where(towards == 1, 0, jnp.where(towards == 3, end, along))
    i_corner = jnp.where((towards == 0) | (towards == 3), end, 0)
    j_corner = jnp.where(towards >= 2, end, 0)
    i = jnp.where(is_edge, i_edge, i_corner)
    j = jnp.where(is_edge, j_edge, j_corner)
    row = jnp.where(turn == 0, i, jnp.where(turn == 1, j, jnp.where(turn == 2, end - i, end - j)))
    col = jnp.where(turn == 0, j, jnp.where(turn == 1, end - i, jnp.where(turn == 2, end - j, i)))
    return jnp.where(code >= 0, row * z.line + source * z.side + col, -1)


def receiver_index(own_e, own_c, z):
    lane = iota((z.tiles, LANES), 1)
    lower = flag(iota((z.tiles, z.tiles), 1) < iota((z.tiles, z.tiles), 0))
    values = jnp.zeros((z.tiles, LANES), F32)
    for base, own in ((0, own_e), (8, own_c)):
        hits = [jnp.broadcast_to(own[:, k : k + 1], (z.tiles, LANES)) == lane for k in range(4)]
        named = sum(jnp.where(hit, 1.0, 0.0) for hit in hits)
        before = mm(lower, named)
        for k in range(4):
            rank = jnp.sum(jnp.where(hits[k], before, 0.0), axis=1, keepdims=True)
            values = jnp.where(lane == base + k, own[:, k : k + 1].astype(F32), values)
            values = jnp.where(lane == base + 4 + k, rank, values)
    ones = jnp.ones((LANES, LANES), BF16)

    def spread(tile, own_lane, is_edge, along):
        rows = tile.shape[0]
        lane = iota((rows, LANES), 1)
        here = mm(flag(tile[:, : z.tiles] == iota((rows, z.tiles), 1)), values)
        own = mm(jnp.where(lane == own_lane, here, 0.0), ones).astype(I32)
        rank = mm(jnp.where(lane == own_lane + 4, here, 0.0), ones).astype(I32)
        return own * z.pair + jnp.where(is_edge, rank * z.side + along, z.slots * z.side + rank)

    line = (z.tiles, z.side, LANES)
    tile = iota(line, 0).reshape(z.line, LANES)
    along = iota(line, 1).reshape(z.line, LANES)
    parts = [spread(tile, k, jnp.full(tile.shape, True), along) for k in (0, 2)]
    column = (z.side + 2, z.tiles, LANES)
    row = iota(column, 0).reshape(z.column, LANES)
    tile = iota(column, 1).reshape(z.column, LANES)
    is_edge = (row > 0) & (row <= z.side)
    for edge, top, bottom in ((3, 3, 2), (1, 0, 1)):
        own_lane = jnp.where(is_edge, edge, jnp.where(row == 0, 8 + top, 8 + bottom))
        parts.append(spread(tile, own_lane, is_edge, row - 1))
    parts.append(jnp.full((z.cells_up - z.cells, LANES), -1, I32))
    return jnp.concatenate(parts, axis=0)


def as_row(index):
    return jnp.transpose(index.astype(F32))[0:8].astype(I32)


def pack_kernel(z, me_ref, eo_ref, co_ref, ids_ref, turn_ref, x_ref, send_ref, col_ref, row_ref):
    owners = jnp.concatenate([eo_ref[...], co_ref[...]], axis=1)
    index = sender_index(me_ref[0], owners, ids_ref[...], turn_ref[...], z)
    pixels = row_first(x_ref[...]).reshape(z.pixels, z.chan)
    sent = mm(pick_rows(index, z.pixels), pixels)
    send_ref[...] = sent.astype(BF16).reshape(send_ref.shape)
    col_ref[...] = index
    row_ref[...] = as_row(index)


def side_kernel(
    z, me_ref, eo_ref, co_ref, cot_ref, wd_ref, w1_ref, w2_ref, col_ref, row_ref, back_ref, cot_out, t1_ref, t2_ref
):
    mine = pl.ds(me_ref[0] * z.tiles, z.tiles)
    index = receiver_index(eo_ref[mine, :], co_ref[mine, :], z)
    col_ref[...] = index
    row_ref[...] = as_row(index)
    chan, half = z.chan, z.side // 2
    for taps, out in ((w1_ref, t1_ref), (w2_ref, t2_ref)):
        for tap in range(9):
            rows = slice(tap * chan, (tap + 1) * chan)
            out[rows, :] = jnp.transpose(taps[rows, :].astype(F32)).astype(BF16)
    cot = cot_ref[...]
    cot_out[...] = cot
    part = half * z.tiles
    for p in range(2):
        for q in range(2):
            tap = wd_ref[(2 * p + q) * chan : (2 * p + q + 1) * chan, :]
            back = lax.dot_general(cot, tap, (((1,), (1,)), ((), ())), preferred_element_type=F32)
            for i in range(half):
                back_ref[pl.ds((2 * i + p) * z.line + q, part, stride=2), :] = back[i * part : (i + 1) * part]


def padded_columns(z, center, arrived, index, west_ref, east_ref, out_ref):
    rims = mm(pick_rows(index, z.sent), arrived)
    north, south = rims[: z.line], rims[z.line : 2 * z.line]
    at = 2 * z.line
    west_ref[pl.ds(0, z.column, stride=z.side), :] = rims[at : at + z.column]
    east_ref[pl.ds(z.side - 1, z.column, stride=z.side), :] = rims[at + z.column : at + 2 * z.column]
    shape = (z.column, z.side, z.chan)
    middle = jnp.concatenate([north, center, south], axis=0).reshape(shape)
    place = iota(shape, 1)
    flat = (z.column * z.side, z.chan)
    left = jnp.where(place == 0, west_ref[...].reshape(shape), pltpu.roll(middle, 1, 1))
    right = jnp.where(place == z.side - 1, east_ref[...].reshape(shape), pltpu.roll(middle, z.side - 1, 1))
    out_ref[:, : z.chan] = left.reshape(flat).astype(BF16)
    out_ref[:, z.chan : 2 * z.chan] = middle.reshape(flat).astype(BF16)
    out_ref[:, 2 * z.chan :] = right.reshape(flat).astype(BF16)


def conv(z, columns_ref, w_ref):
    total = None
    for p in range(3):
        part = jnp.dot(
            columns_ref[p * z.line : p * z.line + z.pixels, :],
            w_ref[3 * p * z.chan : 3 * (p + 1) * z.chan, :],
            preferred_element_type=F32,
        )
        total = part if total is None else total + part
    return total


def silu_and_slope(v):
    s = 1.0 / (1.0 + jnp.exp(-v))
    return v * s, s * (1.0 + v * (1.0 - s))


def first_kernel(
    z, got_ref, cell_ref, x_ref, w_ref, pix_ref, send_ref, hidden_ref, slope_ref, columns_ref, west_ref, east_ref
):
    center = row_first(x_ref[...]).reshape(z.pixels, z.chan)
    padded_columns(z, center, got_ref[...].reshape(z.sent, z.chan), cell_ref[...], west_ref, east_ref, columns_ref)
    hidden, slope = silu_and_slope(conv(z, columns_ref, w_ref))
    hidden = hidden.astype(BF16)
    send_ref[...] = mm(pick_rows(pix_ref[...], z.pixels), hidden).astype(BF16).reshape(send_ref.shape)
    hidden_ref[...] = hidden
    slope_ref[...] = slope


def adjoint(z, slope, turned_ref, slope_ref, wide_ref):
    chan = z.chan
    shape = (z.pixels // z.side, z.side, chan)
    cube = slope.reshape(shape)
    place = iota(shape, 1)
    zero = jnp.zeros((2 * z.line, 3 * chan), BF16)
    wide_ref[: 2 * z.line, :] = zero
    wide_ref[2 * z.line + z.pixels :, :] = zero
    inner = slice(2 * z.line, 2 * z.line + z.pixels)
    after = jnp.where(place == z.side - 1, 0.0, pltpu.roll(cube, z.side - 1, 1))
    before = jnp.where(place == 0, 0.0, pltpu.roll(cube, 1, 1))
    wide_ref[inner, :chan] = after.reshape(z.pixels, chan).astype(BF16)
    wide_ref[inner, chan : 2 * chan] = slope.astype(BF16)
    wide_ref[inner, 2 * chan :] = before.reshape(z.pixels, chan).astype(BF16)
    rows = (z.side + 2) * z.line
    total = None
    for p in range(3):
        part = jnp.dot(
            wide_ref[(2 - p) * z.line : (2 - p) * z.line + rows, :],
            turned_ref[3 * p * chan : 3 * (p + 1) * chan, :],
            preferred_element_type=F32,
        )
        total = part if total is None else total + part
    slope_ref[...] = slope
    blank = jnp.zeros((2 * z.tiles, chan), F32)
    sides = []
    for start, q in ((0, 0), (z.side - 1, 2)):
        line = slope_ref[pl.ds(start, z.side * z.tiles, stride=z.side), :]
        line = jnp.concatenate([blank, line, blank], axis=0).astype(BF16)
        side = None
        for p in range(3):
            part = jnp.dot(
                line[(2 - p) * z.tiles : (2 - p) * z.tiles + z.column],
                turned_ref[(3 * p + q) * chan : (3 * p + q + 1) * chan, :],
                preferred_element_type=F32,
            )
            side = part if side is None else side + part
        sides.append(side)
    spare = jnp.zeros((z.cells_up - z.cells, chan), F32)
    rims = jnp.concatenate([total[: z.line], total[rows - z.line :]] + sides + [spare], axis=0)
    return total[z.line : z.line + z.pixels], rims.astype(BF16)


def second_kernel(
    z, got_ref, cell_ref, cell_row_ref, hidden_ref, w_ref, turned_ref, back_ref,
    send_ref, inner_ref, slope_ref, out_ref, columns_ref, west_ref, east_ref, scratch_ref, wide_ref,
):
    center = hidden_ref[...].astype(F32)
    padded_columns(z, center, got_ref[...].reshape(z.sent, z.chan), cell_ref[...], west_ref, east_ref, columns_ref)
    hidden, slope = silu_and_slope(conv(z, columns_ref, w_ref))
    out_ref[...] = hidden.astype(BF16).astype(F32)
    slope = (back_ref[...] * slope).astype(BF16)
    slope_ref[...] = slope
    inner, rims = adjoint(z, slope.astype(F32), turned_ref, scratch_ref, wide_ref)
    inner_ref[...] = inner
    send_ref[...] = mm(pick_columns(cell_row_ref[0:1, :], z.sent), rims).astype(BF16).reshape(send_ref.shape)


def tap_products(z, columns_ref, slope, scale, total_ref):
    for p in range(3):
        part = mm_t(columns_ref[p * z.line : p * z.line + z.pixels, :], slope)
        total_ref[3 * p * z.chan : 3 * (p + 1) * z.chan, :] = part * scale


def early_kernel(
    z, scale, at_ref, columns_ref, slope_ref, hidden_ref, cot_ref, wd_ref,
    feature_ref, own_ref, other_ref, total_ref, down_ref, block_ref,
):
    chan, half = z.chan, z.side // 2
    part = half * z.tiles
    tap_products(z, columns_ref, slope_ref[...], scale, total_ref)
    for i in range(half):
        for p in range(2):
            for q in range(2):
                block_ref[i * part : (i + 1) * part, (2 * p + q) * chan : (2 * p + q + 1) * chan] = hidden_ref[
                    pl.ds((2 * i + p) * z.line + q, part, stride=2), :
                ].astype(BF16)
    block = block_ref[...]
    feature_ref[...] = jnp.dot(block, wd_ref[...], preferred_element_type=F32).astype(BF16)
    down_ref[...] = mm_t(block, cot_ref[...]) * scale
    sample = at_ref[0]
    for shift in range(z.samples):
        whose = lax.rem(sample + shift, z.samples)
        taps = total_ref[pl.ds(whose * z.tap_rows, z.tap_rows), :]
        down = down_ref[pl.ds(whose * z.down_rows, z.down_rows), :]
        if shift == 0:
            own_ref[: z.tap_rows, :] = taps
            own_ref[z.tap_rows :, :] = down
        else:
            other_ref[shift - 1, : z.tap_rows, :] = taps.astype(BF16)
            other_ref[shift - 1, z.tap_rows :, :] = down.astype(BF16)


def slope_kernel(
    z, scale, at_ref, got_ref, pix_row_ref, inner_ref, slope_in_ref, columns_ref, slope_ref, own_ref, other_ref, total_ref
):
    back = inner_ref[...] + mm(pick_columns(pix_row_ref[0:1, :], z.pixels), got_ref[...].reshape(z.sent, z.chan))
    slope = (back * slope_in_ref[...]).astype(BF16)
    slope_ref[...] = slope
    tap_products(z, columns_ref, slope, scale, total_ref)
    sample = at_ref[0]
    for shift in range(z.samples):
        whose = lax.rem(sample + shift, z.samples)
        taps = total_ref[pl.ds(whose * z.tap_rows, z.tap_rows), :]
        if shift == 0:
            own_ref[...] = taps
        else:
            other_ref[shift - 1] = taps.astype(BF16)


def last_kernel(z, slope_ref, turned_ref, cell_row_ref, send_ref, inner_ref, scratch_ref, wide_ref):
    inner, rims = adjoint(z, slope_ref[...].astype(F32), turned_ref, scratch_ref, wide_ref)
    inner_ref[...] = inner
    send_ref[...] = mm(pick_columns(cell_row_ref[0:1, :], z.sent), rims).astype(BF16).reshape(send_ref.shape)


def join_kernel(z, rim_ref, early_ref, early_got_ref, late_ref, late_got_ref, send_ref, total_ref):
    early, late = early_ref[...], late_ref[...]
    for k in range(z.samples - 1):
        early = early + early_got_ref[k].astype(F32)
        late = late + late_got_ref[k].astype(F32)
    total_ref[: z.early, :] = early
    total_ref[z.early : z.early + z.late, :] = late
    spare = z.devices * z.chunk - z.early - z.late
    if spare:
        total_ref[z.early + z.late :, :] = jnp.zeros((spare, z.chan), F32)
    send_ref[:, : z.pair, :] = rim_ref[...]
    send_ref[:, z.pair :, :] = total_ref[...].astype(BF16).reshape(z.devices, z.chunk, z.chan)


def sum_kernel(z, got_ref, out_ref):
    total = got_ref[0, z.pair :, :].astype(F32)
    for k in range(1, z.devices):
        total = total + got_ref[k, z.pair :, :].astype(F32)
    total = total.astype(BF16)
    for k in range(z.devices):
        out_ref[k] = total


def input_kernel(z, got_ref, pix_row_ref, inner_ref, out_ref):
    arrived = got_ref[:, : z.pair, :].reshape(z.sent, z.chan)
    total = inner_ref[...] + mm(pick_columns(pix_row_ref[0:1, :], z.pixels), arrived)
    for r in range(z.side):
        out_ref[:, r] = total[r * z.line : (r + 1) * z.line].reshape(z.tiles, z.side, z.chan)


def spread_kernel(z, got_ref, one_ref, two_ref, low_ref):
    total = got_ref[...].astype(F32).reshape(z.devices * z.chunk, z.chan)
    two_ref[...] = total[: z.tap_rows]
    low_ref[...] = total[z.tap_rows : z.early]
    one_ref[...] = total[z.early : z.early + z.late]


def vmem(*shape, dtype=F32):
    return pltpu.VMEM(shape, dtype)


def call(body, outs, scratch=(), scalars=0, name=None):
    def run(*operands):
        spec = pl.BlockSpec(memory_space=pltpu.VMEM)
        small = pl.BlockSpec(memory_space=pltpu.SMEM)
        return pl.pallas_call(
            body,
            out_shape=[jax.ShapeDtypeStruct(shape, dtype) for shape, dtype in outs],
            in_specs=[small] * scalars + [spec] * (len(operands) - scalars),
            out_specs=[spec] * len(outs),
            scratch_shapes=list(scratch),
            compiler_params=pltpu.CompilerParams(vmem_limit_bytes=40 * 1024 * 1024),
            name=name,
        )(*operands)

    return run


def exchange(x):
    return lax.all_to_all(x, "tile", split_axis=0, concat_axis=0, tiled=True)


def to_samples(others, samples):
    got = []
    for k in range(samples - 1):
        got.append(lax.ppermute(others[k], "dp", [(s, (s + k + 1) % samples) for s in range(samples)]))
    return jnp.stack(got) if samples > 2 else got[0][None]


def local(inputs, cotangent, w_first, w_second, w_down, edge_owner, corner_owner, neighbour_tile, seam_rotation):
    tiles_in, cot = inputs[0], cotangent[0]
    tiles, side, _, chan = tiles_in.shape
    z = Sizes(tiles, side, chan, lax.axis_size("tile"), lax.axis_size("dp"))
    scale = float(z.samples * z.devices * z.pixels) ** -0.5
    me = lax.axis_index("tile").astype(I32).reshape(1)
    sample = lax.axis_index("dp").astype(I32).reshape(1)
    half = side // 2
    down_pixels = half * half * tiles
    field = ((z.pixels, chan), F32)
    field16 = ((z.pixels, chan), BF16)
    columns = ((z.column * side, 3 * chan), BF16)
    sent = ((z.devices, z.pair, chan), BF16)
    wide = vmem((side + 4) * z.line, 3 * chan, dtype=BF16)
    side_columns = (vmem(z.column * side, chan), vmem(z.column * side, chan))
    flat = vmem(z.pixels, chan)
    taps = vmem(9 * chan, chan)
    bind = functools.partial

    send, pix_col, pix_row = call(
        bind(pack_kernel, z), [sent, ((z.sent, LANES), I32), ((8, z.sent), I32)], scalars=1, name="pack"
    )(me, edge_owner, corner_owner, neighbour_tile, seam_rotation, tiles_in)
    got = exchange(send)
    cot_rows = cot.transpose(1, 0, 2, 3).reshape(down_pixels, chan)
    cell_col, cell_row, back_second, cot_rows, turned_first, turned_second = call(
        bind(side_kernel, z),
        [
            ((z.cells_up, LANES), I32),
            ((8, z.cells_up), I32),
            field,
            ((down_pixels, chan), BF16),
            ((9 * chan, chan), BF16),
            ((9 * chan, chan), BF16),
        ],
        scalars=1,
        name="aside",
    )(me, edge_owner, corner_owner, cot_rows, w_down, w_first, w_second)
    send, hidden, slope_in, columns_first = call(
        bind(first_kernel, z), [sent, field16, field, columns], side_columns, name="first"
    )(got, cell_col, tiles_in, w_first, pix_col)
    got = exchange(send)
    send, inner, slope_second, hidden_second, columns_second = call(
        bind(second_kernel, z), [sent, field, field16, field, columns], side_columns + (flat, wide), name="second"
    )(got, cell_col, cell_row, hidden, w_second, turned_second, back_second)
    got = exchange(send)
    features, early_own, early_other = call(
        bind(early_kernel, z, scale),
        [((down_pixels, chan), BF16), ((z.early, chan), F32), ((z.samples - 1, z.early, chan), BF16)],
        (taps, vmem(4 * chan, chan), vmem(down_pixels, 4 * chan, dtype=BF16)),
        scalars=1,
        name="early",
    )(sample, columns_second, slope_second, hidden_second, cot_rows, w_down)
    features = features.reshape(half, tiles, half, chan).transpose(1, 0, 2, 3)
    early_got = to_samples(early_other, z.samples)
    slope_first, late_own, late_other = call(
        bind(slope_kernel, z, scale),
        [field16, ((z.late, chan), F32), ((z.samples - 1, z.late, chan), BF16)],
        (taps,),
        scalars=1,
        name="slope",
    )(sample, got, pix_row, inner, slope_in, columns_first)
    late_got = to_samples(late_other, z.samples)
    send, inner = call(bind(last_kernel, z), [sent, field], (flat, wide), name="last")(
        slope_first, turned_first, cell_row
    )
    (send,) = call(
        bind(join_kernel, z),
        [((z.devices, z.pair + z.chunk, chan), BF16)],
        (vmem(z.devices * z.chunk, chan),),
        name="join",
    )(send, early_own, early_got, late_own, late_got)
    got = exchange(send)
    (chunk,) = call(bind(sum_kernel, z), [((z.devices, z.chunk, chan), BF16)], name="sum")(got)
    whole = exchange(chunk)
    (input_grad,) = call(bind(input_kernel, z), [((tiles, side, side, chan), F32)], name="input")(got, pix_row, inner)
    grad_first, grad_second, grad_down = call(
        bind(spread_kernel, z),
        [((z.tap_rows, chan), F32), ((z.tap_rows, chan), F32), ((z.down_rows, chan), F32)],
        name="spread",
    )(whole)
    return features[None], input_grad[None], grad_first, grad_second, grad_down


def solution(mesh):
    split = P("dp", "tile", None, None, None)
    return jax.shard_map(
        local,
        mesh=mesh,
        in_specs=(split, split, P(), P(), P(), P(), P(), P(), P()),
        out_specs=(split, split, P("dp", None), P("dp", None), P("dp", None)),
        check_vma=False,
    )
```

```python
import functools
import jax
import jax.numpy as jnp
from jax import lax
from jax.experimental import pallas as pl
from jax.experimental.pallas import tpu as pltpu
from jax.sharding import PartitionSpec as P

F32, BF16, I32 = jnp.float32, jnp.bfloat16, jnp.int32
LANES = 128


class Sizes:
    def __init__(self, tiles, side, chan, devices, samples):
        self.tiles, self.side, self.chan = tiles, side, chan
        self.devices, self.samples = devices, samples
        self.slots = max(2, 4 * tiles // devices + 1)
        self.pair = -(-self.slots * (side + 1) // 16) * 16
        self.sent = devices * self.pair
        self.line = tiles * side
        self.pixels = side * self.line
        self.column = (side + 2) * tiles
        self.cells = 2 * self.line + 2 * self.column
        self.cells_up = -(-self.cells // LANES) * LANES
        self.tap_rows = 9 * chan // samples
        self.down_rows = 4 * chan // samples
        self.late = self.tap_rows // 2
        self.early = (self.tap_rows + self.down_rows) // 2
        self.chunk = -(-(self.early + self.late) // (16 * devices)) * 16
        self.parts = [(s, c) for s in range(samples) for c in range(2)]
        self.slot_rows = -(-self.slots // 8) * 8


def iota(shape, dim):
    return lax.broadcasted_iota(I32, shape, dim)


def mm(a, b):
    return jnp.dot(a.astype(BF16), b.astype(BF16), preferred_element_type=F32)


def mm_t(a, b):
    return lax.dot_general(a, b, (((0,), (0,)), ((), ())), preferred_element_type=F32)


def flag(cond):
    return jnp.where(cond, 1.0, 0.0).astype(BF16)


def pick_rows(index, width):
    rows = index.shape[0]
    lane = iota((rows, LANES), 1)
    return jnp.concatenate([flag(index == lane + at) for at in range(0, width, LANES)], axis=1)


def pick_columns(index, height):
    shape = (height, index.shape[1])
    return flag(jnp.broadcast_to(index, shape) == iota(shape, 0))


def row_first(x):
    tiles, side, _, chan = x.shape
    x = x.astype(F32)
    return jnp.stack([x[:, r].reshape(tiles * side, chan) for r in range(side)], axis=0)


def sender_index(me, owners, local_ids, turns, z):
    requests = z.devices * z.tiles
    row8 = iota((8, requests), 0)
    matched = owners == me
    code = jnp.where(matched, local_ids * 16 + turns * 4 + (row8 & 3) + 1, 0).astype(F32)
    found = jnp.where(matched, 1.0, 0.0)

    def both(values):
        edge = jnp.sum(values[:4], axis=0, keepdims=True)
        corner = jnp.sum(values[4:], axis=0, keepdims=True)
        shape = (z.slot_rows, requests)
        return jnp.concatenate([jnp.broadcast_to(edge, shape), jnp.broadcast_to(corner, shape)], axis=0)

    column = iota((1, 1, requests), 2)
    cube = (z.devices, z.tiles, requests)
    earlier = (iota(cube, 0) == lax.div(column, z.tiles)) & (iota(cube, 1) < lax.rem(column, z.tiles))
    rank = mm(both(found), flag(earlier).reshape(requests, requests))
    slot = iota((2 * z.slot_rows, requests), 0)
    slot = jnp.where(slot < z.slot_rows, slot, slot - z.slot_rows)
    placed = jnp.where(slot.astype(F32) == rank, both(code), 0.0)
    row = iota((1, z.sent), 1)
    device, at = lax.div(row, z.pair), lax.rem(row, z.pair)
    cube = (z.devices, z.tiles, z.sent)
    rows = mm(placed, flag(iota(cube, 0) == device.reshape(1, 1, z.sent)).reshape(requests, z.sent))
    edges = z.slots * z.side
    is_edge = at < edges
    wanted = jnp.where(is_edge, lax.div(at, z.side), at - edges + z.slot_rows)
    wanted = jnp.where(at < edges + z.slots, wanted, -1)
    here = iota((2 * z.slot_rows, z.sent), 0) == wanted
    code = jnp.sum(jnp.where(here, rows, 0.0), axis=0, keepdims=True).astype(I32) - 1
    along = lax.rem(at, z.side)
    source, turn, towards = code >> 4, (code >> 2) & 3, code & 3
    end = z.side - 1
    i_edge = jnp.where(towards == 0, end, jnp.where(towards == 2, 0, along))
    j_edge = jnp.where(towards == 1, 0, jnp.where(towards == 3, end, along))
    i_corner = jnp.where((towards == 0) | (towards == 3), end, 0)
    j_corner = jnp.where(towards >= 2, end, 0)
    i = jnp.where(is_edge, i_edge, i_corner)
    j = jnp.where(is_edge, j_edge, j_corner)
    row = jnp.where(turn == 0, i, jnp.where(turn == 1, j, jnp.where(turn == 2, end - i, end - j)))
    col = jnp.where(turn == 0, j, jnp.where(turn == 1, end - i, jnp.where(turn == 2, end - j, i)))
    return jnp.where(code >= 0, row * z.line + source * z.side + col, -1)


def receiver_index(own, z):
    lane = iota((z.tiles, LANES), 1)
    lower = flag(iota((z.tiles, z.tiles), 1) < iota((z.tiles, z.tiles), 0))
    values = jnp.zeros((z.tiles, LANES), F32)
    for base in (0, 4):
        hits = [jnp.broadcast_to(own[:, base + k : base + k + 1], (z.tiles, LANES)) == lane for k in range(4)]
        named = sum(jnp.where(hit, 1.0, 0.0) for hit in hits)
        before = mm(lower, named)
        for k in range(4):
            rank = jnp.sum(jnp.where(hits[k], before, 0.0), axis=1, keepdims=True)
            values = jnp.where(lane == 2 * base + k, own[:, base + k : base + k + 1].astype(F32), values)
            values = jnp.where(lane == 2 * base + 4 + k, rank, values)
    ones = jnp.ones((LANES, LANES), BF16)

    def spread(tile, own_lane, is_edge, along):
        rows = tile.shape[0]
        lane = iota((rows, LANES), 1)
        here = mm(flag(tile[:, : z.tiles] == iota((rows, z.tiles), 1)), values)
        own = mm(jnp.where(lane == own_lane, here, 0.0), ones).astype(I32)
        rank = mm(jnp.where(lane == own_lane + 4, here, 0.0), ones).astype(I32)
        return own * z.pair + jnp.where(is_edge, rank * z.side + along, z.slots * z.side + rank)

    line = (z.tiles, z.side, LANES)
    tile = iota(line, 0).reshape(z.line, LANES)
    along = iota(line, 1).reshape(z.line, LANES)
    parts = [spread(tile, k, jnp.full(tile.shape, True), along) for k in (0, 2)]
    column = (z.side + 2, z.tiles, LANES)
    row = iota(column, 0).reshape(z.column, LANES)
    tile = iota(column, 1).reshape(z.column, LANES)
    is_edge = (row > 0) & (row <= z.side)
    for edge, top, bottom in ((3, 3, 2), (1, 0, 1)):
        own_lane = jnp.where(is_edge, edge, jnp.where(row == 0, 8 + top, 8 + bottom))
        parts.append(spread(tile, own_lane, is_edge, row - 1))
    parts.append(jnp.full((z.cells_up - z.cells, LANES), -1, I32))
    return jnp.concatenate(parts, axis=0)


def as_column(index):
    return jnp.transpose(jnp.broadcast_to(index.astype(F32), (LANES, index.shape[1]))).astype(I32)


def as_row(index):
    return jnp.transpose(index.astype(F32))[0:8].astype(I32)


def pack_kernel(z, me_ref, eo_ref, co_ref, ids_ref, turn_ref, x_ref, send_ref):
    owners = jnp.concatenate([eo_ref[...], co_ref[...]], axis=0)
    index = sender_index(me_ref[0], owners, ids_ref[...], turn_ref[...], z)
    pixels = row_first(x_ref[...]).reshape(z.pixels, z.chan)
    send_ref[...] = mm(pick_rows(as_column(index), z.pixels), pixels).astype(BF16).reshape(send_ref.shape)


def side_kernel(
    z, me_ref, eo_ref, co_ref, ids_ref, turn_ref, cot_ref, wd_ref, w1_ref, w2_ref,
    column_ref, pix_row_ref, cell_row_ref, back_ref, t1_ref, t2_ref,
):
    me = me_ref[0]
    owners = jnp.concatenate([eo_ref[...], co_ref[...]], axis=0)
    index = sender_index(me, owners, ids_ref[...], turn_ref[...], z)
    column_ref[: z.sent, :] = as_column(index)
    pix_row_ref[...] = jnp.broadcast_to(index, pix_row_ref.shape)
    shape = (z.tiles, z.devices * z.tiles)
    mine = flag(iota(shape, 1) == iota(shape, 0) + me * z.tiles)
    own = lax.dot_general(
        mine, owners.astype(F32).astype(BF16), (((1,), (1,)), ((), ())), preferred_element_type=F32
    )
    index = receiver_index(own.astype(I32), z)
    column_ref[z.sent :, :] = index
    cell_row_ref[...] = as_row(index)
    chan, half = z.chan, z.side // 2
    for taps, out in ((w1_ref, t1_ref), (w2_ref, t2_ref)):
        for tap in range(9):
            rows = slice(tap * chan, (tap + 1) * chan)
            out[rows, :] = jnp.transpose(taps[rows, :].astype(F32)).astype(BF16)
    cot = cot_ref[...]
    part = half * z.tiles
    for p in range(2):
        for q in range(2):
            tap = wd_ref[(2 * p + q) * chan : (2 * p + q + 1) * chan, :]
            back = lax.dot_general(cot, tap, (((1,), (1,)), ((), ())), preferred_element_type=F32)
            for i in range(half):
                back_ref[pl.ds((2 * i + p) * z.line + q, part, stride=2), :] = back[i * part : (i + 1) * part]


def padded_columns(z, center, arrived, index, west_ref, east_ref, out_ref):
    rims = mm(pick_rows(index, z.sent), arrived)
    north, south = rims[: z.line], rims[z.line : 2 * z.line]
    at = 2 * z.line
    west_ref[pl.ds(0, z.column, stride=z.side), :] = rims[at : at + z.column]
    east_ref[pl.ds(z.side - 1, z.column, stride=z.side), :] = rims[at + z.column : at + 2 * z.column]
    shape = (z.column, z.side, z.chan)
    middle = jnp.concatenate([north, center, south], axis=0).reshape(shape)
    place = iota(shape, 1)
    flat = (z.column * z.side, z.chan)
    left = jnp.where(place == 0, west_ref[...].reshape(shape), pltpu.roll(middle, 1, 1))
    right = jnp.where(place == z.side - 1, east_ref[...].reshape(shape), pltpu.roll(middle, z.side - 1, 1))
    out_ref[:, : z.chan] = left.reshape(flat).astype(BF16)
    out_ref[:, z.chan : 2 * z.chan] = middle.reshape(flat).astype(BF16)
    out_ref[:, 2 * z.chan :] = right.reshape(flat).astype(BF16)


def conv(z, columns_ref, w_ref):
    total = None
    for p in range(3):
        part = jnp.dot(
            columns_ref[p * z.line : p * z.line + z.pixels, :],
            w_ref[3 * p * z.chan : 3 * (p + 1) * z.chan, :],
            preferred_element_type=F32,
        )
        total = part if total is None else total + part
    return total


def silu_slope(v):
    s = 1.0 / (1.0 + jnp.exp(-v))
    return s * (1.0 + v * (1.0 - s))


def first_kernel(z, got_ref, index_ref, x_ref, w_ref, send_ref, hidden_ref, columns_ref, west_ref, east_ref):
    center = row_first(x_ref[...]).reshape(z.pixels, z.chan)
    padded_columns(z, center, got_ref[...].reshape(z.sent, z.chan), index_ref[z.sent :, :], west_ref, east_ref, columns_ref)
    v = conv(z, columns_ref, w_ref)
    hidden = (v / (1.0 + jnp.exp(-v))).astype(BF16)
    send_ref[...] = mm(pick_rows(index_ref[: z.sent, :], z.pixels), hidden).astype(BF16).reshape(send_ref.shape)
    hidden_ref[...] = hidden


def again_kernel(z, columns_ref, w_ref, slope_ref):
    slope_ref[...] = silu_slope(conv(z, columns_ref, w_ref))


def shifted(z, slope):
    cube = slope.reshape(slope.shape[0] // z.side, z.side, z.chan)
    place = iota(cube.shape, 1)
    after = jnp.where(place == z.side - 1, 0.0, pltpu.roll(cube, z.side - 1, 1))
    before = jnp.where(place == 0, 0.0, pltpu.roll(cube, 1, 1))
    return [part.reshape(slope.shape).astype(BF16) for part in (after, cube, before)]


def rims_back(z, slope, turned_ref, slope_ref):
    chan = z.chan
    parts = []
    for p, row in ((0, 0), (2, z.side - 1)):
        wide = jnp.concatenate(shifted(z, slope[row * z.line : (row + 1) * z.line]), axis=1)
        parts.append(jnp.dot(wide, turned_ref[3 * p * chan : 3 * (p + 1) * chan, :], preferred_element_type=F32))
    slope_ref[...] = slope
    blank = jnp.zeros((2 * z.tiles, chan), F32)
    for start, q in ((0, 0), (z.side - 1, 2)):
        line = slope_ref[pl.ds(start, z.side * z.tiles, stride=z.side), :]
        line = jnp.concatenate([blank, line, blank], axis=0).astype(BF16)
        side = None
        for p in range(3):
            part = jnp.dot(
                line[(2 - p) * z.tiles : (2 - p) * z.tiles + z.column],
                turned_ref[(3 * p + q) * chan : (3 * p + q + 1) * chan, :],
                preferred_element_type=F32,
            )
            side = part if side is None else side + part
        parts.append(side)
    parts.append(jnp.zeros((z.cells_up - z.cells, chan), F32))
    return jnp.concatenate(parts, axis=0).astype(BF16)


def inner_back(z, slope, turned_ref, wide_ref):
    chan = z.chan
    zero = jnp.zeros((z.line, 3 * chan), BF16)
    wide_ref[: z.line, :] = zero
    wide_ref[z.line + z.pixels :, :] = zero
    for q, part in enumerate(shifted(z, slope)):
        wide_ref[z.line : z.line + z.pixels, q * chan : (q + 1) * chan] = part
    total = None
    for p in range(3):
        part = jnp.dot(
            wide_ref[(2 - p) * z.line : (2 - p) * z.line + z.pixels, :],
            turned_ref[3 * p * chan : 3 * (p + 1) * chan, :],
            preferred_element_type=F32,
        )
        total = part if total is None else total + part
    return total


def second_kernel(
    z, got_ref, index_ref, cell_row_ref, hidden_ref, w_ref, turned_ref, back_ref,
    send_ref, slope_ref, out_ref, columns_ref, west_ref, east_ref, scratch_ref,
):
    center = hidden_ref[...].astype(F32)
    padded_columns(z, center, got_ref[...].reshape(z.sent, z.chan), index_ref[z.sent :, :], west_ref, east_ref, columns_ref)
    push(columns_ref)
    v = conv(z, columns_ref, w_ref)
    s = 1.0 / (1.0 + jnp.exp(-v))
    out_ref[...] = (v * s).astype(BF16)
    push(out_ref)
    slope = (back_ref[...] * (s * (1.0 + v * (1.0 - s)))).astype(BF16)
    slope_ref[...] = slope
    push(slope_ref)
    rims = rims_back(z, slope.astype(F32), turned_ref, scratch_ref)
    send_ref[...] = mm(pick_columns(cell_row_ref[0:1, :], z.sent), rims).astype(BF16).reshape(send_ref.shape)


def tap_products(z, columns_ref, slope, scale, total_ref):
    for p in range(3):
        part = mm_t(columns_ref[p * z.line : p * z.line + z.pixels, :], slope)
        total_ref[3 * p * z.chan : 3 * (p + 1) * z.chan, :] = part * scale


def deal_parts(z, sample_ref, me_ref, source_ref, own_ref, other_refs):
    rows = own_ref.shape[0]
    for k, (shift, core) in enumerate(z.parts):
        whose = lax.rem(sample_ref[0] + shift, z.samples)
        half = jnp.bitwise_xor(me_ref[0] & 1, core)
        part = source_ref[pl.ds((2 * whose + half) * rows, rows), :]
        if k == 0:
            own_ref[...] = part
        else:
            other_refs[k - 1][...] = part.astype(BF16)


def early_kernel(
    z, scale, sample_ref, me_ref, columns_ref, slope_ref, hidden_ref, cot_ref, wd_ref, feature_ref, own_ref, *refs
):
    other_refs, (taps_ref, total_ref, flat_ref, block_ref) = refs[:-4], refs[-4:]
    chan, half = z.chan, z.side // 2
    part = half * z.tiles
    tap_products(z, columns_ref, slope_ref[...], scale, taps_ref)
    flat_ref[...] = hidden_ref[...].astype(F32)
    for i in range(half):
        for p in range(2):
            for q in range(2):
                block_ref[i * part : (i + 1) * part, (2 * p + q) * chan : (2 * p + q + 1) * chan] = flat_ref[
                    pl.ds((2 * i + p) * z.line + q, part, stride=2), :
                ].astype(BF16)
    block = block_ref[...]
    feature_ref[...] = jnp.dot(block, wd_ref[...], preferred_element_type=F32).astype(BF16)
    down = mm_t(block, cot_ref[...]) * scale
    both = z.tap_rows + z.down_rows
    for s in range(z.samples):
        total_ref[s * both : s * both + z.tap_rows, :] = taps_ref[s * z.tap_rows : (s + 1) * z.tap_rows, :]
        total_ref[s * both + z.tap_rows : (s + 1) * both, :] = down[s * z.down_rows : (s + 1) * z.down_rows]
    deal_parts(z, sample_ref, me_ref, total_ref, own_ref, other_refs)


def inner_kernel(z, slope_ref, turned_ref, inner_ref, wide_ref):
    inner_ref[...] = inner_back(z, slope_ref[...].astype(F32), turned_ref, wide_ref)


def slope_kernel(
    z, scale, sample_ref, me_ref, got_ref, pix_row_ref, inner_ref, slope_in_ref, columns_ref,
    slope_ref, own_ref, *refs,
):
    other_refs, total_ref = refs[:-1], refs[-1]
    back = inner_ref[...] + mm(pick_columns(pix_row_ref[0:1, :], z.pixels), got_ref[...].reshape(z.sent, z.chan))
    slope = (back * slope_in_ref[...]).astype(BF16)
    slope_ref[...] = slope
    tap_products(z, columns_ref, slope, scale, total_ref)
    deal_parts(z, sample_ref, me_ref, total_ref, own_ref, other_refs)


def last_kernel(z, slope_ref, turned_ref, cell_row_ref, send_ref, scratch_ref):
    rims = rims_back(z, slope_ref[...].astype(F32), turned_ref, scratch_ref)
    send_ref[...] = mm(pick_columns(cell_row_ref[0:1, :], z.sent), rims).astype(BF16).reshape(send_ref.shape)


def join_kernel(z, rim_ref, early_ref, late_ref, *refs):
    others = len(z.parts) - 1
    send_ref, total_ref = refs[2 * others :]
    early, late = early_ref[...], late_ref[...]
    for k in range(others):
        early = early + refs[k][...].astype(F32)
        late = late + refs[others + k][...].astype(F32)
    total_ref[: z.early, :] = early
    total_ref[z.early : z.early + z.late, :] = late
    spare = z.devices * z.chunk - z.early - z.late
    if spare:
        total_ref[z.early + z.late :, :] = jnp.zeros((spare, z.chan), F32)
    send_ref[:, : z.pair, :] = rim_ref[...]
    send_ref[:, z.pair :, :] = total_ref[...].astype(BF16).reshape(z.devices, z.chunk, z.chan)


def sum_kernel(z, got_ref, out_ref):
    sums = []
    for core in range(2):
        total = got_ref[core, z.pair :, :].astype(F32)
        for k in range(core + 2, z.devices, 2):
            total = total + got_ref[k, z.pair :, :].astype(F32)
        sums.append(total.astype(BF16))
    for k in range(z.devices // 2):
        for core in range(2):
            out_ref[k, core * z.chunk : (core + 1) * z.chunk, :] = sums[core]


def input_kernel(z, got_ref, pix_row_ref, inner_ref, out_ref):
    arrived = got_ref[:, : z.pair, :].reshape(z.sent, z.chan)
    total = inner_ref[...] + mm(pick_columns(pix_row_ref[0:1, :], z.pixels), arrived)
    for r in range(z.side):
        out_ref[:, r] = total[r * z.line : (r + 1) * z.line].reshape(z.tiles, z.side, z.chan)


def spread_kernel(z, me_ref, mine_ref, other_ref, one_ref, two_ref, low_ref):
    first = (me_ref[0] & 1) == 0
    mine, other = mine_ref[...].astype(F32), other_ref[...].astype(F32)
    halves = []
    for core in range(2):
        rows = slice(core * z.chunk, (core + 1) * z.chunk)
        a, b = mine[:, rows], other[:, rows]
        pairs = jnp.stack([jnp.where(first, a, b), jnp.where(first, b, a)], axis=1)
        halves.append(pairs.reshape(z.devices * z.chunk, z.chan))
    one_ref[...] = jnp.concatenate([half[z.early : z.early + z.late] for half in halves], axis=0)
    early = jnp.concatenate([half[: z.early] for half in halves], axis=0)
    two_ref[...] = early[: z.tap_rows]
    low_ref[...] = early[z.tap_rows :]


def vmem(*shape, dtype=F32):
    return pltpu.VMEM(shape, dtype)


class Pulled:
    def __init__(self, source, buffer, semaphore):
        self.buffer, self.shape, self.waits = buffer, buffer.shape, True
        self.copy = pltpu.make_async_copy(source, buffer, semaphore)
        self.copy.start()

    def __getitem__(self, at):
        if self.waits:
            self.copy.wait()
            self.waits = False
        return self.buffer[at]


class Pushed:
    def __init__(self, target, buffer, semaphore):
        self.buffer, self.shape, self.started = buffer, buffer.shape, False
        self.copy = pltpu.make_async_copy(buffer, target, semaphore)

    def __getitem__(self, at):
        return self.buffer[at]

    def __setitem__(self, at, value):
        self.buffer[at] = value

    def send(self):
        if not self.started:
            self.copy.start()
            self.started = True


def push(ref):
    if isinstance(ref, Pushed):
        ref.send()


def call(body, outs, scratch=(), scalars=0, fetch=0, name=None):
    def run(*operands):
        first = len(operands) - fetch
        far = [len(out) == 3 for out in outs]
        fetched = operands[first:]
        sent = [out for out in outs if len(out) == 3]
        ends = (first, fetch, len(outs), fetch, len(sent), len(scratch), 1, 1)

        def kernel(*refs):
            groups, at = [], 0
            for count in ends:
                groups.append(refs[at : at + count])
                at += count
            here, there, results, in_buffers, out_buffers, rest, (in_sems,), (out_sems,) = groups
            pulled = [Pulled(ref, in_buffers[k], in_sems.at[k]) for k, ref in enumerate(there)]
            made, pushed = [], []
            for ref, is_far in zip(results, far):
                if is_far:
                    k = len(pushed)
                    pushed.append(Pushed(ref, out_buffers[k], out_sems.at[k]))
                    ref = pushed[k]
                made.append(ref)
            body(*here, *pulled, *made, *rest)
            for ref in pushed:
                ref.send()
            for ref in pushed:
                ref.copy.wait()

        spec = pl.BlockSpec(memory_space=pltpu.VMEM)
        small = pl.BlockSpec(memory_space=pltpu.SMEM)
        apart = pl.BlockSpec(memory_space=pltpu.HBM)
        return pl.pallas_call(
            kernel,
            out_shape=[
                pltpu.HBM(out[0], out[1]) if is_far else jax.ShapeDtypeStruct(out[0], out[1])
                for out, is_far in zip(outs, far)
            ],
            in_specs=[small] * scalars + [spec] * (first - scalars) + [apart] * fetch,
            out_specs=[apart if is_far else spec for is_far in far],
            scratch_shapes=[pltpu.VMEM(x.shape, x.dtype) for x in fetched]
            + [pltpu.VMEM(out[0], out[1]) for out in sent]
            + list(scratch)
            + [pltpu.SemaphoreType.DMA((max(1, fetch),)), pltpu.SemaphoreType.DMA((max(1, len(sent)),))],
            compiler_params=pltpu.CompilerParams(vmem_limit_bytes=24 * 1024 * 1024),
            name=name,
        )(*operands[:first], *[pltpu.with_memory_space_constraint(x, pltpu.HBM) for x in fetched])

    return run


def array(*shape, dtype=F32):
    return shape, dtype


def far(*shape, dtype=F32):
    return shape, dtype, True


def exchange(x):
    return lax.all_to_all(x, "tile", split_axis=0, concat_axis=0, tiled=True)


def deal(others, z):
    got = []
    for k, (shift, core) in enumerate(z.parts[1:]):
        pairs = [
            (s * z.devices + t, (s + shift) % z.samples * z.devices + (t ^ core))
            for s in range(z.samples)
            for t in range(z.devices)
        ]
        got.append(lax.ppermute(others[k], ("dp", "tile"), pairs))
    return got


def local(inputs, cotangent, w_first, w_second, w_down, edge_owner, corner_owner, neighbour_tile, seam_rotation):
    tiles_in, cot = inputs[0], cotangent[0]
    tiles, side, _, chan = tiles_in.shape
    z = Sizes(tiles, side, chan, lax.axis_size("tile"), lax.axis_size("dp"))
    scale = float(z.samples * z.devices * z.pixels) ** -0.5
    me = lax.axis_index("tile").astype(I32).reshape(1)
    sample = lax.axis_index("dp").astype(I32).reshape(1)
    half = side // 2
    down_pixels = half * half * tiles
    sent = array(z.devices, z.pair, chan, dtype=BF16)
    sent_far = far(z.devices, z.pair, chan, dtype=BF16)
    field, field16 = array(z.pixels, chan), array(z.pixels, chan, dtype=BF16)
    field16_far = far(z.pixels, chan, dtype=BF16)
    columns = array(z.column * side, 3 * chan, dtype=BF16)
    columns_far = far(z.column * side, 3 * chan, dtype=BF16)
    turned = array(9 * chan, chan, dtype=BF16)
    wide = vmem((side + 2) * z.line, 3 * chan, dtype=BF16)
    side_columns = (vmem(z.column * side, chan), vmem(z.column * side, chan))
    flat = vmem(z.pixels, chan)
    taps = vmem(9 * chan, chan)
    bind = functools.partial
    tables = (edge_owner.T, corner_owner.T, neighbour_tile.T, seam_rotation.T)
    others = len(z.parts) - 1

    (send,) = call(bind(pack_kernel, z), [sent_far], scalars=1, fetch=5, name="pack")(me, *tables, tiles_in)
    got = exchange(send)
    cot_rows = cot.transpose(1, 0, 2, 3).reshape(down_pixels, chan)
    index_col, pix_row, cell_row, back_second, turned_first, turned_second = call(
        bind(side_kernel, z),
        [
            array(z.sent + z.cells_up, LANES, dtype=I32),
            array(8, z.sent, dtype=I32),
            array(8, z.cells_up, dtype=I32),
            field,
            turned,
            turned,
        ],
        scalars=1,
        name="aside",
    )(me, *tables, cot_rows, w_down, w_first, w_second)
    send, hidden, columns_first = call(
        bind(first_kernel, z), [sent, field16, columns], side_columns, name="first"
    )(got, index_col, tiles_in, w_first)
    got = exchange(send)
    (slope_in,) = call(bind(again_kernel, z), [field], name="again")(columns_first, w_first)
    send, slope_second, hidden_second, columns_second = call(
        bind(second_kernel, z), [sent_far, field16_far, field16_far, columns_far], side_columns + (flat,), name="second"
    )(got, index_col, cell_row, hidden, w_second, turned_second, back_second)
    got = exchange(send)
    (inner,) = call(bind(inner_kernel, z), [field], (wide,), name="inner")(slope_second, turned_second)
    features, early_own, *early_other = call(
        bind(early_kernel, z, scale),
        [array(down_pixels, chan, dtype=BF16), array(z.early, chan)] + [array(z.early, chan, dtype=BF16)] * others,
        (taps, vmem(2 * z.samples * z.early, chan), flat, vmem(down_pixels, 4 * chan, dtype=BF16)),
        scalars=2,
        name="early",
    )(sample, me, columns_second, slope_second, hidden_second, cot_rows, w_down)
    features = features.reshape(half, tiles, half, chan).transpose(1, 0, 2, 3)
    early_got = deal(early_other, z)
    slope_first, late_own, *late_other = call(
        bind(slope_kernel, z, scale),
        [field16, array(z.late, chan)] + [array(z.late, chan, dtype=BF16)] * others,
        (taps,),
        scalars=2,
        name="slope",
    )(sample, me, got, pix_row, inner, slope_in, columns_first)
    late_got = deal(late_other, z)
    (send,) = call(bind(last_kernel, z), [sent], (flat,), name="last")(slope_first, turned_first, cell_row)
    (send,) = call(
        bind(join_kernel, z),
        [array(z.devices, z.pair + z.chunk, chan, dtype=BF16)],
        (vmem(z.devices * z.chunk, chan),),
        name="join",
    )(send, early_own, late_own, *early_got, *late_got)
    got = exchange(send)
    (inner,) = call(bind(inner_kernel, z), [field], (wide,), name="inner")(slope_first, turned_first)
    (chunk,) = call(bind(sum_kernel, z), [array(z.devices // 2, 2 * z.chunk, chan, dtype=BF16)], name="sum")(got)
    same_core = [list(range(core, z.devices, 2)) for core in range(2)]
    mine = lax.all_to_all(chunk, "tile", split_axis=0, concat_axis=0, tiled=True, axis_index_groups=same_core)
    (input_grad,) = call(bind(input_kernel, z), [array(tiles, side, side, chan)], name="input")(got, pix_row, inner)
    mine, input_grad = lax.optimization_barrier((mine, input_grad))
    other = lax.ppermute(mine, "tile", [(t, t ^ 1) for t in range(z.devices)])
    grad_first, grad_second, grad_down = call(
        bind(spread_kernel, z),
        [array(z.tap_rows, chan), array(z.tap_rows, chan), array(z.down_rows, chan)],
        scalars=1,
        name="spread",
    )(me, mine, other)
    return features[None], input_grad[None], grad_first, grad_second, grad_down


def solution(mesh):
    split = P("dp", "tile", None, None, None)
    return jax.shard_map(
        local,
        mesh=mesh,
        in_specs=(split, split, P(), P(), P(), P(), P(), P(), P()),
        out_specs=(split, split, P("dp", None), P("dp", None), P("dp", None)),
        check_vma=False,
    )
```

```python
import functools
import jax
import jax.numpy as jnp
from jax import lax
from jax.experimental import pallas as pl
from jax.experimental.pallas import tpu as pltpu
from jax.sharding import PartitionSpec as P

F32, BF16, I32 = jnp.float32, jnp.bfloat16, jnp.int32
LANES = 128


class Sizes:
    def __init__(self, tiles, side, chan, devices, samples):
        self.tiles, self.side, self.chan = tiles, side, chan
        self.devices, self.samples = devices, samples
        self.slots = max(2, 4 * tiles // devices + 1)
        self.pair = -(-self.slots * (side + 1) // 16) * 16
        self.sent = devices * self.pair
        self.line = tiles * side
        self.pixels = side * self.line
        self.column = (side + 2) * tiles
        self.cells = 2 * self.line + 2 * self.column
        self.cells_up = -(-self.cells // (2 * LANES)) * 2 * LANES
        self.tap_rows = 9 * chan // samples
        self.down_rows = 4 * chan // samples
        self.late = self.tap_rows // 2
        self.early = (self.tap_rows + self.down_rows) // 2
        self.chunk = -(-(self.early + self.late) // (16 * devices)) * 16
        self.parts = [(s, c) for s in range(samples) for c in range(2)]
        self.slot_rows = -(-self.slots // 8) * 8


def iota(shape, dim):
    return lax.broadcasted_iota(I32, shape, dim)


def mm(a, b):
    return jnp.dot(a.astype(BF16), b.astype(BF16), preferred_element_type=F32)


def mm_t(a, b):
    return lax.dot_general(a, b, (((0,), (0,)), ((), ())), preferred_element_type=F32)


def flag(cond):
    return jnp.where(cond, 1.0, 0.0).astype(BF16)


def pick_rows(index, width):
    rows = index.shape[0]
    lane = iota((rows, LANES), 1)
    return jnp.concatenate([flag(index == lane + at) for at in range(0, width, LANES)], axis=1)


def gather(index, source):
    half, chan = source.shape[0] // 2, source.shape[1]
    source = source.astype(BF16)
    right = index >= half
    wide = mm(pick_rows(jnp.where(right, index - half, index), half), jnp.concatenate([source[:half], source[half:]], axis=1))
    return jnp.where(right, wide[:, chan:], wide[:, :chan])


def pick_columns(index, height):
    shape = (height, index.shape[1])
    return flag(jnp.broadcast_to(index, shape) == iota(shape, 0))


def row_first(x):
    tiles, side, _, chan = x.shape
    x = x.astype(F32)
    return jnp.stack([x[:, r].reshape(tiles * side, chan) for r in range(side)], axis=0)


def sender_index(me, owners, local_ids, turns, z):
    requests = z.devices * z.tiles
    row8 = iota((8, requests), 0)
    matched = owners == me
    code = jnp.where(matched, local_ids * 16 + turns * 4 + (row8 & 3) + 1, 0).astype(F32)
    found = jnp.where(matched, 1.0, 0.0)

    def both(values):
        edge = jnp.sum(values[:4], axis=0, keepdims=True)
        corner = jnp.sum(values[4:], axis=0, keepdims=True)
        shape = (z.slot_rows, requests)
        return jnp.concatenate([jnp.broadcast_to(edge, shape), jnp.broadcast_to(corner, shape)], axis=0)

    column = iota((1, 1, requests), 2)
    cube = (z.devices, z.tiles, requests)
    earlier = (iota(cube, 0) == lax.div(column, z.tiles)) & (iota(cube, 1) < lax.rem(column, z.tiles))
    rank = mm(both(found), flag(earlier).reshape(requests, requests))
    slot = iota((2 * z.slot_rows, requests), 0)
    slot = jnp.where(slot < z.slot_rows, slot, slot - z.slot_rows)
    placed = jnp.where(slot.astype(F32) == rank, both(code), 0.0)
    row = iota((1, z.sent), 1)
    device, at = lax.div(row, z.pair), lax.rem(row, z.pair)
    cube = (z.devices, z.tiles, z.sent)
    rows = mm(placed, flag(iota(cube, 0) == device.reshape(1, 1, z.sent)).reshape(requests, z.sent))
    edges = z.slots * z.side
    is_edge = at < edges
    wanted = jnp.where(is_edge, lax.div(at, z.side), at - edges + z.slot_rows)
    wanted = jnp.where(at < edges + z.slots, wanted, -1)
    here = iota((2 * z.slot_rows, z.sent), 0) == wanted
    code = jnp.sum(jnp.where(here, rows, 0.0), axis=0, keepdims=True).astype(I32) - 1
    along = lax.rem(at, z.side)
    source, turn, towards = code >> 4, (code >> 2) & 3, code & 3
    end = z.side - 1
    i_edge = jnp.where(towards == 0, end, jnp.where(towards == 2, 0, along))
    j_edge = jnp.where(towards == 1, 0, jnp.where(towards == 3, end, along))
    i_corner = jnp.where((towards == 0) | (towards == 3), end, 0)
    j_corner = jnp.where(towards >= 2, end, 0)
    i = jnp.where(is_edge, i_edge, i_corner)
    j = jnp.where(is_edge, j_edge, j_corner)
    row = jnp.where(turn == 0, i, jnp.where(turn == 1, j, jnp.where(turn == 2, end - i, end - j)))
    col = jnp.where(turn == 0, j, jnp.where(turn == 1, end - i, jnp.where(turn == 2, end - j, i)))
    return jnp.where(code >= 0, row * z.line + source * z.side + col, -1)


def receiver_index(own, z):
    lane = iota((z.tiles, LANES), 1)
    lower = flag(iota((z.tiles, z.tiles), 1) < iota((z.tiles, z.tiles), 0))
    values = jnp.zeros((z.tiles, LANES), F32)
    for base in (0, 4):
        hits = [jnp.broadcast_to(own[:, base + k : base + k + 1], (z.tiles, LANES)) == lane for k in range(4)]
        named = sum(jnp.where(hit, 1.0, 0.0) for hit in hits)
        before = mm(lower, named)
        for k in range(4):
            rank = jnp.sum(jnp.where(hits[k], before, 0.0), axis=1, keepdims=True)
            values = jnp.where(lane == 2 * base + k, own[:, base + k : base + k + 1].astype(F32), values)
            values = jnp.where(lane == 2 * base + 4 + k, rank, values)
    ones = jnp.ones((LANES, LANES), BF16)

    def spread(tile, own_lane, is_edge, along):
        rows = tile.shape[0]
        lane = iota((rows, LANES), 1)
        here = mm(flag(tile[:, : z.tiles] == iota((rows, z.tiles), 1)), values)
        own = mm(jnp.where(lane == own_lane, here, 0.0), ones).astype(I32)
        rank = mm(jnp.where(lane == own_lane + 4, here, 0.0), ones).astype(I32)
        return own * z.pair + jnp.where(is_edge, rank * z.side + along, z.slots * z.side + rank)

    line = (z.tiles, z.side, LANES)
    tile = iota(line, 0).reshape(z.line, LANES)
    along = iota(line, 1).reshape(z.line, LANES)
    parts = [spread(tile, k, jnp.full(tile.shape, True), along) for k in (0, 2)]
    column = (z.side + 2, z.tiles, LANES)
    row = iota(column, 0).reshape(z.column, LANES)
    tile = iota(column, 1).reshape(z.column, LANES)
    is_edge = (row > 0) & (row <= z.side)
    for edge, top, bottom in ((3, 3, 2), (1, 0, 1)):
        own_lane = jnp.where(is_edge, edge, jnp.where(row == 0, 8 + top, 8 + bottom))
        parts.append(spread(tile, own_lane, is_edge, row - 1))
    parts.append(jnp.full((z.cells_up - z.cells, LANES), -1, I32))
    return jnp.concatenate(parts, axis=0)


def as_column(index):
    return jnp.transpose(jnp.broadcast_to(index.astype(F32), (LANES, index.shape[1]))).astype(I32)


def pack_kernel(z, me_ref, eo_ref, co_ref, ids_ref, turn_ref, x_ref, send_ref):
    owners = jnp.concatenate([eo_ref[...], co_ref[...]], axis=0)
    index = sender_index(me_ref[0], owners, ids_ref[...], turn_ref[...], z)
    pixels = row_first(x_ref[...]).reshape(z.pixels, z.chan)
    send_ref[...] = gather(as_column(index), pixels).astype(BF16).reshape(send_ref.shape)


def side_kernel(
    z, me_ref, eo_ref, co_ref, ids_ref, turn_ref, cot_ref, wd_ref, w1_ref, w2_ref,
    table_ref, back_ref, t1_ref, t2_ref,
):
    me = me_ref[0]
    owners = jnp.concatenate([eo_ref[...], co_ref[...]], axis=0)
    index = sender_index(me, owners, ids_ref[...], turn_ref[...], z)
    table_ref[0:8, : z.sent] = jnp.broadcast_to(index, (8, z.sent))
    shape = (z.tiles, z.devices * z.tiles)
    mine = flag(iota(shape, 1) == iota(shape, 0) + me * z.tiles)
    own = lax.dot_general(
        mine, owners.astype(F32).astype(BF16), (((1,), (1,)), ((), ())), preferred_element_type=F32
    )
    index = receiver_index(own.astype(I32), z)
    table_ref[8:16, : z.cells_up] = jnp.transpose(index.astype(F32))[0:8].astype(I32)
    cell = iota((16, z.cells_up), 1) + 1
    digits = jnp.where(iota((16, z.cells_up), 0) < 8, cell >> 4, cell & 15).astype(F32)
    found = mm(digits, pick_rows(index, z.sent))
    table_ref[16:24, : z.sent] = jnp.broadcast_to(found[0:1] * 16.0 + found[8:9] - 1.0, (8, z.sent)).astype(I32)
    chan, half = z.chan, z.side // 2
    for taps, out in ((w1_ref, t1_ref), (w2_ref, t2_ref)):
        for tap in range(9):
            rows = slice(tap * chan, (tap + 1) * chan)
            out[rows, :] = jnp.transpose(taps[rows, :].astype(F32)).astype(BF16)
    cot = cot_ref[...]
    part = half * z.tiles
    for p in range(2):
        for q in range(2):
            tap = wd_ref[(2 * p + q) * chan : (2 * p + q + 1) * chan, :]
            back = lax.dot_general(cot, tap, (((1,), (1,)), ((), ())), preferred_element_type=F32)
            for i in range(half):
                back_ref[pl.ds((2 * i + p) * z.line + q, part, stride=2), :] = back[i * part : (i + 1) * part]


def padded_columns(z, center, arrived, index, west_ref, east_ref, out_ref):
    rims = gather(index, arrived)
    north, south = rims[: z.line], rims[z.line : 2 * z.line]
    at = 2 * z.line
    west_ref[pl.ds(0, z.column, stride=z.side), :] = rims[at : at + z.column]
    east_ref[pl.ds(z.side - 1, z.column, stride=z.side), :] = rims[at + z.column : at + 2 * z.column]
    shape = (z.column, z.side, z.chan)
    middle = jnp.concatenate([north, center, south], axis=0).reshape(shape)
    place = iota(shape, 1)
    flat = (z.column * z.side, z.chan)
    left = jnp.where(place == 0, west_ref[...].reshape(shape), pltpu.roll(middle, 1, 1))
    right = jnp.where(place == z.side - 1, east_ref[...].reshape(shape), pltpu.roll(middle, z.side - 1, 1))
    out_ref[:, : z.chan] = left.reshape(flat).astype(BF16)
    out_ref[:, z.chan : 2 * z.chan] = middle.reshape(flat).astype(BF16)
    out_ref[:, 2 * z.chan :] = right.reshape(flat).astype(BF16)


def conv(z, columns_ref, w_ref):
    total = None
    for p in range(3):
        part = jnp.dot(
            columns_ref[p * z.line : p * z.line + z.pixels, :],
            w_ref[3 * p * z.chan : 3 * (p + 1) * z.chan, :],
            preferred_element_type=F32,
        )
        total = part if total is None else total + part
    return total


def silu_slope(v):
    s = 1.0 / (1.0 + jnp.exp(-v))
    return s * (1.0 + v * (1.0 - s))


def first_kernel(z, got_ref, index_ref, x_ref, w_ref, send_ref, hidden_ref, columns_ref, west_ref, east_ref):
    center = row_first(x_ref[...]).reshape(z.pixels, z.chan)
    padded_columns(z, center, got_ref[...].reshape(z.sent, z.chan), as_column(index_ref[8:9, : z.cells_up]), west_ref, east_ref, columns_ref)
    v = conv(z, columns_ref, w_ref)
    hidden = (v / (1.0 + jnp.exp(-v))).astype(BF16)
    send_ref[...] = gather(as_column(index_ref[0:1, : z.sent]), hidden).astype(BF16).reshape(send_ref.shape)
    hidden_ref[...] = hidden


def again_kernel(z, columns_ref, w_ref, slope_ref):
    slope_ref[...] = silu_slope(conv(z, columns_ref, w_ref))


def shifted(z, slope):
    cube = slope.reshape(slope.shape[0] // z.side, z.side, z.chan)
    place = iota(cube.shape, 1)
    after = jnp.where(place == z.side - 1, 0.0, pltpu.roll(cube, z.side - 1, 1))
    before = jnp.where(place == 0, 0.0, pltpu.roll(cube, 1, 1))
    return [part.reshape(slope.shape).astype(BF16) for part in (after, cube, before)]


def rims_back(z, slope, turned_ref, slope_ref):
    chan = z.chan
    parts = []
    for p, row in ((0, 0), (2, z.side - 1)):
        wide = jnp.concatenate(shifted(z, slope[row * z.line : (row + 1) * z.line]), axis=1)
        parts.append(jnp.dot(wide, turned_ref[3 * p * chan : 3 * (p + 1) * chan, :], preferred_element_type=F32))
    slope_ref[...] = slope
    blank = jnp.zeros((2 * z.tiles, chan), F32)
    for start, q in ((0, 0), (z.side - 1, 2)):
        line = slope_ref[pl.ds(start, z.side * z.tiles, stride=z.side), :]
        line = jnp.concatenate([blank, line, blank], axis=0).astype(BF16)
        side = None
        for p in range(3):
            part = jnp.dot(
                line[(2 - p) * z.tiles : (2 - p) * z.tiles + z.column],
                turned_ref[(3 * p + q) * chan : (3 * p + q + 1) * chan, :],
                preferred_element_type=F32,
            )
            side = part if side is None else side + part
        parts.append(side)
    parts.append(jnp.zeros((z.cells_up - z.cells, chan), F32))
    return jnp.concatenate(parts, axis=0).astype(BF16)


def inner_back(z, slope, turned_ref, wide_ref):
    chan = z.chan
    zero = jnp.zeros((z.line, 3 * chan), BF16)
    wide_ref[: z.line, :] = zero
    wide_ref[z.line + z.pixels :, :] = zero
    for q, part in enumerate(shifted(z, slope)):
        wide_ref[z.line : z.line + z.pixels, q * chan : (q + 1) * chan] = part
    total = None
    for p in range(3):
        part = jnp.dot(
            wide_ref[(2 - p) * z.line : (2 - p) * z.line + z.pixels, :],
            turned_ref[3 * p * chan : 3 * (p + 1) * chan, :],
            preferred_element_type=F32,
        )
        total = part if total is None else total + part
    return total


def second_kernel(
    z, got_ref, index_ref, hidden_ref, w_ref, turned_ref, back_ref,
    send_ref, slope_ref, out_ref, columns_ref, west_ref, east_ref, scratch_ref,
):
    center = hidden_ref[...].astype(F32)
    padded_columns(z, center, got_ref[...].reshape(z.sent, z.chan), as_column(index_ref[8:9, : z.cells_up]), west_ref, east_ref, columns_ref)
    push(columns_ref)
    v = conv(z, columns_ref, w_ref)
    s = 1.0 / (1.0 + jnp.exp(-v))
    out_ref[...] = (v * s).astype(BF16)
    push(out_ref)
    slope = (back_ref[...] * (s * (1.0 + v * (1.0 - s)))).astype(BF16)
    slope_ref[...] = slope
    push(slope_ref)
    rims = rims_back(z, slope.astype(F32), turned_ref, scratch_ref)
    send_ref[...] = gather(as_column(index_ref[16:17, : z.sent]), rims).astype(BF16).reshape(send_ref.shape)


def tap_products(z, columns_ref, slope, scale, total_ref):
    turned = jnp.transpose(slope.astype(F32)).astype(BF16)
    for p in range(3):
        part = jnp.dot(turned, columns_ref[p * z.line : p * z.line + z.pixels, :], preferred_element_type=F32)
        total_ref[3 * p * z.chan : 3 * (p + 1) * z.chan, :] = jnp.transpose(part * scale)


def deal_parts(z, sample_ref, me_ref, source_ref, own_ref, other_refs):
    rows = own_ref.shape[0]
    for k, (shift, core) in enumerate(z.parts):
        whose = lax.rem(sample_ref[0] + shift, z.samples)
        half = jnp.bitwise_xor(me_ref[0] & 1, core)
        part = source_ref[pl.ds((2 * whose + half) * rows, rows), :]
        if k == 0:
            own_ref[...] = part
        else:
            other_refs[k - 1][...] = part.astype(BF16)


def early_kernel(
    z, scale, sample_ref, me_ref, columns_ref, slope_ref, hidden_ref, cot_ref, wd_ref, feature_ref, own_ref, *refs
):
    other_refs, (taps_ref, total_ref, flat_ref, block_ref) = refs[:-4], refs[-4:]
    chan, half = z.chan, z.side // 2
    part = half * z.tiles
    tap_products(z, columns_ref, slope_ref[...], scale, taps_ref)
    flat_ref[...] = hidden_ref[...].astype(F32)
    for i in range(half):
        for p in range(2):
            for q in range(2):
                block_ref[i * part : (i + 1) * part, (2 * p + q) * chan : (2 * p + q + 1) * chan] = flat_ref[
                    pl.ds((2 * i + p) * z.line + q, part, stride=2), :
                ].astype(BF16)
    block = block_ref[...]
    feature_ref[...] = jnp.dot(block, wd_ref[...], preferred_element_type=F32).astype(BF16)
    down = mm_t(block, cot_ref[...]) * scale
    both = z.tap_rows + z.down_rows
    for s in range(z.samples):
        total_ref[s * both : s * both + z.tap_rows, :] = taps_ref[s * z.tap_rows : (s + 1) * z.tap_rows, :]
        total_ref[s * both + z.tap_rows : (s + 1) * both, :] = down[s * z.down_rows : (s + 1) * z.down_rows]
    deal_parts(z, sample_ref, me_ref, total_ref, own_ref, other_refs)


def inner_kernel(z, slope_ref, turned_ref, inner_ref, wide_ref):
    inner_ref[...] = inner_back(z, slope_ref[...].astype(F32), turned_ref, wide_ref)


def slope_kernel(
    z, scale, sample_ref, me_ref, got_ref, pix_row_ref, inner_ref, slope_in_ref, columns_ref,
    slope_ref, own_ref, *refs,
):
    other_refs, total_ref = refs[:-1], refs[-1]
    back = inner_ref[...] + mm(pick_columns(pix_row_ref[0:1, : z.sent], z.pixels), got_ref[...].reshape(z.sent, z.chan))
    slope = (back * slope_in_ref[...]).astype(BF16)
    slope_ref[...] = slope
    tap_products(z, columns_ref, slope, scale, total_ref)
    deal_parts(z, sample_ref, me_ref, total_ref, own_ref, other_refs)


def last_kernel(z, slope_ref, turned_ref, index_ref, send_ref, scratch_ref):
    rims = rims_back(z, slope_ref[...].astype(F32), turned_ref, scratch_ref)
    send_ref[...] = gather(as_column(index_ref[16:17, : z.sent]), rims).astype(BF16).reshape(send_ref.shape)


def gain_kernel(own_ref, *refs):
    others, out_ref = refs[:-1], refs[-1]
    total = own_ref[...]
    for other in others:
        total = total + other[...].astype(F32)
    out_ref[...] = total


def join_kernel(z, rim_ref, early_ref, late_ref, *refs):
    others, (send_ref, total_ref) = refs[:-2], refs[-2:]
    late = late_ref[...]
    for other in others:
        late = late + other[...].astype(F32)
    total_ref[: z.early, :] = early_ref[...]
    total_ref[z.early : z.early + z.late, :] = late
    spare = z.devices * z.chunk - z.early - z.late
    if spare:
        total_ref[z.early + z.late :, :] = jnp.zeros((spare, z.chan), F32)
    send_ref[:, : z.pair, :] = rim_ref[...]
    send_ref[:, z.pair :, :] = total_ref[...].astype(BF16).reshape(z.devices, z.chunk, z.chan)


def sum_kernel(z, got_ref, out_ref):
    sums = []
    for core in range(2):
        total = got_ref[core, z.pair :, :].astype(F32)
        for k in range(core + 2, z.devices, 2):
            total = total + got_ref[k, z.pair :, :].astype(F32)
        sums.append(total.astype(BF16))
    for k in range(z.devices // 2):
        for core in range(2):
            out_ref[k, core * z.chunk : (core + 1) * z.chunk, :] = sums[core]


def input_kernel(z, got_ref, pix_row_ref, inner_ref, out_ref):
    arrived = got_ref[:, : z.pair, :].reshape(z.sent, z.chan)
    total = inner_ref[...] + mm(pick_columns(pix_row_ref[0:1, : z.sent], z.pixels), arrived)
    for r in range(z.side):
        out_ref[:, r] = total[r * z.line : (r + 1) * z.line].reshape(z.tiles, z.side, z.chan)


def spread_kernel(z, me_ref, mine_ref, other_ref, one_ref, two_ref, low_ref):
    first = (me_ref[0] & 1) == 0
    mine, other = mine_ref[...].astype(F32), other_ref[...].astype(F32)
    halves = []
    for core in range(2):
        rows = slice(core * z.chunk, (core + 1) * z.chunk)
        a, b = mine[:, rows], other[:, rows]
        pairs = jnp.stack([jnp.where(first, a, b), jnp.where(first, b, a)], axis=1)
        halves.append(pairs.reshape(z.devices * z.chunk, z.chan))
    one_ref[...] = jnp.concatenate([half[z.early : z.early + z.late] for half in halves], axis=0)
    early = jnp.concatenate([half[: z.early] for half in halves], axis=0)
    two_ref[...] = early[: z.tap_rows]
    low_ref[...] = early[z.tap_rows :]


def vmem(*shape, dtype=F32):
    return pltpu.VMEM(shape, dtype)


class Pulled:
    def __init__(self, source, buffer, semaphore):
        self.buffer, self.shape, self.waits = buffer, buffer.shape, True
        self.copy = pltpu.make_async_copy(source, buffer, semaphore)
        self.copy.start()

    def __getitem__(self, at):
        if self.waits:
            self.copy.wait()
            self.waits = False
        return self.buffer[at]


class Pushed:
    def __init__(self, target, buffer, semaphore):
        self.buffer, self.shape, self.started = buffer, buffer.shape, False
        self.copy = pltpu.make_async_copy(buffer, target, semaphore)

    def __getitem__(self, at):
        return self.buffer[at]

    def __setitem__(self, at, value):
        self.buffer[at] = value

    def send(self):
        if not self.started:
            self.copy.start()
            self.started = True


def push(ref):
    if isinstance(ref, Pushed):
        ref.send()


def call(body, outs, scratch=(), scalars=0, fetch=0, name=None):
    def run(*operands):
        first = len(operands) - fetch
        far = [len(out) == 3 for out in outs]
        fetched = operands[first:]
        sent = [out for out in outs if len(out) == 3]
        ends = (first, fetch, len(outs), fetch, len(sent), len(scratch), 1, 1)

        def kernel(*refs):
            groups, at = [], 0
            for count in ends:
                groups.append(refs[at : at + count])
                at += count
            here, there, results, in_buffers, out_buffers, rest, (in_sems,), (out_sems,) = groups
            pulled = [Pulled(ref, in_buffers[k], in_sems.at[k]) for k, ref in enumerate(there)]
            made, pushed = [], []
            for ref, is_far in zip(results, far):
                if is_far:
                    k = len(pushed)
                    pushed.append(Pushed(ref, out_buffers[k], out_sems.at[k]))
                    ref = pushed[k]
                made.append(ref)
            body(*here, *pulled, *made, *rest)
            for ref in pushed:
                ref.send()
            for ref in pushed:
                ref.copy.wait()

        spec = pl.BlockSpec(memory_space=pltpu.VMEM)
        small = pl.BlockSpec(memory_space=pltpu.SMEM)
        apart = pl.BlockSpec(memory_space=pltpu.HBM)
        return pl.pallas_call(
            kernel,
            out_shape=[
                pltpu.HBM(out[0], out[1]) if is_far else jax.ShapeDtypeStruct(out[0], out[1])
                for out, is_far in zip(outs, far)
            ],
            in_specs=[small] * scalars + [spec] * (first - scalars) + [apart] * fetch,
            out_specs=[apart if is_far else spec for is_far in far],
            scratch_shapes=[pltpu.VMEM(x.shape, x.dtype) for x in fetched]
            + [pltpu.VMEM(out[0], out[1]) for out in sent]
            + list(scratch)
            + [pltpu.SemaphoreType.DMA((max(1, fetch),)), pltpu.SemaphoreType.DMA((max(1, len(sent)),))],
            compiler_params=pltpu.CompilerParams(vmem_limit_bytes=24 * 1024 * 1024),
            name=name,
        )(*operands[:first], *[pltpu.with_memory_space_constraint(x, pltpu.HBM) for x in fetched])

    return run


def array(*shape, dtype=F32):
    return shape, dtype


def far(*shape, dtype=F32):
    return shape, dtype, True


def exchange(x):
    return lax.all_to_all(x, "tile", split_axis=0, concat_axis=0, tiled=True)


def deal(others, z):
    got = []
    for k, (shift, core) in enumerate(z.parts[1:]):
        pairs = [
            (s * z.devices + t, (s + shift) % z.samples * z.devices + (t ^ core))
            for s in range(z.samples)
            for t in range(z.devices)
        ]
        got.append(lax.ppermute(others[k], ("dp", "tile"), pairs))
    return got


def local(inputs, cotangent, w_first, w_second, w_down, edge_owner, corner_owner, neighbour_tile, seam_rotation):
    tiles_in, cot = inputs[0], cotangent[0]
    tiles, side, _, chan = tiles_in.shape
    z = Sizes(tiles, side, chan, lax.axis_size("tile"), lax.axis_size("dp"))
    scale = float(z.samples * z.devices * z.pixels) ** -0.5
    me = lax.axis_index("tile").astype(I32).reshape(1)
    sample = lax.axis_index("dp").astype(I32).reshape(1)
    half = side // 2
    down_pixels = half * half * tiles
    sent = array(z.devices, z.pair, chan, dtype=BF16)
    sent_far = far(z.devices, z.pair, chan, dtype=BF16)
    field, field16 = array(z.pixels, chan), array(z.pixels, chan, dtype=BF16)
    field16_far = far(z.pixels, chan, dtype=BF16)
    columns = array(z.column * side, 3 * chan, dtype=BF16)
    columns_far = far(z.column * side, 3 * chan, dtype=BF16)
    turned = array(9 * chan, chan, dtype=BF16)
    wide = vmem((side + 2) * z.line, 3 * chan, dtype=BF16)
    side_columns = (vmem(z.column * side, chan), vmem(z.column * side, chan))
    flat = vmem(z.pixels, chan)
    taps = vmem(9 * chan, chan)
    bind = functools.partial
    tables = (edge_owner.T, corner_owner.T, neighbour_tile.T, seam_rotation.T)
    others = len(z.parts) - 1

    (send,) = call(bind(pack_kernel, z), [sent_far], scalars=1, fetch=5, name="pack")(me, *tables, tiles_in)
    got = exchange(send)
    cot_rows = cot.transpose(1, 0, 2, 3).reshape(down_pixels, chan)
    index, back_second, turned_first, turned_second = call(
        bind(side_kernel, z),
        [
            array(24, max(z.sent, z.cells_up), dtype=I32),
            field,
            turned,
            turned,
        ],
        scalars=1,
        name="aside",
    )(me, *tables, cot_rows, w_down, w_first, w_second)
    send, hidden, columns_first = call(
        bind(first_kernel, z), [sent, field16, columns], side_columns, name="first"
    )(got, index, tiles_in, w_first)
    got = exchange(send)
    (slope_in,) = call(bind(again_kernel, z), [field], name="again")(columns_first, w_first)
    send, slope_second, hidden_second, columns_second = call(
        bind(second_kernel, z), [sent_far, field16, field16, columns_far], side_columns + (flat,), name="second"
    )(got, index, hidden, w_second, turned_second, back_second)
    got = exchange(send)
    (inner,) = call(bind(inner_kernel, z), [field], (wide,), name="inner")(slope_second, turned_second)
    features, early_own, *early_other = call(
        bind(early_kernel, z, scale),
        [array(down_pixels, chan, dtype=BF16), array(z.early, chan)] + [array(z.early, chan, dtype=BF16)] * others,
        (taps, vmem(2 * z.samples * z.early, chan), flat, vmem(down_pixels, 4 * chan, dtype=BF16)),
        scalars=2,
        name="early",
    )(sample, me, columns_second, slope_second, hidden_second, cot_rows, w_down)
    features = features.reshape(half, tiles, half, chan).transpose(1, 0, 2, 3)
    (early,) = call(gain_kernel, [array(z.early, chan)], name="gain")(early_own, *deal(early_other, z))
    slope_first, late_own, *late_other = call(
        bind(slope_kernel, z, scale),
        [field16, array(z.late, chan)] + [array(z.late, chan, dtype=BF16)] * others,
        (taps,),
        scalars=2,
        name="slope",
    )(sample, me, got, index, inner, slope_in, columns_first)
    late_got = deal(late_other, z)
    (send,) = call(bind(last_kernel, z), [sent], (flat,), name="last")(slope_first, turned_first, index)
    (inner,) = call(bind(inner_kernel, z), [field], (wide,), name="inner")(slope_first, turned_first)
    send, inner, features = lax.optimization_barrier((send, inner, features))
    (send,) = call(
        bind(join_kernel, z),
        [array(z.devices, z.pair + z.chunk, chan, dtype=BF16)],
        (vmem(z.devices * z.chunk, chan),),
        name="join",
    )(send, early, late_own, *late_got)
    got = exchange(send)
    (chunk,) = call(bind(sum_kernel, z), [array(z.devices // 2, 2 * z.chunk, chan, dtype=BF16)], name="sum")(got)
    same_core = [list(range(core, z.devices, 2)) for core in range(2)]
    mine = lax.all_to_all(chunk, "tile", split_axis=0, concat_axis=0, tiled=True, axis_index_groups=same_core)
    (input_grad,) = call(bind(input_kernel, z), [array(tiles, side, side, chan)], name="input")(got, index, inner)
    other = lax.ppermute(mine, "tile", [(t, t ^ 1) for t in range(z.devices)])
    grad_first, grad_second, grad_down = call(
        bind(spread_kernel, z),
        [array(z.tap_rows, chan), array(z.tap_rows, chan), array(z.down_rows, chan)],
        scalars=1,
        name="spread",
    )(me, mine, other)
    return features[None], input_grad[None], grad_first, grad_second, grad_down


def solution(mesh):
    split = P("dp", "tile", None, None, None)
    return jax.shard_map(
        local,
        mesh=mesh,
        in_specs=(split, split, P(), P(), P(), P(), P(), P(), P()),
        out_specs=(split, split, P("dp", None), P("dp", None), P("dp", None)),
        check_vma=False,
    )
```

```python
import functools
import jax
import jax.numpy as jnp
from jax import lax
from jax.experimental import pallas as pl
from jax.experimental.pallas import tpu as pltpu
from jax.sharding import PartitionSpec as P

F32, BF16, I32 = jnp.float32, jnp.bfloat16, jnp.int32
LANES = 128


class Sizes:
    def __init__(self, tiles, side, chan, devices, samples):
        self.tiles, self.side, self.chan = tiles, side, chan
        self.devices, self.samples = devices, samples
        self.slots = max(2, 4 * tiles // devices + 1)
        self.pair = -(-self.slots * (side + 1) // 16) * 16
        self.sent = devices * self.pair
        self.line = tiles * side
        self.pixels = side * self.line
        self.column = (side + 2) * tiles
        self.cells = 2 * self.line + 2 * self.column
        self.cells_up = -(-self.cells // (2 * LANES)) * 2 * LANES
        self.tap_rows = 9 * chan // samples
        self.down_rows = 4 * chan // samples
        self.late = self.tap_rows // 2
        self.early = (self.tap_rows + self.down_rows) // 2
        self.chunk = -(-(self.early + self.late) // (16 * devices)) * 16
        self.parts = [(s, c) for s in range(samples) for c in range(2)]
        self.slot_rows = -(-self.slots // 8) * 8


def iota(shape, dim):
    return lax.broadcasted_iota(I32, shape, dim)


def mm(a, b):
    return jnp.dot(a.astype(BF16), b.astype(BF16), preferred_element_type=F32)


def mm_t(a, b):
    return lax.dot_general(a, b, (((0,), (0,)), ((), ())), preferred_element_type=F32)


def flag(cond):
    return jnp.where(cond, 1.0, 0.0).astype(BF16)


def pick_rows(index, width):
    rows = index.shape[0]
    lane = iota((rows, LANES), 1)
    return jnp.concatenate([flag(index == lane + at) for at in range(0, width, LANES)], axis=1)


def gather(index, source):
    half, chan = source.shape[0] // 2, source.shape[1]
    source = source.astype(BF16)
    right = index >= half
    wide = mm(pick_rows(jnp.where(right, index - half, index), half), jnp.concatenate([source[:half], source[half:]], axis=1))
    return jnp.where(right, wide[:, chan:], wide[:, :chan])


def pick_columns(index, height):
    shape = (height, index.shape[1])
    return flag(jnp.broadcast_to(index, shape) == iota(shape, 0))


def row_first(x):
    tiles, side, _, chan = x.shape
    x = x.astype(F32)
    return jnp.stack([x[:, r].reshape(tiles * side, chan) for r in range(side)], axis=0)


def sender_index(me, owners, local_ids, turns, z):
    requests = z.devices * z.tiles
    row8 = iota((8, requests), 0)
    matched = owners == me
    code = jnp.where(matched, local_ids * 16 + turns * 4 + (row8 & 3) + 1, 0).astype(F32)
    found = jnp.where(matched, 1.0, 0.0)

    def both(values):
        edge = jnp.sum(values[:4], axis=0, keepdims=True)
        corner = jnp.sum(values[4:], axis=0, keepdims=True)
        shape = (z.slot_rows, requests)
        return jnp.concatenate([jnp.broadcast_to(edge, shape), jnp.broadcast_to(corner, shape)], axis=0)

    column = iota((1, 1, requests), 2)
    cube = (z.devices, z.tiles, requests)
    earlier = (iota(cube, 0) == lax.div(column, z.tiles)) & (iota(cube, 1) < lax.rem(column, z.tiles))
    rank = mm(both(found), flag(earlier).reshape(requests, requests))
    slot = iota((2 * z.slot_rows, requests), 0)
    slot = jnp.where(slot < z.slot_rows, slot, slot - z.slot_rows)
    placed = jnp.where(slot.astype(F32) == rank, both(code), 0.0)
    row = iota((1, z.sent), 1)
    device, at = lax.div(row, z.pair), lax.rem(row, z.pair)
    cube = (z.devices, z.tiles, z.sent)
    rows = mm(placed, flag(iota(cube, 0) == device.reshape(1, 1, z.sent)).reshape(requests, z.sent))
    edges = z.slots * z.side
    is_edge = at < edges
    wanted = jnp.where(is_edge, lax.div(at, z.side), at - edges + z.slot_rows)
    wanted = jnp.where(at < edges + z.slots, wanted, -1)
    here = iota((2 * z.slot_rows, z.sent), 0) == wanted
    code = jnp.sum(jnp.where(here, rows, 0.0), axis=0, keepdims=True).astype(I32) - 1
    along = lax.rem(at, z.side)
    source, turn, towards = code >> 4, (code >> 2) & 3, code & 3
    end = z.side - 1
    i_edge = jnp.where(towards == 0, end, jnp.where(towards == 2, 0, along))
    j_edge = jnp.where(towards == 1, 0, jnp.where(towards == 3, end, along))
    i_corner = jnp.where((towards == 0) | (towards == 3), end, 0)
    j_corner = jnp.where(towards >= 2, end, 0)
    i = jnp.where(is_edge, i_edge, i_corner)
    j = jnp.where(is_edge, j_edge, j_corner)
    row = jnp.where(turn == 0, i, jnp.where(turn == 1, j, jnp.where(turn == 2, end - i, end - j)))
    col = jnp.where(turn == 0, j, jnp.where(turn == 1, end - i, jnp.where(turn == 2, end - j, i)))
    return jnp.where(code >= 0, row * z.line + source * z.side + col, -1)


def receiver_index(own, z):
    lane = iota((z.tiles, LANES), 1)
    lower = flag(iota((z.tiles, z.tiles), 1) < iota((z.tiles, z.tiles), 0))
    values = jnp.zeros((z.tiles, LANES), F32)
    for base in (0, 4):
        hits = [jnp.broadcast_to(own[:, base + k : base + k + 1], (z.tiles, LANES)) == lane for k in range(4)]
        named = sum(jnp.where(hit, 1.0, 0.0) for hit in hits)
        before = mm(lower, named)
        for k in range(4):
            rank = jnp.sum(jnp.where(hits[k], before, 0.0), axis=1, keepdims=True)
            values = jnp.where(lane == 2 * base + k, own[:, base + k : base + k + 1].astype(F32), values)
            values = jnp.where(lane == 2 * base + 4 + k, rank, values)
    ones = jnp.ones((LANES, LANES), BF16)

    def spread(tile, own_lane, is_edge, along):
        rows = tile.shape[0]
        lane = iota((rows, LANES), 1)
        here = mm(flag(tile[:, : z.tiles] == iota((rows, z.tiles), 1)), values)
        own = mm(jnp.where(lane == own_lane, here, 0.0), ones).astype(I32)
        rank = mm(jnp.where(lane == own_lane + 4, here, 0.0), ones).astype(I32)
        return own * z.pair + jnp.where(is_edge, rank * z.side + along, z.slots * z.side + rank)

    line = (z.tiles, z.side, LANES)
    tile = iota(line, 0).reshape(z.line, LANES)
    along = iota(line, 1).reshape(z.line, LANES)
    parts = [spread(tile, k, jnp.full(tile.shape, True), along) for k in (0, 2)]
    column = (z.side + 2, z.tiles, LANES)
    row = iota(column, 0).reshape(z.column, LANES)
    tile = iota(column, 1).reshape(z.column, LANES)
    is_edge = (row > 0) & (row <= z.side)
    for edge, top, bottom in ((3, 3, 2), (1, 0, 1)):
        own_lane = jnp.where(is_edge, edge, jnp.where(row == 0, 8 + top, 8 + bottom))
        parts.append(spread(tile, own_lane, is_edge, row - 1))
    parts.append(jnp.full((z.cells_up - z.cells, LANES), -1, I32))
    return jnp.concatenate(parts, axis=0)


def as_column(index):
    return jnp.transpose(jnp.broadcast_to(index.astype(F32), (LANES, index.shape[1]))).astype(I32)


def pack_kernel(z, me_ref, eo_ref, co_ref, ids_ref, turn_ref, x_ref, send_ref):
    owners = jnp.concatenate([eo_ref[...], co_ref[...]], axis=0)
    index = sender_index(me_ref[0], owners, ids_ref[...], turn_ref[...], z)
    pixels = row_first(x_ref[...]).reshape(z.pixels, z.chan)
    send_ref[...] = gather(as_column(index), pixels).astype(BF16).reshape(send_ref.shape)


def side_kernel(
    z, me_ref, eo_ref, co_ref, ids_ref, turn_ref, cot_ref, wd_ref, w1_ref, w2_ref,
    table_ref, back_ref, t1_ref, t2_ref,
):
    me = me_ref[0]
    owners = jnp.concatenate([eo_ref[...], co_ref[...]], axis=0)
    index = sender_index(me, owners, ids_ref[...], turn_ref[...], z)
    table_ref[0:8, : z.sent] = jnp.broadcast_to(index, (8, z.sent))
    shape = (z.tiles, z.devices * z.tiles)
    mine = flag(iota(shape, 1) == iota(shape, 0) + me * z.tiles)
    own = lax.dot_general(
        mine, owners.astype(F32).astype(BF16), (((1,), (1,)), ((), ())), preferred_element_type=F32
    )
    index = receiver_index(own.astype(I32), z)
    table_ref[8:16, : z.cells_up] = jnp.transpose(index.astype(F32))[0:8].astype(I32)
    cell = iota((16, z.cells_up), 1) + 1
    digits = jnp.where(iota((16, z.cells_up), 0) < 8, cell >> 4, cell & 15).astype(F32)
    found = mm(digits, pick_rows(index, z.sent))
    table_ref[16:24, : z.sent] = jnp.broadcast_to(found[0:1] * 16.0 + found[8:9] - 1.0, (8, z.sent)).astype(I32)
    chan, half = z.chan, z.side // 2
    for taps, out in ((w1_ref, t1_ref), (w2_ref, t2_ref)):
        for tap in range(9):
            rows = slice(tap * chan, (tap + 1) * chan)
            out[rows, :] = jnp.transpose(taps[rows, :].astype(F32)).astype(BF16)
    cot = cot_ref[...]
    part = half * z.tiles
    for p in range(2):
        for q in range(2):
            tap = wd_ref[(2 * p + q) * chan : (2 * p + q + 1) * chan, :]
            back = lax.dot_general(cot, tap, (((1,), (1,)), ((), ())), preferred_element_type=F32)
            for i in range(half):
                back_ref[pl.ds((2 * i + p) * z.line + q, part, stride=2), :] = back[i * part : (i + 1) * part]


def padded_columns(z, center, arrived, index, west_ref, east_ref, out_ref):
    rims = gather(index, arrived)
    north, south = rims[: z.line], rims[z.line : 2 * z.line]
    at = 2 * z.line
    west_ref[pl.ds(0, z.column, stride=z.side), :] = rims[at : at + z.column]
    east_ref[pl.ds(z.side - 1, z.column, stride=z.side), :] = rims[at + z.column : at + 2 * z.column]
    shape = (z.column, z.side, z.chan)
    middle = jnp.concatenate([north, center, south], axis=0).reshape(shape)
    place = iota(shape, 1)
    flat = (z.column * z.side, z.chan)
    left = jnp.where(place == 0, west_ref[...].reshape(shape), pltpu.roll(middle, 1, 1))
    right = jnp.where(place == z.side - 1, east_ref[...].reshape(shape), pltpu.roll(middle, z.side - 1, 1))
    out_ref[:, : z.chan] = left.reshape(flat).astype(BF16)
    out_ref[:, z.chan : 2 * z.chan] = middle.reshape(flat).astype(BF16)
    out_ref[:, 2 * z.chan :] = right.reshape(flat).astype(BF16)


def conv(z, columns_ref, w_ref):
    total = None
    for p in range(3):
        part = jnp.dot(
            columns_ref[p * z.line : p * z.line + z.pixels, :],
            w_ref[3 * p * z.chan : 3 * (p + 1) * z.chan, :],
            preferred_element_type=F32,
        )
        total = part if total is None else total + part
    return total


def silu_slope(v):
    s = 1.0 / (1.0 + jnp.exp(-v))
    return s * (1.0 + v * (1.0 - s))


def first_kernel(z, got_ref, index_ref, x_ref, w_ref, send_ref, hidden_ref, columns_ref, west_ref, east_ref):
    center = row_first(x_ref[...]).reshape(z.pixels, z.chan)
    padded_columns(z, center, got_ref[...].reshape(z.sent, z.chan), as_column(index_ref[8:9, : z.cells_up]), west_ref, east_ref, columns_ref)
    v = conv(z, columns_ref, w_ref)
    hidden = (v / (1.0 + jnp.exp(-v))).astype(BF16)
    send_ref[...] = gather(as_column(index_ref[0:1, : z.sent]), hidden).astype(BF16).reshape(send_ref.shape)
    hidden_ref[...] = hidden


def again_kernel(z, columns_ref, w_ref, slope_ref):
    slope_ref[...] = silu_slope(conv(z, columns_ref, w_ref))


def shifted(z, slope):
    cube = slope.reshape(slope.shape[0] // z.side, z.side, z.chan)
    place = iota(cube.shape, 1)
    after = jnp.where(place == z.side - 1, 0.0, pltpu.roll(cube, z.side - 1, 1))
    before = jnp.where(place == 0, 0.0, pltpu.roll(cube, 1, 1))
    return [part.reshape(slope.shape).astype(BF16) for part in (after, cube, before)]


def rims_back(z, slope, turned_ref, slope_ref):
    chan = z.chan
    parts = []
    for p, row in ((0, 0), (2, z.side - 1)):
        wide = jnp.concatenate(shifted(z, slope[row * z.line : (row + 1) * z.line]), axis=1)
        parts.append(jnp.dot(wide, turned_ref[3 * p * chan : 3 * (p + 1) * chan, :], preferred_element_type=F32))
    slope_ref[...] = slope
    blank = jnp.zeros((2 * z.tiles, chan), F32)
    for start, q in ((0, 0), (z.side - 1, 2)):
        line = slope_ref[pl.ds(start, z.side * z.tiles, stride=z.side), :]
        line = jnp.concatenate([blank, line, blank], axis=0).astype(BF16)
        side = None
        for p in range(3):
            part = jnp.dot(
                line[(2 - p) * z.tiles : (2 - p) * z.tiles + z.column],
                turned_ref[(3 * p + q) * chan : (3 * p + q + 1) * chan, :],
                preferred_element_type=F32,
            )
            side = part if side is None else side + part
        parts.append(side)
    parts.append(jnp.zeros((z.cells_up - z.cells, chan), F32))
    return jnp.concatenate(parts, axis=0).astype(BF16)


def inner_back(z, slope, turned_ref, wide_ref):
    chan = z.chan
    zero = jnp.zeros((z.line, 3 * chan), BF16)
    wide_ref[: z.line, :] = zero
    wide_ref[z.line + z.pixels :, :] = zero
    for q, part in enumerate(shifted(z, slope)):
        wide_ref[z.line : z.line + z.pixels, q * chan : (q + 1) * chan] = part
    total = None
    for p in range(3):
        part = jnp.dot(
            wide_ref[(2 - p) * z.line : (2 - p) * z.line + z.pixels, :],
            turned_ref[3 * p * chan : 3 * (p + 1) * chan, :],
            preferred_element_type=F32,
        )
        total = part if total is None else total + part
    return total


def second_kernel(
    z, got_ref, index_ref, hidden_ref, w_ref, turned_ref, back_ref,
    send_ref, slope_ref, out_ref, columns_ref, west_ref, east_ref, scratch_ref,
):
    center = hidden_ref[...].astype(F32)
    padded_columns(z, center, got_ref[...].reshape(z.sent, z.chan), as_column(index_ref[8:9, : z.cells_up]), west_ref, east_ref, columns_ref)
    push(columns_ref)
    v = conv(z, columns_ref, w_ref)
    s = 1.0 / (1.0 + jnp.exp(-v))
    out_ref[...] = (v * s).astype(BF16)
    push(out_ref)
    slope = (back_ref[...] * (s * (1.0 + v * (1.0 - s)))).astype(BF16)
    slope_ref[...] = slope
    push(slope_ref)
    rims = rims_back(z, slope.astype(F32), turned_ref, scratch_ref)
    send_ref[...] = gather(as_column(index_ref[16:17, : z.sent]), rims).astype(BF16).reshape(send_ref.shape)


def tap_products(z, columns_ref, slope, scale, total_ref):
    blank = jnp.zeros((2 * z.line, z.chan), BF16)
    padded = jnp.concatenate([blank, slope, blank], axis=0)
    rows = (z.side + 2) * z.line
    wide = jnp.concatenate([padded[(2 - p) * z.line : (2 - p) * z.line + rows] for p in range(3)], axis=1)
    total = mm_t(columns_ref[...], wide) * scale
    for p in range(3):
        total_ref[3 * p * z.chan : 3 * (p + 1) * z.chan, :] = total[:, p * z.chan : (p + 1) * z.chan]


def deal_parts(z, sample_ref, me_ref, source_ref, own_ref, other_refs):
    rows = own_ref.shape[0]
    for k, (shift, core) in enumerate(z.parts):
        whose = lax.rem(sample_ref[0] + shift, z.samples)
        half = jnp.bitwise_xor(me_ref[0] & 1, core)
        part = source_ref[pl.ds((2 * whose + half) * rows, rows), :]
        if k == 0:
            own_ref[...] = part
        else:
            other_refs[k - 1][...] = part.astype(BF16)


def early_kernel(
    z, scale, sample_ref, me_ref, columns_ref, slope_ref, hidden_ref, cot_ref, wd_ref, feature_ref, own_ref, *refs
):
    other_refs, (taps_ref, total_ref, flat_ref, block_ref) = refs[:-4], refs[-4:]
    chan, half = z.chan, z.side // 2
    part = half * z.tiles
    tap_products(z, columns_ref, slope_ref[...], scale, taps_ref)
    flat_ref[...] = hidden_ref[...].astype(F32)
    for i in range(half):
        for p in range(2):
            for q in range(2):
                block_ref[i * part : (i + 1) * part, (2 * p + q) * chan : (2 * p + q + 1) * chan] = flat_ref[
                    pl.ds((2 * i + p) * z.line + q, part, stride=2), :
                ].astype(BF16)
    block = block_ref[...]
    feature_ref[...] = jnp.dot(block, wd_ref[...], preferred_element_type=F32).astype(BF16)
    down = mm_t(block, cot_ref[...]) * scale
    both = z.tap_rows + z.down_rows
    for s in range(z.samples):
        total_ref[s * both : s * both + z.tap_rows, :] = taps_ref[s * z.tap_rows : (s + 1) * z.tap_rows, :]
        total_ref[s * both + z.tap_rows : (s + 1) * both, :] = down[s * z.down_rows : (s + 1) * z.down_rows]
    deal_parts(z, sample_ref, me_ref, total_ref, own_ref, other_refs)


def inner_kernel(z, slope_ref, turned_ref, inner_ref, wide_ref):
    inner_ref[...] = inner_back(z, slope_ref[...].astype(F32), turned_ref, wide_ref)


def slope_kernel(
    z, scale, sample_ref, me_ref, got_ref, pix_row_ref, inner_ref, slope_in_ref, columns_ref,
    slope_ref, own_ref, *refs,
):
    other_refs, total_ref = refs[:-1], refs[-1]
    back = inner_ref[...] + mm(pick_columns(pix_row_ref[0:1, : z.sent], z.pixels), got_ref[...].reshape(z.sent, z.chan))
    slope = (back * slope_in_ref[...]).astype(BF16)
    slope_ref[...] = slope
    tap_products(z, columns_ref, slope, scale, total_ref)
    deal_parts(z, sample_ref, me_ref, total_ref, own_ref, other_refs)


def last_kernel(z, slope_ref, turned_ref, index_ref, send_ref, scratch_ref):
    rims = rims_back(z, slope_ref[...].astype(F32), turned_ref, scratch_ref)
    send_ref[...] = gather(as_column(index_ref[16:17, : z.sent]), rims).astype(BF16).reshape(send_ref.shape)


def gain_kernel(own_ref, *refs):
    others, out_ref = refs[:-1], refs[-1]
    total = own_ref[...]
    for other in others:
        total = total + other[...].astype(F32)
    out_ref[...] = total


def join_kernel(z, rim_ref, early_ref, late_ref, *refs):
    others, (send_ref, total_ref) = refs[:-2], refs[-2:]
    late = late_ref[...]
    for other in others:
        late = late + other[...].astype(F32)
    total_ref[: z.early, :] = early_ref[...]
    total_ref[z.early : z.early + z.late, :] = late
    spare = z.devices * z.chunk - z.early - z.late
    if spare:
        total_ref[z.early + z.late :, :] = jnp.zeros((spare, z.chan), F32)
    send_ref[:, : z.pair, :] = rim_ref[...]
    send_ref[:, z.pair :, :] = total_ref[...].astype(BF16).reshape(z.devices, z.chunk, z.chan)


def sum_kernel(z, got_ref, out_ref):
    sums = []
    for core in range(2):
        total = got_ref[core, z.pair :, :].astype(F32)
        for k in range(core + 2, z.devices, 2):
            total = total + got_ref[k, z.pair :, :].astype(F32)
        sums.append(total.astype(BF16))
    for k in range(z.devices // 2):
        for core in range(2):
            out_ref[k, core * z.chunk : (core + 1) * z.chunk, :] = sums[core]


def input_kernel(z, got_ref, pix_row_ref, inner_ref, out_ref):
    arrived = got_ref[:, : z.pair, :].reshape(z.sent, z.chan)
    total = inner_ref[...] + mm(pick_columns(pix_row_ref[0:1, : z.sent], z.pixels), arrived)
    for r in range(z.side):
        out_ref[:, r] = total[r * z.line : (r + 1) * z.line].reshape(z.tiles, z.side, z.chan)


def spread_kernel(z, me_ref, mine_ref, other_ref, one_ref, two_ref, low_ref):
    first = (me_ref[0] & 1) == 0
    mine, other = mine_ref[...].astype(F32), other_ref[...].astype(F32)
    halves = []
    for core in range(2):
        rows = slice(core * z.chunk, (core + 1) * z.chunk)
        a, b = mine[:, rows], other[:, rows]
        pairs = jnp.stack([jnp.where(first, a, b), jnp.where(first, b, a)], axis=1)
        halves.append(pairs.reshape(z.devices * z.chunk, z.chan))
    one_ref[...] = jnp.concatenate([half[z.early : z.early + z.late] for half in halves], axis=0)
    early = jnp.concatenate([half[: z.early] for half in halves], axis=0)
    two_ref[...] = early[: z.tap_rows]
    low_ref[...] = early[z.tap_rows :]


def vmem(*shape, dtype=F32):
    return pltpu.VMEM(shape, dtype)


class Pulled:
    def __init__(self, source, buffer, semaphore):
        self.buffer, self.shape, self.waits = buffer, buffer.shape, True
        self.copy = pltpu.make_async_copy(source, buffer, semaphore)
        self.copy.start()

    def __getitem__(self, at):
        if self.waits:
            self.copy.wait()
            self.waits = False
        return self.buffer[at]


class Pushed:
    def __init__(self, target, buffer, semaphore):
        self.buffer, self.shape, self.started = buffer, buffer.shape, False
        self.copy = pltpu.make_async_copy(buffer, target, semaphore)

    def __getitem__(self, at):
        return self.buffer[at]

    def __setitem__(self, at, value):
        self.buffer[at] = value

    def send(self):
        if not self.started:
            self.copy.start()
            self.started = True


def push(ref):
    if isinstance(ref, Pushed):
        ref.send()


def call(body, outs, scratch=(), scalars=0, fetch=0, name=None):
    def run(*operands):
        first = len(operands) - fetch
        far = [len(out) == 3 for out in outs]
        fetched = operands[first:]
        sent = [out for out in outs if len(out) == 3]
        ends = (first, fetch, len(outs), fetch, len(sent), len(scratch), 1, 1)

        def kernel(*refs):
            groups, at = [], 0
            for count in ends:
                groups.append(refs[at : at + count])
                at += count
            here, there, results, in_buffers, out_buffers, rest, (in_sems,), (out_sems,) = groups
            pulled = [Pulled(ref, in_buffers[k], in_sems.at[k]) for k, ref in enumerate(there)]
            made, pushed = [], []
            for ref, is_far in zip(results, far):
                if is_far:
                    k = len(pushed)
                    pushed.append(Pushed(ref, out_buffers[k], out_sems.at[k]))
                    ref = pushed[k]
                made.append(ref)
            body(*here, *pulled, *made, *rest)
            for ref in pushed:
                ref.send()
            for ref in pushed:
                ref.copy.wait()

        spec = pl.BlockSpec(memory_space=pltpu.VMEM)
        small = pl.BlockSpec(memory_space=pltpu.SMEM)
        apart = pl.BlockSpec(memory_space=pltpu.HBM)
        return pl.pallas_call(
            kernel,
            out_shape=[
                pltpu.HBM(out[0], out[1]) if is_far else jax.ShapeDtypeStruct(out[0], out[1])
                for out, is_far in zip(outs, far)
            ],
            in_specs=[small] * scalars + [spec] * (first - scalars) + [apart] * fetch,
            out_specs=[apart if is_far else spec for is_far in far],
            scratch_shapes=[pltpu.VMEM(x.shape, x.dtype) for x in fetched]
            + [pltpu.VMEM(out[0], out[1]) for out in sent]
            + list(scratch)
            + [pltpu.SemaphoreType.DMA((max(1, fetch),)), pltpu.SemaphoreType.DMA((max(1, len(sent)),))],
            compiler_params=pltpu.CompilerParams(vmem_limit_bytes=24 * 1024 * 1024),
            name=name,
        )(*operands[:first], *[pltpu.with_memory_space_constraint(x, pltpu.HBM) for x in fetched])

    return run


def array(*shape, dtype=F32):
    return shape, dtype


def far(*shape, dtype=F32):
    return shape, dtype, True


def exchange(x):
    return lax.all_to_all(x, "tile", split_axis=0, concat_axis=0, tiled=True)


def deal(others, z):
    got = []
    for k, (shift, core) in enumerate(z.parts[1:]):
        pairs = [
            (s * z.devices + t, (s + shift) % z.samples * z.devices + (t ^ core))
            for s in range(z.samples)
            for t in range(z.devices)
        ]
        got.append(lax.ppermute(others[k], ("dp", "tile"), pairs))
    return got


def local(inputs, cotangent, w_first, w_second, w_down, edge_owner, corner_owner, neighbour_tile, seam_rotation):
    tiles_in, cot = inputs[0], cotangent[0]
    tiles, side, _, chan = tiles_in.shape
    z = Sizes(tiles, side, chan, lax.axis_size("tile"), lax.axis_size("dp"))
    scale = float(z.samples * z.devices * z.pixels) ** -0.5
    me = lax.axis_index("tile").astype(I32).reshape(1)
    sample = lax.axis_index("dp").astype(I32).reshape(1)
    half = side // 2
    down_pixels = half * half * tiles
    sent = array(z.devices, z.pair, chan, dtype=BF16)
    sent_far = far(z.devices, z.pair, chan, dtype=BF16)
    field, field16 = array(z.pixels, chan), array(z.pixels, chan, dtype=BF16)
    field16_far = far(z.pixels, chan, dtype=BF16)
    columns = array(z.column * side, 3 * chan, dtype=BF16)
    columns_far = far(z.column * side, 3 * chan, dtype=BF16)
    turned = array(9 * chan, chan, dtype=BF16)
    wide = vmem((side + 2) * z.line, 3 * chan, dtype=BF16)
    side_columns = (vmem(z.column * side, chan), vmem(z.column * side, chan))
    flat = vmem(z.pixels, chan)
    taps = vmem(9 * chan, chan)
    bind = functools.partial
    tables = (edge_owner.T, corner_owner.T, neighbour_tile.T, seam_rotation.T)
    others = len(z.parts) - 1

    (send,) = call(bind(pack_kernel, z), [sent_far], scalars=1, fetch=5, name="pack")(me, *tables, tiles_in)
    got = exchange(send)
    cot_rows = cot.transpose(1, 0, 2, 3).reshape(down_pixels, chan)
    index, back_second, turned_first, turned_second = call(
        bind(side_kernel, z),
        [
            array(24, max(z.sent, z.cells_up), dtype=I32),
            field,
            turned,
            turned,
        ],
        scalars=1,
        name="aside",
    )(me, *tables, cot_rows, w_down, w_first, w_second)
    send, hidden, columns_first = call(
        bind(first_kernel, z), [sent, field16, columns], side_columns, name="first"
    )(got, index, tiles_in, w_first)
    got = exchange(send)
    (slope_in,) = call(bind(again_kernel, z), [field], name="again")(columns_first, w_first)
    send, slope_second, hidden_second, columns_second = call(
        bind(second_kernel, z), [sent_far, field16, field16, columns_far], side_columns + (flat,), name="second"
    )(got, index, hidden, w_second, turned_second, back_second)
    got = exchange(send)
    (inner,) = call(bind(inner_kernel, z), [field], (wide,), name="inner")(slope_second, turned_second)
    features, early_own, *early_other = call(
        bind(early_kernel, z, scale),
        [array(down_pixels, chan, dtype=BF16), array(z.early, chan)] + [array(z.early, chan, dtype=BF16)] * others,
        (taps, vmem(2 * z.samples * z.early, chan), flat, vmem(down_pixels, 4 * chan, dtype=BF16)),
        scalars=2,
        name="early",
    )(sample, me, columns_second, slope_second, hidden_second, cot_rows, w_down)
    features = features.reshape(half, tiles, half, chan).transpose(1, 0, 2, 3)
    (early,) = call(gain_kernel, [array(z.early, chan)], name="gain")(early_own, *deal(early_other, z))
    slope_first, late_own, *late_other = call(
        bind(slope_kernel, z, scale),
        [field16, array(z.late, chan)] + [array(z.late, chan, dtype=BF16)] * others,
        (taps,),
        scalars=2,
        name="slope",
    )(sample, me, got, index, inner, slope_in, columns_first)
    late_got = deal(late_other, z)
    (send,) = call(bind(last_kernel, z), [sent], (flat,), name="last")(slope_first, turned_first, index)
    (inner,) = call(bind(inner_kernel, z), [field], (wide,), name="inner")(slope_first, turned_first)
    send, inner, features = lax.optimization_barrier((send, inner, features))
    (send,) = call(
        bind(join_kernel, z),
        [array(z.devices, z.pair + z.chunk, chan, dtype=BF16)],
        (vmem(z.devices * z.chunk, chan),),
        name="join",
    )(send, early, late_own, *late_got)
    got = exchange(send)
    (chunk,) = call(bind(sum_kernel, z), [array(z.devices // 2, 2 * z.chunk, chan, dtype=BF16)], name="sum")(got)
    same_core = [list(range(core, z.devices, 2)) for core in range(2)]
    mine = lax.all_to_all(chunk, "tile", split_axis=0, concat_axis=0, tiled=True, axis_index_groups=same_core)
    (input_grad,) = call(bind(input_kernel, z), [array(tiles, side, side, chan)], name="input")(got, index, inner)
    other = lax.ppermute(mine, "tile", [(t, t ^ 1) for t in range(z.devices)])
    grad_first, grad_second, grad_down = call(
        bind(spread_kernel, z),
        [array(z.tap_rows, chan), array(z.tap_rows, chan), array(z.down_rows, chan)],
        scalars=1,
        name="spread",
    )(me, mine, other)
    return features[None], input_grad[None], grad_first, grad_second, grad_down


def solution(mesh):
    split = P("dp", "tile", None, None, None)
    return jax.shard_map(
        local,
        mesh=mesh,
        in_specs=(split, split, P(), P(), P(), P(), P(), P(), P()),
        out_specs=(split, split, P("dp", None), P("dp", None), P("dp", None)),
        check_vma=False,
    )
```

```python
import functools
import jax
import jax.numpy as jnp
from jax import lax
from jax.experimental import pallas as pl
from jax.experimental.pallas import tpu as pltpu
from jax.sharding import PartitionSpec as P

F32, BF16, I32 = jnp.float32, jnp.bfloat16, jnp.int32
LANES = 128
ORDERS = {
    16: (9, 7, 8, 12, 5, 4, 0, 6, 10, 13, 15, 2, 11, 3, 1, 14),
    8: (4, 2, 6, 3, 0, 1, 5, 7),
}


def order_of(count):
    return ORDERS.get(count, tuple(range(count)))


class Sizes:
    def __init__(self, tiles, side, chan, devices, samples):
        self.tiles, self.side, self.chan = tiles, side, chan
        self.devices, self.samples = devices, samples
        self.slots = max(2, 4 * tiles // devices + 1)
        self.pair = -(-self.slots * (side + 1) // 16) * 16
        self.sent = devices * self.pair
        self.line = tiles * side
        self.pixels = side * self.line
        self.column = (side + 2) * tiles
        self.cells = 2 * self.line + 2 * self.column
        self.cells_up = -(-self.cells // (2 * LANES)) * 2 * LANES
        self.tap_rows = 9 * chan // samples
        self.down_rows = 4 * chan // samples
        self.late = self.tap_rows // 2
        self.early = (self.tap_rows + self.down_rows) // 2
        self.chunk = -(-(self.early + self.late) // (16 * devices)) * 16
        self.parts = [(s, c) for s in range(samples) for c in range(2)]
        self.order = order_of(devices)
        self.place = tuple(self.order.index(device) for device in range(devices))
        self.ring = order_of(devices // 2)
        self.slot_rows = -(-self.slots // 8) * 8


def iota(shape, dim):
    return lax.broadcasted_iota(I32, shape, dim)


def mm(a, b):
    return jnp.dot(a.astype(BF16), b.astype(BF16), preferred_element_type=F32)


def mm_t(a, b):
    return lax.dot_general(a, b, (((0,), (0,)), ((), ())), preferred_element_type=F32)


def flag(cond):
    return jnp.where(cond, 1.0, 0.0).astype(BF16)


def pick_rows(index, width):
    rows = index.shape[0]
    lane = iota((rows, LANES), 1)
    return jnp.concatenate([flag(index == lane + at) for at in range(0, width, LANES)], axis=1)


def gather(index, source):
    half, chan = source.shape[0] // 2, source.shape[1]
    source = source.astype(BF16)
    right = index >= half
    wide = mm(pick_rows(jnp.where(right, index - half, index), half), jnp.concatenate([source[:half], source[half:]], axis=1))
    return jnp.where(right, wide[:, chan:], wide[:, :chan])


def pick_columns(index, height):
    shape = (height, index.shape[1])
    return flag(jnp.broadcast_to(index, shape) == iota(shape, 0))


def row_first(x):
    tiles, side, _, chan = x.shape
    x = x.astype(F32)
    return jnp.stack([x[:, r].reshape(tiles * side, chan) for r in range(side)], axis=0)


def relabel(values, table):
    if table == tuple(range(len(table))):
        return values
    new = jnp.zeros_like(values)
    for old, label in enumerate(table):
        new = jnp.where(values == old, label, new)
    return new


def sender_index(me, owners, local_ids, turns, z):
    requests = z.devices * z.tiles
    row8 = iota((8, requests), 0)
    matched = owners == me
    code = jnp.where(matched, local_ids * 16 + turns * 4 + (row8 & 3) + 1, 0).astype(F32)
    found = jnp.where(matched, 1.0, 0.0)

    def both(values):
        edge = jnp.sum(values[:4], axis=0, keepdims=True)
        corner = jnp.sum(values[4:], axis=0, keepdims=True)
        shape = (z.slot_rows, requests)
        return jnp.concatenate([jnp.broadcast_to(edge, shape), jnp.broadcast_to(corner, shape)], axis=0)

    column = iota((1, 1, requests), 2)
    cube = (z.devices, z.tiles, requests)
    earlier = (iota(cube, 0) == lax.div(column, z.tiles)) & (iota(cube, 1) < lax.rem(column, z.tiles))
    rank = mm(both(found), flag(earlier).reshape(requests, requests))
    slot = iota((2 * z.slot_rows, requests), 0)
    slot = jnp.where(slot < z.slot_rows, slot, slot - z.slot_rows)
    placed = jnp.where(slot.astype(F32) == rank, both(code), 0.0)
    row = iota((1, z.sent), 1)
    device, at = relabel(lax.div(row, z.pair), z.order), lax.rem(row, z.pair)
    cube = (z.devices, z.tiles, z.sent)
    rows = mm(placed, flag(iota(cube, 0) == device.reshape(1, 1, z.sent)).reshape(requests, z.sent))
    edges = z.slots * z.side
    is_edge = at < edges
    wanted = jnp.where(is_edge, lax.div(at, z.side), at - edges + z.slot_rows)
    wanted = jnp.where(at < edges + z.slots, wanted, -1)
    here = iota((2 * z.slot_rows, z.sent), 0) == wanted
    code = jnp.sum(jnp.where(here, rows, 0.0), axis=0, keepdims=True).astype(I32) - 1
    along = lax.rem(at, z.side)
    source, turn, towards = code >> 4, (code >> 2) & 3, code & 3
    end = z.side - 1
    i_edge = jnp.where(towards == 0, end, jnp.where(towards == 2, 0, along))
    j_edge = jnp.where(towards == 1, 0, jnp.where(towards == 3, end, along))
    i_corner = jnp.where((towards == 0) | (towards == 3), end, 0)
    j_corner = jnp.where(towards >= 2, end, 0)
    i = jnp.where(is_edge, i_edge, i_corner)
    j = jnp.where(is_edge, j_edge, j_corner)
    row = jnp.where(turn == 0, i, jnp.where(turn == 1, j, jnp.where(turn == 2, end - i, end - j)))
    col = jnp.where(turn == 0, j, jnp.where(turn == 1, end - i, jnp.where(turn == 2, end - j, i)))
    return jnp.where(code >= 0, row * z.line + source * z.side + col, -1)


def receiver_index(own, z):
    lane = iota((z.tiles, LANES), 1)
    lower = flag(iota((z.tiles, z.tiles), 1) < iota((z.tiles, z.tiles), 0))
    values = jnp.zeros((z.tiles, LANES), F32)
    for base in (0, 4):
        hits = [jnp.broadcast_to(own[:, base + k : base + k + 1], (z.tiles, LANES)) == lane for k in range(4)]
        named = sum(jnp.where(hit, 1.0, 0.0) for hit in hits)
        before = mm(lower, named)
        for k in range(4):
            rank = jnp.sum(jnp.where(hits[k], before, 0.0), axis=1, keepdims=True)
            values = jnp.where(lane == 2 * base + k, own[:, base + k : base + k + 1].astype(F32), values)
            values = jnp.where(lane == 2 * base + 4 + k, rank, values)
    ones = jnp.ones((LANES, LANES), BF16)

    def spread(tile, own_lane, is_edge, along):
        rows = tile.shape[0]
        lane = iota((rows, LANES), 1)
        here = mm(flag(tile[:, : z.tiles] == iota((rows, z.tiles), 1)), values)
        own = mm(jnp.where(lane == own_lane, here, 0.0), ones).astype(I32)
        rank = mm(jnp.where(lane == own_lane + 4, here, 0.0), ones).astype(I32)
        return own * z.pair + jnp.where(is_edge, rank * z.side + along, z.slots * z.side + rank)

    line = (z.tiles, z.side, LANES)
    tile = iota(line, 0).reshape(z.line, LANES)
    along = iota(line, 1).reshape(z.line, LANES)
    parts = [spread(tile, k, jnp.full(tile.shape, True), along) for k in (0, 2)]
    column = (z.side + 2, z.tiles, LANES)
    row = iota(column, 0).reshape(z.column, LANES)
    tile = iota(column, 1).reshape(z.column, LANES)
    is_edge = (row > 0) & (row <= z.side)
    for edge, top, bottom in ((3, 3, 2), (1, 0, 1)):
        own_lane = jnp.where(is_edge, edge, jnp.where(row == 0, 8 + top, 8 + bottom))
        parts.append(spread(tile, own_lane, is_edge, row - 1))
    parts.append(jnp.full((z.cells_up - z.cells, LANES), -1, I32))
    return jnp.concatenate(parts, axis=0)


def as_column(index):
    return jnp.transpose(jnp.broadcast_to(index.astype(F32), (LANES, index.shape[1]))).astype(I32)


def pack_kernel(z, me_ref, eo_ref, co_ref, ids_ref, turn_ref, x_ref, send_ref):
    owners = jnp.concatenate([eo_ref[...], co_ref[...]], axis=0)
    index = sender_index(me_ref[0], owners, ids_ref[...], turn_ref[...], z)
    pixels = row_first(x_ref[...]).reshape(z.pixels, z.chan)
    send_ref[...] = gather(as_column(index), pixels).astype(BF16).reshape(send_ref.shape)


def side_kernel(
    z, me_ref, eo_ref, co_ref, ids_ref, turn_ref, cot_ref, wd_ref, w1_ref, w2_ref,
    table_ref, back_ref, t1_ref, t2_ref,
):
    me = me_ref[0]
    owners = jnp.concatenate([eo_ref[...], co_ref[...]], axis=0)
    index = sender_index(me, owners, ids_ref[...], turn_ref[...], z)
    table_ref[0:8, : z.sent] = jnp.broadcast_to(index, (8, z.sent))
    shape = (z.tiles, z.devices * z.tiles)
    mine = flag(iota(shape, 1) == iota(shape, 0) + me * z.tiles)
    own = lax.dot_general(
        mine, owners.astype(F32).astype(BF16), (((1,), (1,)), ((), ())), preferred_element_type=F32
    )
    index = receiver_index(relabel(own.astype(I32), z.place), z)
    table_ref[8:16, : z.cells_up] = jnp.transpose(index.astype(F32))[0:8].astype(I32)
    cell = iota((16, z.cells_up), 1) + 1
    digits = jnp.where(iota((16, z.cells_up), 0) < 8, cell >> 4, cell & 15).astype(F32)
    found = mm(digits, pick_rows(index, z.sent))
    table_ref[16:24, : z.sent] = jnp.broadcast_to(found[0:1] * 16.0 + found[8:9] - 1.0, (8, z.sent)).astype(I32)
    chan, half = z.chan, z.side // 2
    for taps, out in ((w1_ref, t1_ref), (w2_ref, t2_ref)):
        for tap in range(9):
            rows = slice(tap * chan, (tap + 1) * chan)
            out[rows, :] = jnp.transpose(taps[rows, :].astype(F32)).astype(BF16)
    cot = cot_ref[...]
    part = half * z.tiles
    for p in range(2):
        for q in range(2):
            tap = wd_ref[(2 * p + q) * chan : (2 * p + q + 1) * chan, :]
            back = lax.dot_general(cot, tap, (((1,), (1,)), ((), ())), preferred_element_type=F32)
            for i in range(half):
                back_ref[pl.ds((2 * i + p) * z.line + q, part, stride=2), :] = back[i * part : (i + 1) * part]


def padded_columns(z, center, arrived, index, west_ref, east_ref, out_ref):
    rims = gather(index, arrived)
    north, south = rims[: z.line], rims[z.line : 2 * z.line]
    at = 2 * z.line
    west_ref[pl.ds(0, z.column, stride=z.side), :] = rims[at : at + z.column]
    east_ref[pl.ds(z.side - 1, z.column, stride=z.side), :] = rims[at + z.column : at + 2 * z.column]
    shape = (z.column, z.side, z.chan)
    middle = jnp.concatenate([north, center, south], axis=0).reshape(shape)
    place = iota(shape, 1)
    flat = (z.column * z.side, z.chan)
    left = jnp.where(place == 0, west_ref[...].reshape(shape), pltpu.roll(middle, 1, 1))
    right = jnp.where(place == z.side - 1, east_ref[...].reshape(shape), pltpu.roll(middle, z.side - 1, 1))
    out_ref[:, : z.chan] = left.reshape(flat).astype(BF16)
    out_ref[:, z.chan : 2 * z.chan] = middle.reshape(flat).astype(BF16)
    out_ref[:, 2 * z.chan :] = right.reshape(flat).astype(BF16)


def conv(z, columns_ref, w_ref):
    total = None
    for p in range(3):
        part = jnp.dot(
            columns_ref[p * z.line : p * z.line + z.pixels, :],
            w_ref[3 * p * z.chan : 3 * (p + 1) * z.chan, :],
            preferred_element_type=F32,
        )
        total = part if total is None else total + part
    return total


def silu_slope(v):
    s = 1.0 / (1.0 + jnp.exp(-v))
    return s * (1.0 + v * (1.0 - s))


def first_kernel(z, got_ref, index_ref, x_ref, w_ref, send_ref, hidden_ref, columns_ref, west_ref, east_ref):
    center = row_first(x_ref[...]).reshape(z.pixels, z.chan)
    padded_columns(z, center, got_ref[...].reshape(z.sent, z.chan), as_column(index_ref[8:9, : z.cells_up]), west_ref, east_ref, columns_ref)
    v = conv(z, columns_ref, w_ref)
    hidden = (v / (1.0 + jnp.exp(-v))).astype(BF16)
    send_ref[...] = gather(as_column(index_ref[0:1, : z.sent]), hidden).astype(BF16).reshape(send_ref.shape)
    hidden_ref[...] = hidden


def again_kernel(z, columns_ref, w_ref, slope_ref):
    slope_ref[...] = silu_slope(conv(z, columns_ref, w_ref))


def shifted(z, slope):
    cube = slope.reshape(slope.shape[0] // z.side, z.side, z.chan)
    place = iota(cube.shape, 1)
    after = jnp.where(place == z.side - 1, 0.0, pltpu.roll(cube, z.side - 1, 1))
    before = jnp.where(place == 0, 0.0, pltpu.roll(cube, 1, 1))
    return [part.reshape(slope.shape).astype(BF16) for part in (after, cube, before)]


def rims_back(z, slope, turned_ref, slope_ref):
    chan = z.chan
    parts = []
    for p, row in ((0, 0), (2, z.side - 1)):
        wide = jnp.concatenate(shifted(z, slope[row * z.line : (row + 1) * z.line]), axis=1)
        parts.append(jnp.dot(wide, turned_ref[3 * p * chan : 3 * (p + 1) * chan, :], preferred_element_type=F32))
    slope_ref[...] = slope
    blank = jnp.zeros((2 * z.tiles, chan), F32)
    for start, q in ((0, 0), (z.side - 1, 2)):
        line = slope_ref[pl.ds(start, z.side * z.tiles, stride=z.side), :]
        line = jnp.concatenate([blank, line, blank], axis=0).astype(BF16)
        side = None
        for p in range(3):
            part = jnp.dot(
                line[(2 - p) * z.tiles : (2 - p) * z.tiles + z.column],
                turned_ref[(3 * p + q) * chan : (3 * p + q + 1) * chan, :],
                preferred_element_type=F32,
            )
            side = part if side is None else side + part
        parts.append(side)
    parts.append(jnp.zeros((z.cells_up - z.cells, chan), F32))
    return jnp.concatenate(parts, axis=0).astype(BF16)


def inner_back(z, slope, turned_ref, wide_ref):
    chan = z.chan
    zero = jnp.zeros((z.line, 3 * chan), BF16)
    wide_ref[: z.line, :] = zero
    wide_ref[z.line + z.pixels :, :] = zero
    for q, part in enumerate(shifted(z, slope)):
        wide_ref[z.line : z.line + z.pixels, q * chan : (q + 1) * chan] = part
    total = None
    for p in range(3):
        part = jnp.dot(
            wide_ref[(2 - p) * z.line : (2 - p) * z.line + z.pixels, :],
            turned_ref[3 * p * chan : 3 * (p + 1) * chan, :],
            preferred_element_type=F32,
        )
        total = part if total is None else total + part
    return total


def second_kernel(
    z, got_ref, index_ref, hidden_ref, w_ref, turned_ref, back_ref,
    send_ref, slope_ref, out_ref, columns_ref, west_ref, east_ref, scratch_ref,
):
    center = hidden_ref[...].astype(F32)
    padded_columns(z, center, got_ref[...].reshape(z.sent, z.chan), as_column(index_ref[8:9, : z.cells_up]), west_ref, east_ref, columns_ref)
    push(columns_ref)
    v = conv(z, columns_ref, w_ref)
    s = 1.0 / (1.0 + jnp.exp(-v))
    out_ref[...] = (v * s).astype(BF16)
    push(out_ref)
    slope = (back_ref[...] * (s * (1.0 + v * (1.0 - s)))).astype(BF16)
    slope_ref[...] = slope
    push(slope_ref)
    rims = rims_back(z, slope.astype(F32), turned_ref, scratch_ref)
    send_ref[...] = gather(as_column(index_ref[16:17, : z.sent]), rims).astype(BF16).reshape(send_ref.shape)


def tap_products(z, columns_ref, slope, scale, total_ref):
    blank = jnp.zeros((2 * z.line, z.chan), BF16)
    padded = jnp.concatenate([blank, slope, blank], axis=0)
    rows = (z.side + 2) * z.line
    wide = jnp.concatenate([padded[(2 - p) * z.line : (2 - p) * z.line + rows] for p in range(3)], axis=1)
    total = mm_t(columns_ref[...], wide) * scale
    for p in range(3):
        total_ref[3 * p * z.chan : 3 * (p + 1) * z.chan, :] = total[:, p * z.chan : (p + 1) * z.chan]


def deal_parts(z, sample_ref, me_ref, source_ref, own_ref, other_refs):
    rows = own_ref.shape[0]
    for k, (shift, core) in enumerate(z.parts):
        whose = lax.rem(sample_ref[0] + shift, z.samples)
        half = jnp.bitwise_xor(me_ref[0] & 1, core)
        part = source_ref[pl.ds((2 * whose + half) * rows, rows), :]
        if k == 0:
            own_ref[...] = part
        else:
            other_refs[k - 1][...] = part.astype(BF16)


def early_kernel(
    z, scale, sample_ref, me_ref, columns_ref, slope_ref, hidden_ref, cot_ref, wd_ref, feature_ref, own_ref, *refs
):
    other_refs, (taps_ref, total_ref, flat_ref, block_ref) = refs[:-4], refs[-4:]
    chan, half = z.chan, z.side // 2
    part = half * z.tiles
    tap_products(z, columns_ref, slope_ref[...], scale, taps_ref)
    flat_ref[...] = hidden_ref[...].astype(F32)
    for i in range(half):
        for p in range(2):
            for q in range(2):
                block_ref[i * part : (i + 1) * part, (2 * p + q) * chan : (2 * p + q + 1) * chan] = flat_ref[
                    pl.ds((2 * i + p) * z.line + q, part, stride=2), :
                ].astype(BF16)
    block = block_ref[...]
    feature_ref[...] = jnp.dot(block, wd_ref[...], preferred_element_type=F32).astype(BF16)
    down = mm_t(block, cot_ref[...]) * scale
    both = z.tap_rows + z.down_rows
    for s in range(z.samples):
        total_ref[s * both : s * both + z.tap_rows, :] = taps_ref[s * z.tap_rows : (s + 1) * z.tap_rows, :]
        total_ref[s * both + z.tap_rows : (s + 1) * both, :] = down[s * z.down_rows : (s + 1) * z.down_rows]
    deal_parts(z, sample_ref, me_ref, total_ref, own_ref, other_refs)


def inner_kernel(z, slope_ref, turned_ref, inner_ref, wide_ref):
    inner_ref[...] = inner_back(z, slope_ref[...].astype(F32), turned_ref, wide_ref)


def slope_kernel(
    z, scale, sample_ref, me_ref, got_ref, pix_row_ref, inner_ref, slope_in_ref, columns_ref,
    slope_ref, own_ref, *refs,
):
    other_refs, total_ref = refs[:-1], refs[-1]
    back = inner_ref[...] + mm(pick_columns(pix_row_ref[0:1, : z.sent], z.pixels), got_ref[...].reshape(z.sent, z.chan))
    slope = (back * slope_in_ref[...]).astype(BF16)
    slope_ref[...] = slope
    tap_products(z, columns_ref, slope, scale, total_ref)
    deal_parts(z, sample_ref, me_ref, total_ref, own_ref, other_refs)


def last_kernel(z, slope_ref, turned_ref, index_ref, send_ref, scratch_ref):
    rims = rims_back(z, slope_ref[...].astype(F32), turned_ref, scratch_ref)
    send_ref[...] = gather(as_column(index_ref[16:17, : z.sent]), rims).astype(BF16).reshape(send_ref.shape)


def gain_kernel(own_ref, *refs):
    others, out_ref = refs[:-1], refs[-1]
    total = own_ref[...]
    for other in others:
        total = total + other[...].astype(F32)
    out_ref[...] = total


def join_kernel(z, rim_ref, early_ref, late_ref, *refs):
    others, (send_ref, total_ref) = refs[:-2], refs[-2:]
    late = late_ref[...]
    for other in others:
        late = late + other[...].astype(F32)
    total_ref[: z.early, :] = early_ref[...]
    total_ref[z.early : z.early + z.late, :] = late
    spare = z.devices * z.chunk - z.early - z.late
    if spare:
        total_ref[z.early + z.late :, :] = jnp.zeros((spare, z.chan), F32)
    send_ref[:, : z.pair, :] = rim_ref[...]
    send_ref[:, z.pair :, :] = total_ref[...].astype(BF16).reshape(z.devices, z.chunk, z.chan)


def sum_kernel(z, got_ref, out_ref):
    sums = []
    for core in range(2):
        first, *rest = [z.place[device] for device in range(core, z.devices, 2)]
        total = got_ref[first, z.pair :, :].astype(F32)
        for k in rest:
            total = total + got_ref[k, z.pair :, :].astype(F32)
        sums.append(total.astype(BF16))
    for k in range(z.devices // 2):
        for core in range(2):
            out_ref[k, core * z.chunk : (core + 1) * z.chunk, :] = sums[core]


def input_kernel(z, got_ref, pix_row_ref, inner_ref, out_ref):
    arrived = got_ref[:, : z.pair, :].reshape(z.sent, z.chan)
    total = inner_ref[...] + mm(pick_columns(pix_row_ref[0:1, : z.sent], z.pixels), arrived)
    for r in range(z.side):
        out_ref[:, r] = total[r * z.line : (r + 1) * z.line].reshape(z.tiles, z.side, z.chan)


def spread_kernel(z, me_ref, mine_ref, other_ref, one_ref, two_ref, low_ref):
    first = (me_ref[0] & 1) == 0
    mine, other = mine_ref[...].astype(F32), other_ref[...].astype(F32)
    halves = []
    for core in range(2):
        rows = slice(core * z.chunk, (core + 1) * z.chunk)
        a, b = mine[:, rows], other[:, rows]
        by_core = jnp.where(first, a, b), jnp.where(first, b, a)
        chunks = [by_core[device % 2][z.ring.index(device // 2)] for device in z.order]
        halves.append(jnp.concatenate(chunks, axis=0))
    one_ref[...] = jnp.concatenate([half[z.early : z.early + z.late] for half in halves], axis=0)
    early = jnp.concatenate([half[: z.early] for half in halves], axis=0)
    two_ref[...] = early[: z.tap_rows]
    low_ref[...] = early[z.tap_rows :]


def vmem(*shape, dtype=F32):
    return pltpu.VMEM(shape, dtype)


class Pulled:
    def __init__(self, source, buffer, semaphore):
        self.buffer, self.shape, self.waits = buffer, buffer.shape, True
        self.copy = pltpu.make_async_copy(source, buffer, semaphore)
        self.copy.start()

    def __getitem__(self, at):
        if self.waits:
            self.copy.wait()
            self.waits = False
        return self.buffer[at]


class Pushed:
    def __init__(self, target, buffer, semaphore):
        self.buffer, self.shape, self.started = buffer, buffer.shape, False
        self.copy = pltpu.make_async_copy(buffer, target, semaphore)

    def __getitem__(self, at):
        return self.buffer[at]

    def __setitem__(self, at, value):
        self.buffer[at] = value

    def send(self):
        if not self.started:
            self.copy.start()
            self.started = True


def push(ref):
    if isinstance(ref, Pushed):
        ref.send()


def call(body, outs, scratch=(), scalars=0, fetch=0, name=None):
    def run(*operands):
        first = len(operands) - fetch
        far = [len(out) == 3 for out in outs]
        fetched = operands[first:]
        sent = [out for out in outs if len(out) == 3]
        ends = (first, fetch, len(outs), fetch, len(sent), len(scratch), 1, 1)

        def kernel(*refs):
            groups, at = [], 0
            for count in ends:
                groups.append(refs[at : at + count])
                at += count
            here, there, results, in_buffers, out_buffers, rest, (in_sems,), (out_sems,) = groups
            pulled = [Pulled(ref, in_buffers[k], in_sems.at[k]) for k, ref in enumerate(there)]
            made, pushed = [], []
            for ref, is_far in zip(results, far):
                if is_far:
                    k = len(pushed)
                    pushed.append(Pushed(ref, out_buffers[k], out_sems.at[k]))
                    ref = pushed[k]
                made.append(ref)
            body(*here, *pulled, *made, *rest)
            for ref in pushed:
                ref.send()
            for ref in pushed:
                ref.copy.wait()

        spec = pl.BlockSpec(memory_space=pltpu.VMEM)
        small = pl.BlockSpec(memory_space=pltpu.SMEM)
        apart = pl.BlockSpec(memory_space=pltpu.HBM)
        return pl.pallas_call(
            kernel,
            out_shape=[
                pltpu.HBM(out[0], out[1]) if is_far else jax.ShapeDtypeStruct(out[0], out[1])
                for out, is_far in zip(outs, far)
            ],
            in_specs=[small] * scalars + [spec] * (first - scalars) + [apart] * fetch,
            out_specs=[apart if is_far else spec for is_far in far],
            scratch_shapes=[pltpu.VMEM(x.shape, x.dtype) for x in fetched]
            + [pltpu.VMEM(out[0], out[1]) for out in sent]
            + list(scratch)
            + [pltpu.SemaphoreType.DMA((max(1, fetch),)), pltpu.SemaphoreType.DMA((max(1, len(sent)),))],
            compiler_params=pltpu.CompilerParams(vmem_limit_bytes=24 * 1024 * 1024),
            name=name,
        )(*operands[:first], *[pltpu.with_memory_space_constraint(x, pltpu.HBM) for x in fetched])

    return run


def array(*shape, dtype=F32):
    return shape, dtype


def far(*shape, dtype=F32):
    return shape, dtype, True


def exchange(x, groups):
    return lax.all_to_all(x, "tile", split_axis=0, concat_axis=0, tiled=True, axis_index_groups=groups)


def deal(others, z):
    got = []
    for k, (shift, core) in enumerate(z.parts[1:]):
        pairs = [
            (s * z.devices + t, (s + shift) % z.samples * z.devices + (t ^ core))
            for s in range(z.samples)
            for t in range(z.devices)
        ]
        got.append(lax.ppermute(others[k], ("dp", "tile"), pairs))
    return got


def local(inputs, cotangent, w_first, w_second, w_down, edge_owner, corner_owner, neighbour_tile, seam_rotation):
    tiles_in, cot = inputs[0], cotangent[0]
    tiles, side, _, chan = tiles_in.shape
    z = Sizes(tiles, side, chan, lax.axis_size("tile"), lax.axis_size("dp"))
    scale = float(z.samples * z.devices * z.pixels) ** -0.5
    me = lax.axis_index("tile").astype(I32).reshape(1)
    sample = lax.axis_index("dp").astype(I32).reshape(1)
    half = side // 2
    down_pixels = half * half * tiles
    sent = array(z.devices, z.pair, chan, dtype=BF16)
    sent_far = far(z.devices, z.pair, chan, dtype=BF16)
    field, field16 = array(z.pixels, chan), array(z.pixels, chan, dtype=BF16)
    field16_far = far(z.pixels, chan, dtype=BF16)
    columns = array(z.column * side, 3 * chan, dtype=BF16)
    columns_far = far(z.column * side, 3 * chan, dtype=BF16)
    turned = array(9 * chan, chan, dtype=BF16)
    wide = vmem((side + 2) * z.line, 3 * chan, dtype=BF16)
    side_columns = (vmem(z.column * side, chan), vmem(z.column * side, chan))
    flat = vmem(z.pixels, chan)
    taps = vmem(9 * chan, chan)
    bind = functools.partial
    tables = (edge_owner.T, corner_owner.T, neighbour_tile.T, seam_rotation.T)
    others = len(z.parts) - 1
    everyone = [list(z.order)]
    same_core = [[2 * chip + core for chip in z.ring] for core in range(2)]

    (send,) = call(bind(pack_kernel, z), [sent_far], scalars=1, fetch=5, name="pack")(me, *tables, tiles_in)
    got = exchange(send, everyone)
    cot_rows = cot.transpose(1, 0, 2, 3).reshape(down_pixels, chan)
    index, back_second, turned_first, turned_second = call(
        bind(side_kernel, z),
        [
            array(24, max(z.sent, z.cells_up), dtype=I32),
            field,
            turned,
            turned,
        ],
        scalars=1,
        name="aside",
    )(me, *tables, cot_rows, w_down, w_first, w_second)
    send, hidden, columns_first = call(
        bind(first_kernel, z), [sent, field16, columns], side_columns, name="first"
    )(got, index, tiles_in, w_first)
    got = exchange(send, everyone)
    (slope_in,) = call(bind(again_kernel, z), [field], name="again")(columns_first, w_first)
    send, slope_second, hidden_second, columns_second = call(
        bind(second_kernel, z), [sent_far, field16, field16, columns_far], side_columns + (flat,), name="second"
    )(got, index, hidden, w_second, turned_second, back_second)
    got = exchange(send, everyone)
    (inner,) = call(bind(inner_kernel, z), [field], (wide,), name="inner")(slope_second, turned_second)
    features, early_own, *early_other = call(
        bind(early_kernel, z, scale),
        [array(down_pixels, chan, dtype=BF16), array(z.early, chan)] + [array(z.early, chan, dtype=BF16)] * others,
        (taps, vmem(2 * z.samples * z.early, chan), flat, vmem(down_pixels, 4 * chan, dtype=BF16)),
        scalars=2,
        name="early",
    )(sample, me, columns_second, slope_second, hidden_second, cot_rows, w_down)
    features = features.reshape(half, tiles, half, chan).transpose(1, 0, 2, 3)
    (early,) = call(gain_kernel, [array(z.early, chan)], name="gain")(early_own, *deal(early_other, z))
    slope_first, late_own, *late_other = call(
        bind(slope_kernel, z, scale),
        [field16, array(z.late, chan)] + [array(z.late, chan, dtype=BF16)] * others,
        (taps,),
        scalars=2,
        name="slope",
    )(sample, me, got, index, inner, slope_in, columns_first)
    late_got = deal(late_other, z)
    (send,) = call(bind(last_kernel, z), [sent], (flat,), name="last")(slope_first, turned_first, index)
    (inner,) = call(bind(inner_kernel, z), [field], (wide,), name="inner")(slope_first, turned_first)
    send, inner, features = lax.optimization_barrier((send, inner, features))
    (send,) = call(
        bind(join_kernel, z),
        [array(z.devices, z.pair + z.chunk, chan, dtype=BF16)],
        (vmem(z.devices * z.chunk, chan),),
        name="join",
    )(send, early, late_own, *late_got)
    got = exchange(send, everyone)
    (chunk,) = call(bind(sum_kernel, z), [array(z.devices // 2, 2 * z.chunk, chan, dtype=BF16)], name="sum")(got)
    mine = exchange(chunk, same_core)
    (input_grad,) = call(bind(input_kernel, z), [array(tiles, side, side, chan)], name="input")(got, index, inner)
    other = lax.ppermute(mine, "tile", [(t, t ^ 1) for t in range(z.devices)])
    grad_first, grad_second, grad_down = call(
        bind(spread_kernel, z),
        [array(z.tap_rows, chan), array(z.tap_rows, chan), array(z.down_rows, chan)],
        scalars=1,
        name="spread",
    )(me, mine, other)
    return features[None], input_grad[None], grad_first, grad_second, grad_down


def solution(mesh):
    split = P("dp", "tile", None, None, None)
    return jax.shard_map(
        local,
        mesh=mesh,
        in_specs=(split, split, P(), P(), P(), P(), P(), P(), P()),
        out_specs=(split, split, P("dp", None), P("dp", None), P("dp", None)),
        check_vma=False,
    )
```

```python
import functools
import jax
import jax.numpy as jnp
from jax import lax
from jax.experimental import pallas as pl
from jax.experimental.pallas import tpu as pltpu
from jax.sharding import PartitionSpec as P

F32, BF16, I32 = jnp.float32, jnp.bfloat16, jnp.int32
LANES = 128
ORDERS = {
    16: (9, 7, 8, 12, 5, 4, 0, 13, 10, 15, 6, 2, 11, 3, 1, 14),
    8: (5, 2, 0, 6, 1, 7, 3, 4),
}


def order_of(count):
    return ORDERS.get(count, tuple(range(count)))


class Sizes:
    def __init__(self, tiles, side, chan, devices, samples):
        self.tiles, self.side, self.chan = tiles, side, chan
        self.devices, self.samples = devices, samples
        self.slots = max(2, 4 * tiles // devices + 1)
        self.pair = -(-self.slots * (side + 1) // 16) * 16
        self.sent = devices * self.pair
        self.line = tiles * side
        self.pixels = side * self.line
        self.column = (side + 2) * tiles
        self.cells = 2 * self.line + 2 * self.column
        self.cells_up = -(-self.cells // (2 * LANES)) * 2 * LANES
        self.tap_rows = 9 * chan // samples
        self.down_rows = 4 * chan // samples
        self.late = self.tap_rows // 2
        self.early = (self.tap_rows + self.down_rows) // 2
        self.chunk = -(-(self.early + self.late) // (16 * devices)) * 16
        self.parts = [(s, c) for s in range(samples) for c in range(2)]
        self.order = order_of(devices)
        self.place = tuple(self.order.index(device) for device in range(devices))
        self.ring = order_of(devices // 2)
        self.slot_rows = -(-self.slots // 8) * 8


def iota(shape, dim):
    return lax.broadcasted_iota(I32, shape, dim)


def mm(a, b):
    return jnp.dot(a.astype(BF16), b.astype(BF16), preferred_element_type=F32)


def mm_t(a, b):
    return lax.dot_general(a, b, (((0,), (0,)), ((), ())), preferred_element_type=F32)


def flag(cond):
    return jnp.where(cond, 1.0, 0.0).astype(BF16)


def pick_rows(index, width):
    rows = index.shape[0]
    lane = iota((rows, LANES), 1)
    return jnp.concatenate([flag(index == lane + at) for at in range(0, width, LANES)], axis=1)


def gather(index, source):
    half, chan = source.shape[0] // 2, source.shape[1]
    source = source.astype(BF16)
    right = index >= half
    wide = mm(pick_rows(jnp.where(right, index - half, index), half), jnp.concatenate([source[:half], source[half:]], axis=1))
    return jnp.where(right, wide[:, chan:], wide[:, :chan])


def pick_columns(index, height):
    shape = (height, index.shape[1])
    return flag(jnp.broadcast_to(index, shape) == iota(shape, 0))


def row_first(x):
    tiles, side, _, chan = x.shape
    x = x.astype(F32)
    return jnp.stack([x[:, r].reshape(tiles * side, chan) for r in range(side)], axis=0)


def relabel(values, table):
    if table == tuple(range(len(table))):
        return values
    new = jnp.zeros_like(values)
    for old, label in enumerate(table):
        new = jnp.where(values == old, label, new)
    return new


def sender_index(me, owners, local_ids, turns, z):
    requests = z.devices * z.tiles
    row8 = iota((8, requests), 0)
    matched = owners == me
    code = jnp.where(matched, local_ids * 16 + turns * 4 + (row8 & 3) + 1, 0).astype(F32)
    found = jnp.where(matched, 1.0, 0.0)

    def both(values):
        edge = jnp.sum(values[:4], axis=0, keepdims=True)
        corner = jnp.sum(values[4:], axis=0, keepdims=True)
        shape = (z.slot_rows, requests)
        return jnp.concatenate([jnp.broadcast_to(edge, shape), jnp.broadcast_to(corner, shape)], axis=0)

    column = iota((1, 1, requests), 2)
    cube = (z.devices, z.tiles, requests)
    earlier = (iota(cube, 0) == lax.div(column, z.tiles)) & (iota(cube, 1) < lax.rem(column, z.tiles))
    rank = mm(both(found), flag(earlier).reshape(requests, requests))
    slot = iota((2 * z.slot_rows, requests), 0)
    slot = jnp.where(slot < z.slot_rows, slot, slot - z.slot_rows)
    placed = jnp.where(slot.astype(F32) == rank, both(code), 0.0)
    row = iota((1, z.sent), 1)
    device, at = relabel(lax.div(row, z.pair), z.order), lax.rem(row, z.pair)
    cube = (z.devices, z.tiles, z.sent)
    rows = mm(placed, flag(iota(cube, 0) == device.reshape(1, 1, z.sent)).reshape(requests, z.sent))
    edges = z.slots * z.side
    is_edge = at < edges
    wanted = jnp.where(is_edge, lax.div(at, z.side), at - edges + z.slot_rows)
    wanted = jnp.where(at < edges + z.slots, wanted, -1)
    here = iota((2 * z.slot_rows, z.sent), 0) == wanted
    code = jnp.sum(jnp.where(here, rows, 0.0), axis=0, keepdims=True).astype(I32) - 1
    along = lax.rem(at, z.side)
    source, turn, towards = code >> 4, (code >> 2) & 3, code & 3
    end = z.side - 1
    i_edge = jnp.where(towards == 0, end, jnp.where(towards == 2, 0, along))
    j_edge = jnp.where(towards == 1, 0, jnp.where(towards == 3, end, along))
    i_corner = jnp.where((towards == 0) | (towards == 3), end, 0)
    j_corner = jnp.where(towards >= 2, end, 0)
    i = jnp.where(is_edge, i_edge, i_corner)
    j = jnp.where(is_edge, j_edge, j_corner)
    row = jnp.where(turn == 0, i, jnp.where(turn == 1, j, jnp.where(turn == 2, end - i, end - j)))
    col = jnp.where(turn == 0, j, jnp.where(turn == 1, end - i, jnp.where(turn == 2, end - j, i)))
    return jnp.where(code >= 0, row * z.line + source * z.side + col, -1)


def receiver_index(own, z):
    lane = iota((z.tiles, LANES), 1)
    lower = flag(iota((z.tiles, z.tiles), 1) < iota((z.tiles, z.tiles), 0))
    values = jnp.zeros((z.tiles, LANES), F32)
    for base in (0, 4):
        hits = [jnp.broadcast_to(own[:, base + k : base + k + 1], (z.tiles, LANES)) == lane for k in range(4)]
        named = sum(jnp.where(hit, 1.0, 0.0) for hit in hits)
        before = mm(lower, named)
        for k in range(4):
            rank = jnp.sum(jnp.where(hits[k], before, 0.0), axis=1, keepdims=True)
            values = jnp.where(lane == 2 * base + k, own[:, base + k : base + k + 1].astype(F32), values)
            values = jnp.where(lane == 2 * base + 4 + k, rank, values)
    ones = jnp.ones((LANES, LANES), BF16)

    def spread(tile, own_lane, is_edge, along):
        rows = tile.shape[0]
        lane = iota((rows, LANES), 1)
        here = mm(flag(tile[:, : z.tiles] == iota((rows, z.tiles), 1)), values)
        own = mm(jnp.where(lane == own_lane, here, 0.0), ones).astype(I32)
        rank = mm(jnp.where(lane == own_lane + 4, here, 0.0), ones).astype(I32)
        return own * z.pair + jnp.where(is_edge, rank * z.side + along, z.slots * z.side + rank)

    line = (z.tiles, z.side, LANES)
    tile = iota(line, 0).reshape(z.line, LANES)
    along = iota(line, 1).reshape(z.line, LANES)
    parts = [spread(tile, k, jnp.full(tile.shape, True), along) for k in (0, 2)]
    column = (z.side + 2, z.tiles, LANES)
    row = iota(column, 0).reshape(z.column, LANES)
    tile = iota(column, 1).reshape(z.column, LANES)
    is_edge = (row > 0) & (row <= z.side)
    for edge, top, bottom in ((3, 3, 2), (1, 0, 1)):
        own_lane = jnp.where(is_edge, edge, jnp.where(row == 0, 8 + top, 8 + bottom))
        parts.append(spread(tile, own_lane, is_edge, row - 1))
    parts.append(jnp.full((z.cells_up - z.cells, LANES), -1, I32))
    return jnp.concatenate(parts, axis=0)


def as_column(index):
    return jnp.transpose(jnp.broadcast_to(index.astype(F32), (LANES, index.shape[1]))).astype(I32)


def pack_kernel(z, me_ref, eo_ref, co_ref, ids_ref, turn_ref, x_ref, send_ref):
    owners = jnp.concatenate([eo_ref[...], co_ref[...]], axis=0)
    index = sender_index(me_ref[0], owners, ids_ref[...], turn_ref[...], z)
    pixels = row_first(x_ref[...]).reshape(z.pixels, z.chan)
    send_ref[...] = gather(as_column(index), pixels).astype(BF16).reshape(send_ref.shape)


def side_kernel(
    z, me_ref, eo_ref, co_ref, ids_ref, turn_ref, cot_ref, wd_ref, w1_ref, w2_ref,
    table_ref, back_ref, t1_ref, t2_ref,
):
    me = me_ref[0]
    owners = jnp.concatenate([eo_ref[...], co_ref[...]], axis=0)
    index = sender_index(me, owners, ids_ref[...], turn_ref[...], z)
    table_ref[0:8, : z.sent] = jnp.broadcast_to(index, (8, z.sent))
    shape = (z.tiles, z.devices * z.tiles)
    mine = flag(iota(shape, 1) == iota(shape, 0) + me * z.tiles)
    own = lax.dot_general(
        mine, owners.astype(F32).astype(BF16), (((1,), (1,)), ((), ())), preferred_element_type=F32
    )
    index = receiver_index(relabel(own.astype(I32), z.place), z)
    table_ref[8:16, : z.cells_up] = jnp.transpose(index.astype(F32))[0:8].astype(I32)
    cell = iota((16, z.cells_up), 1) + 1
    digits = jnp.where(iota((16, z.cells_up), 0) < 8, cell >> 4, cell & 15).astype(F32)
    found = mm(digits, pick_rows(index, z.sent))
    table_ref[16:24, : z.sent] = jnp.broadcast_to(found[0:1] * 16.0 + found[8:9] - 1.0, (8, z.sent)).astype(I32)
    chan, half = z.chan, z.side // 2
    for taps, out in ((w1_ref, t1_ref), (w2_ref, t2_ref)):
        for tap in range(9):
            rows = slice(tap * chan, (tap + 1) * chan)
            out[rows, :] = jnp.transpose(taps[rows, :].astype(F32)).astype(BF16)
    cot = cot_ref[...]
    part = half * z.tiles
    for p in range(2):
        for q in range(2):
            tap = wd_ref[(2 * p + q) * chan : (2 * p + q + 1) * chan, :]
            back = lax.dot_general(cot, tap, (((1,), (1,)), ((), ())), preferred_element_type=F32)
            for i in range(half):
                back_ref[pl.ds((2 * i + p) * z.line + q, part, stride=2), :] = back[i * part : (i + 1) * part]


def padded_columns(z, center, arrived, index, west_ref, east_ref, out_ref):
    rims = gather(index, arrived)
    at = 2 * z.line
    strip = jnp.concatenate([rims[: z.line], center, rims[z.line : at], rims[at : at + 2 * z.column]], axis=0)
    fill_columns(z, strip, west_ref, east_ref, out_ref)
    return strip


def fill_columns(z, strip, west_ref, east_ref, out_ref):
    rows = z.column * z.side
    west_ref[pl.ds(0, z.column, stride=z.side), :] = strip[rows : rows + z.column]
    east_ref[pl.ds(z.side - 1, z.column, stride=z.side), :] = strip[rows + z.column :]
    shape = (z.column, z.side, z.chan)
    middle = strip[:rows].reshape(shape)
    place = iota(shape, 1)
    flat = (rows, z.chan)
    left = jnp.where(place == 0, west_ref[...].reshape(shape), pltpu.roll(middle, 1, 1))
    right = jnp.where(place == z.side - 1, east_ref[...].reshape(shape), pltpu.roll(middle, z.side - 1, 1))
    out_ref[:, : z.chan] = left.reshape(flat).astype(BF16)
    out_ref[:, z.chan : 2 * z.chan] = middle.reshape(flat).astype(BF16)
    out_ref[:, 2 * z.chan :] = right.reshape(flat).astype(BF16)


def conv(z, columns_ref, w_ref):
    total = None
    for p in range(3):
        part = jnp.dot(
            columns_ref[p * z.line : p * z.line + z.pixels, :],
            w_ref[3 * p * z.chan : 3 * (p + 1) * z.chan, :],
            preferred_element_type=F32,
        )
        total = part if total is None else total + part
    return total


def silu_slope(v):
    s = 1.0 / (1.0 + jnp.exp(-v))
    return s * (1.0 + v * (1.0 - s))


def first_kernel(z, got_ref, index_ref, x_ref, w_ref, send_ref, hidden_ref, strip_ref, columns_ref, west_ref, east_ref):
    center = row_first(x_ref[...]).reshape(z.pixels, z.chan)
    strip = padded_columns(z, center, got_ref[...].reshape(z.sent, z.chan), as_column(index_ref[8:9, : z.cells_up]), west_ref, east_ref, columns_ref)
    strip_ref[...] = strip.astype(BF16)
    v = conv(z, columns_ref, w_ref)
    hidden = (v / (1.0 + jnp.exp(-v))).astype(BF16)
    send_ref[...] = gather(as_column(index_ref[0:1, : z.sent]), hidden).astype(BF16).reshape(send_ref.shape)
    hidden_ref[...] = hidden


def again_kernel(z, strip_ref, w_ref, slope_ref, columns_ref, west_ref, east_ref):
    fill_columns(z, strip_ref[...].astype(F32), west_ref, east_ref, columns_ref)
    slope_ref[...] = silu_slope(conv(z, columns_ref, w_ref))


def shifted(z, slope):
    cube = slope.reshape(slope.shape[0] // z.side, z.side, z.chan)
    place = iota(cube.shape, 1)
    after = jnp.where(place == z.side - 1, 0.0, pltpu.roll(cube, z.side - 1, 1))
    before = jnp.where(place == 0, 0.0, pltpu.roll(cube, 1, 1))
    return [part.reshape(slope.shape).astype(BF16) for part in (after, cube, before)]


def rims_back(z, slope, turned_ref, slope_ref):
    chan = z.chan
    parts = []
    for p, row in ((0, 0), (2, z.side - 1)):
        wide = jnp.concatenate(shifted(z, slope[row * z.line : (row + 1) * z.line]), axis=1)
        parts.append(jnp.dot(wide, turned_ref[3 * p * chan : 3 * (p + 1) * chan, :], preferred_element_type=F32))
    slope_ref[...] = slope
    blank = jnp.zeros((2 * z.tiles, chan), F32)
    for start, q in ((0, 0), (z.side - 1, 2)):
        line = slope_ref[pl.ds(start, z.side * z.tiles, stride=z.side), :]
        line = jnp.concatenate([blank, line, blank], axis=0).astype(BF16)
        side = None
        for p in range(3):
            part = jnp.dot(
                line[(2 - p) * z.tiles : (2 - p) * z.tiles + z.column],
                turned_ref[(3 * p + q) * chan : (3 * p + q + 1) * chan, :],
                preferred_element_type=F32,
            )
            side = part if side is None else side + part
        parts.append(side)
    parts.append(jnp.zeros((z.cells_up - z.cells, chan), F32))
    return jnp.concatenate(parts, axis=0).astype(BF16)


def inner_back(z, slope, turned_ref, wide_ref):
    chan = z.chan
    zero = jnp.zeros((z.line, 3 * chan), BF16)
    wide_ref[: z.line, :] = zero
    wide_ref[z.line + z.pixels :, :] = zero
    for q, part in enumerate(shifted(z, slope)):
        wide_ref[z.line : z.line + z.pixels, q * chan : (q + 1) * chan] = part
    total = None
    for p in range(3):
        part = jnp.dot(
            wide_ref[(2 - p) * z.line : (2 - p) * z.line + z.pixels, :],
            turned_ref[3 * p * chan : 3 * (p + 1) * chan, :],
            preferred_element_type=F32,
        )
        total = part if total is None else total + part
    return total


def second_kernel(
    z, got_ref, index_ref, hidden_ref, w_ref, turned_ref, back_ref,
    send_ref, slope_ref, out_ref, strip_ref, columns_ref, west_ref, east_ref, scratch_ref,
):
    center = hidden_ref[...].astype(F32)
    strip = padded_columns(z, center, got_ref[...].reshape(z.sent, z.chan), as_column(index_ref[8:9, : z.cells_up]), west_ref, east_ref, columns_ref)
    strip_ref[...] = strip.astype(BF16)
    v = conv(z, columns_ref, w_ref)
    s = 1.0 / (1.0 + jnp.exp(-v))
    out_ref[...] = (v * s).astype(BF16)
    push(out_ref)
    slope = (back_ref[...] * (s * (1.0 + v * (1.0 - s)))).astype(BF16)
    slope_ref[...] = slope
    push(slope_ref)
    rims = rims_back(z, slope.astype(F32), turned_ref, scratch_ref)
    send_ref[...] = gather(as_column(index_ref[16:17, : z.sent]), rims).astype(BF16).reshape(send_ref.shape)


def tap_products(z, columns_ref, slope, scale, total_ref):
    blank = jnp.zeros((2 * z.line, z.chan), BF16)
    padded = jnp.concatenate([blank, slope, blank], axis=0)
    rows = (z.side + 2) * z.line
    wide = jnp.concatenate([padded[(2 - p) * z.line : (2 - p) * z.line + rows] for p in range(3)], axis=1)
    total = mm_t(columns_ref[...], wide) * scale
    for p in range(3):
        total_ref[3 * p * z.chan : 3 * (p + 1) * z.chan, :] = total[:, p * z.chan : (p + 1) * z.chan]


def deal_parts(z, sample_ref, me_ref, source_ref, own_ref, other_refs):
    rows = own_ref.shape[0]
    for k, (shift, core) in enumerate(z.parts):
        whose = lax.rem(sample_ref[0] + shift, z.samples)
        half = jnp.bitwise_xor(me_ref[0] & 1, core)
        part = source_ref[pl.ds((2 * whose + half) * rows, rows), :]
        if k == 0:
            own_ref[...] = part
        else:
            other_refs[k - 1][...] = part.astype(BF16)


def early_kernel(
    z, scale, sample_ref, me_ref, slope_ref, hidden_ref, cot_ref, wd_ref, strip_ref, feature_ref, own_ref, *refs
):
    other_refs, (taps_ref, total_ref, flat_ref, block_ref, columns_ref, west_ref, east_ref) = refs[:-7], refs[-7:]
    chan, half = z.chan, z.side // 2
    part = half * z.tiles
    flat_ref[...] = hidden_ref[...].astype(F32)
    for i in range(half):
        for p in range(2):
            for q in range(2):
                block_ref[i * part : (i + 1) * part, (2 * p + q) * chan : (2 * p + q + 1) * chan] = flat_ref[
                    pl.ds((2 * i + p) * z.line + q, part, stride=2), :
                ].astype(BF16)
    block = block_ref[...]
    feature_ref[...] = jnp.dot(block, wd_ref[...], preferred_element_type=F32).astype(BF16)
    down = mm_t(block, cot_ref[...]) * scale
    fill_columns(z, strip_ref[...].astype(F32), west_ref, east_ref, columns_ref)
    tap_products(z, columns_ref, slope_ref[...], scale, taps_ref)
    both = z.tap_rows + z.down_rows
    for s in range(z.samples):
        total_ref[s * both : s * both + z.tap_rows, :] = taps_ref[s * z.tap_rows : (s + 1) * z.tap_rows, :]
        total_ref[s * both + z.tap_rows : (s + 1) * both, :] = down[s * z.down_rows : (s + 1) * z.down_rows]
    deal_parts(z, sample_ref, me_ref, total_ref, own_ref, other_refs)


def inner_kernel(z, slope_ref, turned_ref, inner_ref, wide_ref):
    inner_ref[...] = inner_back(z, slope_ref[...].astype(F32), turned_ref, wide_ref)


def slope_kernel(
    z, scale, sample_ref, me_ref, got_ref, pix_row_ref, inner_ref, slope_in_ref, columns_ref,
    slope_ref, own_ref, *refs,
):
    other_refs, total_ref = refs[:-1], refs[-1]
    back = inner_ref[...] + mm(pick_columns(pix_row_ref[0:1, : z.sent], z.pixels), got_ref[...].reshape(z.sent, z.chan))
    slope = (back * slope_in_ref[...]).astype(BF16)
    slope_ref[...] = slope
    tap_products(z, columns_ref, slope, scale, total_ref)
    deal_parts(z, sample_ref, me_ref, total_ref, own_ref, other_refs)


def last_kernel(z, slope_ref, turned_ref, index_ref, send_ref, scratch_ref):
    rims = rims_back(z, slope_ref[...].astype(F32), turned_ref, scratch_ref)
    send_ref[...] = gather(as_column(index_ref[16:17, : z.sent]), rims).astype(BF16).reshape(send_ref.shape)


def gain_kernel(own_ref, *refs):
    others, out_ref = refs[:-1], refs[-1]
    total = own_ref[...]
    for other in others:
        total = total + other[...].astype(F32)
    out_ref[...] = total


def join_kernel(z, rim_ref, early_ref, late_ref, *refs):
    others, (send_ref, total_ref) = refs[:-2], refs[-2:]
    late = late_ref[...]
    for other in others:
        late = late + other[...].astype(F32)
    total_ref[: z.early, :] = early_ref[...]
    total_ref[z.early : z.early + z.late, :] = late
    spare = z.devices * z.chunk - z.early - z.late
    if spare:
        total_ref[z.early + z.late :, :] = jnp.zeros((spare, z.chan), F32)
    send_ref[:, : z.pair, :] = rim_ref[...]
    send_ref[:, z.pair :, :] = total_ref[...].astype(BF16).reshape(z.devices, z.chunk, z.chan)


def sum_kernel(z, got_ref, out_ref):
    sums = []
    for core in range(2):
        first, *rest = [z.place[device] for device in range(core, z.devices, 2)]
        total = got_ref[first, z.pair :, :].astype(F32)
        for k in rest:
            total = total + got_ref[k, z.pair :, :].astype(F32)
        sums.append(total.astype(BF16))
    for k in range(z.devices // 2):
        for core in range(2):
            out_ref[k, core * z.chunk : (core + 1) * z.chunk, :] = sums[core]


def input_kernel(z, got_ref, pix_row_ref, inner_ref, out_ref):
    arrived = got_ref[:, : z.pair, :].reshape(z.sent, z.chan)
    total = inner_ref[...] + mm(pick_columns(pix_row_ref[0:1, : z.sent], z.pixels), arrived)
    for r in range(z.side):
        out_ref[:, r] = total[r * z.line : (r + 1) * z.line].reshape(z.tiles, z.side, z.chan)


def spread_kernel(z, me_ref, mine_ref, other_ref, one_ref, two_ref, low_ref):
    first = (me_ref[0] & 1) == 0
    mine, other = mine_ref[...].astype(F32), other_ref[...].astype(F32)
    halves = []
    for core in range(2):
        rows = slice(core * z.chunk, (core + 1) * z.chunk)
        a, b = mine[:, rows], other[:, rows]
        by_core = jnp.where(first, a, b), jnp.where(first, b, a)
        chunks = [by_core[device % 2][z.ring.index(device // 2)] for device in z.order]
        halves.append(jnp.concatenate(chunks, axis=0))
    one_ref[...] = jnp.concatenate([half[z.early : z.early + z.late] for half in halves], axis=0)
    early = jnp.concatenate([half[: z.early] for half in halves], axis=0)
    two_ref[...] = early[: z.tap_rows]
    low_ref[...] = early[z.tap_rows :]


def vmem(*shape, dtype=F32):
    return pltpu.VMEM(shape, dtype)


class Pulled:
    def __init__(self, source, buffer, semaphore):
        self.buffer, self.shape, self.waits = buffer, buffer.shape, True
        self.copy = pltpu.make_async_copy(source, buffer, semaphore)
        self.copy.start()

    def __getitem__(self, at):
        if self.waits:
            self.copy.wait()
            self.waits = False
        return self.buffer[at]


class Pushed:
    def __init__(self, target, buffer, semaphore):
        self.buffer, self.shape, self.started = buffer, buffer.shape, False
        self.copy = pltpu.make_async_copy(buffer, target, semaphore)

    def __getitem__(self, at):
        return self.buffer[at]

    def __setitem__(self, at, value):
        self.buffer[at] = value

    def send(self):
        if not self.started:
            self.copy.start()
            self.started = True


def push(ref):
    if isinstance(ref, Pushed):
        ref.send()


def call(body, outs, scratch=(), scalars=0, fetch=0, name=None):
    def run(*operands):
        first = len(operands) - fetch
        far = [len(out) == 3 for out in outs]
        fetched = operands[first:]
        sent = [out for out in outs if len(out) == 3]
        ends = (first, fetch, len(outs), fetch, len(sent), len(scratch), 1, 1)

        def kernel(*refs):
            groups, at = [], 0
            for count in ends:
                groups.append(refs[at : at + count])
                at += count
            here, there, results, in_buffers, out_buffers, rest, (in_sems,), (out_sems,) = groups
            pulled = [Pulled(ref, in_buffers[k], in_sems.at[k]) for k, ref in enumerate(there)]
            made, pushed = [], []
            for ref, is_far in zip(results, far):
                if is_far:
                    k = len(pushed)
                    pushed.append(Pushed(ref, out_buffers[k], out_sems.at[k]))
                    ref = pushed[k]
                made.append(ref)
            body(*here, *pulled, *made, *rest)
            for ref in pushed:
                ref.send()
            for ref in pushed:
                ref.copy.wait()

        spec = pl.BlockSpec(memory_space=pltpu.VMEM)
        small = pl.BlockSpec(memory_space=pltpu.SMEM)
        apart = pl.BlockSpec(memory_space=pltpu.HBM)
        return pl.pallas_call(
            kernel,
            out_shape=[
                pltpu.HBM(out[0], out[1]) if is_far else jax.ShapeDtypeStruct(out[0], out[1])
                for out, is_far in zip(outs, far)
            ],
            in_specs=[small] * scalars + [spec] * (first - scalars) + [apart] * fetch,
            out_specs=[apart if is_far else spec for is_far in far],
            scratch_shapes=[pltpu.VMEM(x.shape, x.dtype) for x in fetched]
            + [pltpu.VMEM(out[0], out[1]) for out in sent]
            + list(scratch)
            + [pltpu.SemaphoreType.DMA((max(1, fetch),)), pltpu.SemaphoreType.DMA((max(1, len(sent)),))],
            compiler_params=pltpu.CompilerParams(vmem_limit_bytes=24 * 1024 * 1024),
            name=name,
        )(*operands[:first], *[pltpu.with_memory_space_constraint(x, pltpu.HBM) for x in fetched])

    return run


def array(*shape, dtype=F32):
    return shape, dtype


def far(*shape, dtype=F32):
    return shape, dtype, True


def exchange(x, groups):
    return lax.all_to_all(x, "tile", split_axis=0, concat_axis=0, tiled=True, axis_index_groups=groups)


def deal(others, z):
    got = []
    for k, (shift, core) in enumerate(z.parts[1:]):
        pairs = [
            (s * z.devices + t, (s + shift) % z.samples * z.devices + (t ^ core))
            for s in range(z.samples)
            for t in range(z.devices)
        ]
        got.append(lax.ppermute(others[k], ("dp", "tile"), pairs))
    return got


def local(inputs, cotangent, w_first, w_second, w_down, edge_owner, corner_owner, neighbour_tile, seam_rotation):
    tiles_in, cot = inputs[0], cotangent[0]
    tiles, side, _, chan = tiles_in.shape
    z = Sizes(tiles, side, chan, lax.axis_size("tile"), lax.axis_size("dp"))
    scale = float(z.samples * z.devices * z.pixels) ** -0.5
    me = lax.axis_index("tile").astype(I32).reshape(1)
    sample = lax.axis_index("dp").astype(I32).reshape(1)
    half = side // 2
    down_pixels = half * half * tiles
    sent = array(z.devices, z.pair, chan, dtype=BF16)
    sent_far = far(z.devices, z.pair, chan, dtype=BF16)
    field, field16 = array(z.pixels, chan), array(z.pixels, chan, dtype=BF16)
    field16_far = far(z.pixels, chan, dtype=BF16)
    columns = array(z.column * side, 3 * chan, dtype=BF16)
    wide_columns = vmem(z.column * side, 3 * chan, dtype=BF16)
    strip = array(z.column * (side + 2), chan, dtype=BF16)
    turned = array(9 * chan, chan, dtype=BF16)
    wide = vmem((side + 2) * z.line, 3 * chan, dtype=BF16)
    side_columns = (vmem(z.column * side, chan), vmem(z.column * side, chan))
    flat = vmem(z.pixels, chan)
    taps = vmem(9 * chan, chan)
    bind = functools.partial
    tables = (edge_owner.T, corner_owner.T, neighbour_tile.T, seam_rotation.T)
    others = len(z.parts) - 1
    everyone = [list(z.order)]
    same_core = [[2 * chip + core for chip in z.ring] for core in range(2)]

    (send,) = call(bind(pack_kernel, z), [sent_far], scalars=1, fetch=5, name="pack")(me, *tables, tiles_in)
    got = exchange(send, everyone)
    cot_rows = cot.transpose(1, 0, 2, 3).reshape(down_pixels, chan)
    index, back_second, turned_first, turned_second = call(
        bind(side_kernel, z),
        [
            array(24, max(z.sent, z.cells_up), dtype=I32),
            field,
            turned,
            turned,
        ],
        scalars=1,
        name="aside",
    )(me, *tables, cot_rows, w_down, w_first, w_second)
    send, hidden, strip_first = call(
        bind(first_kernel, z), [sent, field16, strip], (wide_columns,) + side_columns, name="first"
    )(got, index, tiles_in, w_first)
    got = exchange(send, everyone)
    slope_in, columns_first = call(bind(again_kernel, z), [field, columns], side_columns, name="again")(
        strip_first, w_first
    )
    send, slope_second, hidden_second, strip_second = call(
        bind(second_kernel, z), [sent_far, field16, field16, strip], (wide_columns,) + side_columns + (flat,), name="second"
    )(got, index, hidden, w_second, turned_second, back_second)
    got = exchange(send, everyone)
    (inner,) = call(bind(inner_kernel, z), [field], (wide,), name="inner")(slope_second, turned_second)
    features, early_own, *early_other = call(
        bind(early_kernel, z, scale),
        [array(down_pixels, chan, dtype=BF16), array(z.early, chan)] + [array(z.early, chan, dtype=BF16)] * others,
        (taps, vmem(2 * z.samples * z.early, chan), flat, vmem(down_pixels, 4 * chan, dtype=BF16), wide_columns)
        + side_columns,
        scalars=2,
        name="early",
    )(sample, me, slope_second, hidden_second, cot_rows, w_down, strip_second)
    features = features.reshape(half, tiles, half, chan).transpose(1, 0, 2, 3)
    (early,) = call(gain_kernel, [array(z.early, chan)], name="gain")(early_own, *deal(early_other, z))
    slope_first, late_own, *late_other = call(
        bind(slope_kernel, z, scale),
        [field16, array(z.late, chan)] + [array(z.late, chan, dtype=BF16)] * others,
        (taps,),
        scalars=2,
        name="slope",
    )(sample, me, got, index, inner, slope_in, columns_first)
    late_got = deal(late_other, z)
    (send,) = call(bind(last_kernel, z), [sent], (flat,), name="last")(slope_first, turned_first, index)
    (inner,) = call(bind(inner_kernel, z), [field], (wide,), name="inner")(slope_first, turned_first)
    send, inner, features = lax.optimization_barrier((send, inner, features))
    (send,) = call(
        bind(join_kernel, z),
        [array(z.devices, z.pair + z.chunk, chan, dtype=BF16)],
        (vmem(z.devices * z.chunk, chan),),
        name="join",
    )(send, early, late_own, *late_got)
    got = exchange(send, everyone)
    (chunk,) = call(bind(sum_kernel, z), [array(z.devices // 2, 2 * z.chunk, chan, dtype=BF16)], name="sum")(got)
    mine = exchange(chunk, same_core)
    (input_grad,) = call(bind(input_kernel, z), [array(tiles, side, side, chan)], name="input")(got, index, inner)
    other = lax.ppermute(mine, "tile", [(t, t ^ 1) for t in range(z.devices)])
    grad_first, grad_second, grad_down = call(
        bind(spread_kernel, z),
        [array(z.tap_rows, chan), array(z.tap_rows, chan), array(z.down_rows, chan)],
        scalars=1,
        name="spread",
    )(me, mine, other)
    return features[None], input_grad[None], grad_first, grad_second, grad_down


def solution(mesh):
    split = P("dp", "tile", None, None, None)
    return jax.shard_map(
        local,
        mesh=mesh,
        in_specs=(split, split, P(), P(), P(), P(), P(), P(), P()),
        out_specs=(split, split, P("dp", None), P("dp", None), P("dp", None)),
        check_vma=False,
    )
```

```python
import functools
import jax
import jax.numpy as jnp
from jax import lax
from jax.experimental import pallas as pl
from jax.experimental.pallas import tpu as pltpu
from jax.sharding import PartitionSpec as P

F32, BF16, I32 = jnp.float32, jnp.bfloat16, jnp.int32
LANES = 128
ORDERS = {
    16: (9, 7, 8, 12, 5, 4, 0, 13, 10, 15, 6, 2, 11, 3, 1, 14),
    8: (5, 2, 0, 6, 1, 7, 3, 4),
}


def order_of(count):
    return ORDERS.get(count, tuple(range(count)))


class Sizes:
    def __init__(self, tiles, side, chan, devices, samples):
        self.tiles, self.side, self.chan = tiles, side, chan
        self.devices, self.samples = devices, samples
        self.slots = max(2, 4 * tiles // devices + 1)
        self.pair = -(-self.slots * (side + 1) // 16) * 16
        self.sent = devices * self.pair
        self.line = tiles * side
        self.pixels = side * self.line
        self.column = (side + 2) * tiles
        self.cells = 2 * self.line + 2 * self.column
        self.cells_up = -(-self.cells // (2 * LANES)) * 2 * LANES
        self.cells_read = -(-self.cells // LANES) * LANES
        self.tap_rows = 9 * chan // samples
        self.down_rows = 4 * chan // samples
        self.late = self.tap_rows // 2
        self.early = (self.tap_rows + self.down_rows) // 2
        self.chunk = -(-(self.early + self.late) // (16 * devices)) * 16
        self.parts = [(s, c) for s in range(samples) for c in range(2)]
        self.order = order_of(devices)
        self.place = tuple(self.order.index(device) for device in range(devices))
        self.ring = order_of(devices // 2)
        self.slot_rows = -(-self.slots // 8) * 8


def iota(shape, dim):
    return lax.broadcasted_iota(I32, shape, dim)


def mm(a, b):
    return jnp.dot(a.astype(BF16), b.astype(BF16), preferred_element_type=F32)


def mm_t(a, b):
    return lax.dot_general(a, b, (((0,), (0,)), ((), ())), preferred_element_type=F32)


def flag(cond):
    return jnp.where(cond, 1.0, 0.0).astype(BF16)


def pick_rows(index, width):
    rows = index.shape[0]
    lane = iota((rows, LANES), 1)
    return jnp.concatenate([flag(index == lane + at) for at in range(0, width, LANES)], axis=1)


def gather(index, source):
    half, chan = source.shape[0] // 2, source.shape[1]
    source = source.astype(BF16)
    right = index >= half
    wide = mm(pick_rows(jnp.where(right, index - half, index), half), jnp.concatenate([source[:half], source[half:]], axis=1))
    return jnp.where(right, wide[:, chan:], wide[:, :chan])


def pick_columns(index, height):
    shape = (height, index.shape[1])
    return flag(jnp.broadcast_to(index, shape) == iota(shape, 0))


def row_first(x):
    tiles, side, _, chan = x.shape
    x = x.astype(F32)
    return jnp.stack([x[:, r].reshape(tiles * side, chan) for r in range(side)], axis=0)


def relabel(values, table):
    if table == tuple(range(len(table))):
        return values
    new = jnp.zeros_like(values)
    for old, label in enumerate(table):
        new = jnp.where(values == old, label, new)
    return new


def sender_index(me, owners, local_ids, turns, z):
    requests = z.devices * z.tiles
    row8 = iota((8, requests), 0)
    matched = owners == me
    code = jnp.where(matched, local_ids * 16 + turns * 4 + (row8 & 3) + 1, 0).astype(F32)
    found = jnp.where(matched, 1.0, 0.0)

    def both(values):
        edge = jnp.sum(values[:4], axis=0, keepdims=True)
        corner = jnp.sum(values[4:], axis=0, keepdims=True)
        shape = (z.slot_rows, requests)
        return jnp.concatenate([jnp.broadcast_to(edge, shape), jnp.broadcast_to(corner, shape)], axis=0)

    column = iota((1, 1, requests), 2)
    cube = (z.devices, z.tiles, requests)
    earlier = (iota(cube, 0) == lax.div(column, z.tiles)) & (iota(cube, 1) < lax.rem(column, z.tiles))
    rank = mm(both(found), flag(earlier).reshape(requests, requests))
    slot = iota((2 * z.slot_rows, requests), 0)
    slot = jnp.where(slot < z.slot_rows, slot, slot - z.slot_rows)
    placed = jnp.where(slot.astype(F32) == rank, both(code), 0.0)
    row = iota((1, z.sent), 1)
    device, at = relabel(lax.div(row, z.pair), z.order), lax.rem(row, z.pair)
    cube = (z.devices, z.tiles, z.sent)
    rows = mm(placed, flag(iota(cube, 0) == device.reshape(1, 1, z.sent)).reshape(requests, z.sent))
    edges = z.slots * z.side
    is_edge = at < edges
    wanted = jnp.where(is_edge, lax.div(at, z.side), at - edges + z.slot_rows)
    wanted = jnp.where(at < edges + z.slots, wanted, -1)
    here = iota((2 * z.slot_rows, z.sent), 0) == wanted
    code = jnp.sum(jnp.where(here, rows, 0.0), axis=0, keepdims=True).astype(I32) - 1
    along = lax.rem(at, z.side)
    source, turn, towards = code >> 4, (code >> 2) & 3, code & 3
    end = z.side - 1
    i_edge = jnp.where(towards == 0, end, jnp.where(towards == 2, 0, along))
    j_edge = jnp.where(towards == 1, 0, jnp.where(towards == 3, end, along))
    i_corner = jnp.where((towards == 0) | (towards == 3), end, 0)
    j_corner = jnp.where(towards >= 2, end, 0)
    i = jnp.where(is_edge, i_edge, i_corner)
    j = jnp.where(is_edge, j_edge, j_corner)
    row = jnp.where(turn == 0, i, jnp.where(turn == 1, j, jnp.where(turn == 2, end - i, end - j)))
    col = jnp.where(turn == 0, j, jnp.where(turn == 1, end - i, jnp.where(turn == 2, end - j, i)))
    return jnp.where(code >= 0, row * z.line + source * z.side + col, -1)


def receiver_index(own, z):
    lane = iota((z.tiles, LANES), 1)
    lower = flag(iota((z.tiles, z.tiles), 1) < iota((z.tiles, z.tiles), 0))
    values = jnp.zeros((z.tiles, LANES), F32)
    for base in (0, 4):
        hits = [jnp.broadcast_to(own[:, base + k : base + k + 1], (z.tiles, LANES)) == lane for k in range(4)]
        named = sum(jnp.where(hit, 1.0, 0.0) for hit in hits)
        before = mm(lower, named)
        for k in range(4):
            rank = jnp.sum(jnp.where(hits[k], before, 0.0), axis=1, keepdims=True)
            values = jnp.where(lane == 2 * base + k, own[:, base + k : base + k + 1].astype(F32), values)
            values = jnp.where(lane == 2 * base + 4 + k, rank, values)
    ones = jnp.ones((LANES, LANES), BF16)

    def spread(tile, own_lane, is_edge, along):
        rows = tile.shape[0]
        lane = iota((rows, LANES), 1)
        here = mm(flag(tile[:, : z.tiles] == iota((rows, z.tiles), 1)), values)
        own = mm(jnp.where(lane == own_lane, here, 0.0), ones).astype(I32)
        rank = mm(jnp.where(lane == own_lane + 4, here, 0.0), ones).astype(I32)
        return own * z.pair + jnp.where(is_edge, rank * z.side + along, z.slots * z.side + rank)

    line = (z.tiles, z.side, LANES)
    tile = iota(line, 0).reshape(z.line, LANES)
    along = iota(line, 1).reshape(z.line, LANES)
    parts = [spread(tile, k, jnp.full(tile.shape, True), along) for k in (0, 2)]
    column = (z.side + 2, z.tiles, LANES)
    row = iota(column, 0).reshape(z.column, LANES)
    tile = iota(column, 1).reshape(z.column, LANES)
    is_edge = (row > 0) & (row <= z.side)
    for edge, top, bottom in ((3, 3, 2), (1, 0, 1)):
        own_lane = jnp.where(is_edge, edge, jnp.where(row == 0, 8 + top, 8 + bottom))
        parts.append(spread(tile, own_lane, is_edge, row - 1))
    parts.append(jnp.full((z.cells_up - z.cells, LANES), -1, I32))
    return jnp.concatenate(parts, axis=0)


def as_column(index):
    return jnp.transpose(jnp.broadcast_to(index.astype(F32), (LANES, index.shape[1]))).astype(I32)


def pack_kernel(z, me_ref, eo_ref, co_ref, ids_ref, turn_ref, x_ref, send_ref):
    owners = jnp.concatenate([eo_ref[...], co_ref[...]], axis=0)
    index = sender_index(me_ref[0], owners, ids_ref[...], turn_ref[...], z)
    pixels = row_first(x_ref[...]).reshape(z.pixels, z.chan)
    send_ref[...] = gather(as_column(index), pixels).astype(BF16).reshape(send_ref.shape)


def side_kernel(
    z, me_ref, eo_ref, co_ref, ids_ref, turn_ref, cot_ref, wd_ref, w1_ref, w2_ref,
    table_ref, back_ref, t1_ref, t2_ref,
):
    me = me_ref[0]
    owners = jnp.concatenate([eo_ref[...], co_ref[...]], axis=0)
    index = sender_index(me, owners, ids_ref[...], turn_ref[...], z)
    table_ref[0:8, : z.sent] = jnp.broadcast_to(index, (8, z.sent))
    shape = (z.tiles, z.devices * z.tiles)
    mine = flag(iota(shape, 1) == iota(shape, 0) + me * z.tiles)
    own = lax.dot_general(
        mine, owners.astype(F32).astype(BF16), (((1,), (1,)), ((), ())), preferred_element_type=F32
    )
    index = receiver_index(relabel(own.astype(I32), z.place), z)
    table_ref[8:16, : z.cells_up] = jnp.transpose(index.astype(F32))[0:8].astype(I32)
    cell = iota((16, z.cells_up), 1) + 1
    digits = jnp.where(iota((16, z.cells_up), 0) < 8, cell >> 4, cell & 15).astype(F32)
    found = mm(digits, pick_rows(index, z.sent))
    table_ref[16:24, : z.sent] = jnp.broadcast_to(found[0:1] * 16.0 + found[8:9] - 1.0, (8, z.sent)).astype(I32)
    chan, half = z.chan, z.side // 2
    for taps, out in ((w1_ref, t1_ref), (w2_ref, t2_ref)):
        for tap in range(9):
            rows = slice(tap * chan, (tap + 1) * chan)
            out[rows, :] = jnp.transpose(taps[rows, :].astype(F32)).astype(BF16)
    cot = cot_ref[...]
    part = half * z.tiles
    for p in range(2):
        for q in range(2):
            tap = wd_ref[(2 * p + q) * chan : (2 * p + q + 1) * chan, :]
            back = lax.dot_general(cot, tap, (((1,), (1,)), ((), ())), preferred_element_type=F32)
            for i in range(half):
                back_ref[pl.ds((2 * i + p) * z.line + q, part, stride=2), :] = back[i * part : (i + 1) * part]


def padded_columns(z, center, arrived, index, west_ref, east_ref, out_ref):
    rims = gather(index, arrived)
    at = 2 * z.line
    strip = jnp.concatenate([rims[: z.line], center, rims[z.line : at], rims[at : at + 2 * z.column]], axis=0)
    fill_columns(z, strip, west_ref, east_ref, out_ref)
    return strip


def fill_columns(z, strip, west_ref, east_ref, out_ref):
    rows = z.column * z.side
    west_ref[pl.ds(0, z.column, stride=z.side), :] = strip[rows : rows + z.column]
    east_ref[pl.ds(z.side - 1, z.column, stride=z.side), :] = strip[rows + z.column :]
    shape = (z.column, z.side, z.chan)
    middle = strip[:rows].reshape(shape)
    place = iota(shape, 1)
    flat = (rows, z.chan)
    left = jnp.where(place == 0, west_ref[...].reshape(shape), pltpu.roll(middle, 1, 1))
    right = jnp.where(place == z.side - 1, east_ref[...].reshape(shape), pltpu.roll(middle, z.side - 1, 1))
    out_ref[:, : z.chan] = left.reshape(flat).astype(BF16)
    out_ref[:, z.chan : 2 * z.chan] = middle.reshape(flat).astype(BF16)
    out_ref[:, 2 * z.chan :] = right.reshape(flat).astype(BF16)


def conv(z, columns_ref, w_ref):
    total = None
    for p in range(3):
        part = jnp.dot(
            columns_ref[p * z.line : p * z.line + z.pixels, :],
            w_ref[3 * p * z.chan : 3 * (p + 1) * z.chan, :],
            preferred_element_type=F32,
        )
        total = part if total is None else total + part
    return total


def silu_slope(v):
    s = 1.0 / (1.0 + jnp.exp(-v))
    return s * (1.0 + v * (1.0 - s))


def first_kernel(z, got_ref, index_ref, x_ref, w_ref, send_ref, hidden_ref, strip_ref, columns_ref, west_ref, east_ref):
    center = row_first(x_ref[...]).reshape(z.pixels, z.chan)
    strip = padded_columns(z, center, got_ref[...].reshape(z.sent, z.chan), as_column(index_ref[8:9, : z.cells_read]), west_ref, east_ref, columns_ref)
    strip_ref[...] = strip.astype(BF16)
    v = conv(z, columns_ref, w_ref)
    hidden = (v / (1.0 + jnp.exp(-v))).astype(BF16)
    send_ref[...] = gather(as_column(index_ref[0:1, : z.sent]), hidden).astype(BF16).reshape(send_ref.shape)
    hidden_ref[...] = hidden


def again_kernel(z, strip_ref, w_ref, slope_ref, columns_ref, west_ref, east_ref):
    fill_columns(z, strip_ref[...].astype(F32), west_ref, east_ref, columns_ref)
    slope_ref[...] = silu_slope(conv(z, columns_ref, w_ref))


def shifted(z, slope):
    cube = slope.reshape(slope.shape[0] // z.side, z.side, z.chan)
    place = iota(cube.shape, 1)
    after = jnp.where(place == z.side - 1, 0.0, pltpu.roll(cube, z.side - 1, 1))
    before = jnp.where(place == 0, 0.0, pltpu.roll(cube, 1, 1))
    return [part.reshape(slope.shape).astype(BF16) for part in (after, cube, before)]


def rims_back(z, slope, turned_ref, slope_ref):
    chan = z.chan
    parts = []
    for p, row in ((0, 0), (2, z.side - 1)):
        wide = jnp.concatenate(shifted(z, slope[row * z.line : (row + 1) * z.line]), axis=1)
        parts.append(jnp.dot(wide, turned_ref[3 * p * chan : 3 * (p + 1) * chan, :], preferred_element_type=F32))
    slope_ref[...] = slope
    blank = jnp.zeros((2 * z.tiles, chan), F32)
    for start, q in ((0, 0), (z.side - 1, 2)):
        line = slope_ref[pl.ds(start, z.side * z.tiles, stride=z.side), :]
        line = jnp.concatenate([blank, line, blank], axis=0).astype(BF16)
        side = None
        for p in range(3):
            part = jnp.dot(
                line[(2 - p) * z.tiles : (2 - p) * z.tiles + z.column],
                turned_ref[(3 * p + q) * chan : (3 * p + q + 1) * chan, :],
                preferred_element_type=F32,
            )
            side = part if side is None else side + part
        parts.append(side)
    parts.append(jnp.zeros((z.cells_up - z.cells, chan), F32))
    return jnp.concatenate(parts, axis=0).astype(BF16)


def inner_back(z, slope, turned_ref, wide_ref):
    chan = z.chan
    zero = jnp.zeros((z.line, 3 * chan), BF16)
    wide_ref[: z.line, :] = zero
    wide_ref[z.line + z.pixels :, :] = zero
    for q, part in enumerate(shifted(z, slope)):
        wide_ref[z.line : z.line + z.pixels, q * chan : (q + 1) * chan] = part
    total = None
    for p in range(3):
        part = jnp.dot(
            wide_ref[(2 - p) * z.line : (2 - p) * z.line + z.pixels, :],
            turned_ref[3 * p * chan : 3 * (p + 1) * chan, :],
            preferred_element_type=F32,
        )
        total = part if total is None else total + part
    return total


def second_kernel(
    z, got_ref, index_ref, hidden_ref, w_ref, turned_ref, back_ref,
    send_ref, slope_ref, out_ref, strip_ref, columns_ref, west_ref, east_ref, scratch_ref,
):
    center = hidden_ref[...].astype(F32)
    strip = padded_columns(z, center, got_ref[...].reshape(z.sent, z.chan), as_column(index_ref[8:9, : z.cells_read]), west_ref, east_ref, columns_ref)
    strip_ref[...] = strip.astype(BF16)
    v = conv(z, columns_ref, w_ref)
    s = 1.0 / (1.0 + jnp.exp(-v))
    out_ref[...] = (v * s).astype(BF16)
    push(out_ref)
    slope = (back_ref[...] * (s * (1.0 + v * (1.0 - s)))).astype(BF16)
    slope_ref[...] = slope
    push(slope_ref)
    rims = rims_back(z, slope.astype(F32), turned_ref, scratch_ref)
    send_ref[...] = gather(as_column(index_ref[16:17, : z.sent]), rims).astype(BF16).reshape(send_ref.shape)


def tap_products(z, columns_ref, slope, scale, total_ref):
    blank = jnp.zeros((2 * z.line, z.chan), BF16)
    padded = jnp.concatenate([blank, slope, blank], axis=0)
    rows = (z.side + 2) * z.line
    wide = jnp.concatenate([padded[(2 - p) * z.line : (2 - p) * z.line + rows] for p in range(3)], axis=1)
    total = mm_t(columns_ref[...], wide) * scale
    for p in range(3):
        total_ref[3 * p * z.chan : 3 * (p + 1) * z.chan, :] = total[:, p * z.chan : (p + 1) * z.chan]


def deal_parts(z, sample_ref, me_ref, source_ref, own_ref, other_refs):
    rows = own_ref.shape[0]
    for k, (shift, core) in enumerate(z.parts):
        whose = lax.rem(sample_ref[0] + shift, z.samples)
        half = jnp.bitwise_xor(me_ref[0] & 1, core)
        part = source_ref[pl.ds((2 * whose + half) * rows, rows), :]
        if k == 0:
            own_ref[...] = part
        else:
            other_refs[k - 1][...] = part.astype(BF16)


def early_kernel(
    z, scale, sample_ref, me_ref, slope_ref, hidden_ref, cot_ref, wd_ref, strip_ref, feature_ref, own_ref, *refs
):
    other_refs, (taps_ref, total_ref, flat_ref, block_ref, columns_ref, west_ref, east_ref) = refs[:-7], refs[-7:]
    chan, half = z.chan, z.side // 2
    part = half * z.tiles
    flat_ref[...] = hidden_ref[...].astype(F32)
    for i in range(half):
        for p in range(2):
            for q in range(2):
                block_ref[i * part : (i + 1) * part, (2 * p + q) * chan : (2 * p + q + 1) * chan] = flat_ref[
                    pl.ds((2 * i + p) * z.line + q, part, stride=2), :
                ].astype(BF16)
    block = block_ref[...]
    feature_ref[...] = jnp.dot(block, wd_ref[...], preferred_element_type=F32).astype(BF16)
    down = mm_t(block, cot_ref[...]) * scale
    fill_columns(z, strip_ref[...].astype(F32), west_ref, east_ref, columns_ref)
    tap_products(z, columns_ref, slope_ref[...], scale, taps_ref)
    both = z.tap_rows + z.down_rows
    for s in range(z.samples):
        total_ref[s * both : s * both + z.tap_rows, :] = taps_ref[s * z.tap_rows : (s + 1) * z.tap_rows, :]
        total_ref[s * both + z.tap_rows : (s + 1) * both, :] = down[s * z.down_rows : (s + 1) * z.down_rows]
    deal_parts(z, sample_ref, me_ref, total_ref, own_ref, other_refs)


def inner_kernel(z, slope_ref, turned_ref, inner_ref, wide_ref):
    inner_ref[...] = inner_back(z, slope_ref[...].astype(F32), turned_ref, wide_ref)


def slope_kernel(
    z, scale, sample_ref, me_ref, got_ref, pix_row_ref, inner_ref, slope_in_ref, columns_ref,
    slope_ref, own_ref, *refs,
):
    other_refs, total_ref = refs[:-1], refs[-1]
    back = inner_ref[...] + mm(pick_columns(pix_row_ref[0:1, : z.sent], z.pixels), got_ref[...].reshape(z.sent, z.chan))
    slope = (back * slope_in_ref[...]).astype(BF16)
    slope_ref[...] = slope
    tap_products(z, columns_ref, slope, scale, total_ref)
    deal_parts(z, sample_ref, me_ref, total_ref, own_ref, other_refs)


def last_kernel(z, slope_ref, turned_ref, index_ref, send_ref, scratch_ref):
    rims = rims_back(z, slope_ref[...].astype(F32), turned_ref, scratch_ref)
    send_ref[...] = gather(as_column(index_ref[16:17, : z.sent]), rims).astype(BF16).reshape(send_ref.shape)


def gain_kernel(own_ref, *refs):
    others, out_ref = refs[:-1], refs[-1]
    total = own_ref[...]
    for other in others:
        total = total + other[...].astype(F32)
    out_ref[...] = total


def join_kernel(z, rim_ref, early_ref, late_ref, *refs):
    others, (send_ref, total_ref) = refs[:-2], refs[-2:]
    late = late_ref[...]
    for other in others:
        late = late + other[...].astype(F32)
    total_ref[: z.early, :] = early_ref[...]
    total_ref[z.early : z.early + z.late, :] = late
    spare = z.devices * z.chunk - z.early - z.late
    if spare:
        total_ref[z.early + z.late :, :] = jnp.zeros((spare, z.chan), F32)
    send_ref[:, : z.pair, :] = rim_ref[...]
    send_ref[:, z.pair :, :] = total_ref[...].astype(BF16).reshape(z.devices, z.chunk, z.chan)


def sum_kernel(z, got_ref, out_ref):
    sums = []
    for core in range(2):
        first, *rest = [z.place[device] for device in range(core, z.devices, 2)]
        total = got_ref[first, z.pair :, :].astype(F32)
        for k in rest:
            total = total + got_ref[k, z.pair :, :].astype(F32)
        sums.append(total.astype(BF16))
    for k in range(z.devices // 2):
        for core in range(2):
            out_ref[k, core * z.chunk : (core + 1) * z.chunk, :] = sums[core]


def input_kernel(z, got_ref, pix_row_ref, inner_ref, out_ref):
    arrived = got_ref[:, : z.pair, :].reshape(z.sent, z.chan)
    total = inner_ref[...] + mm(pick_columns(pix_row_ref[0:1, : z.sent], z.pixels), arrived)
    for r in range(z.side):
        out_ref[:, r] = total[r * z.line : (r + 1) * z.line].reshape(z.tiles, z.side, z.chan)


def spread_kernel(z, me_ref, mine_ref, other_ref, one_ref, two_ref, low_ref):
    first = (me_ref[0] & 1) == 0
    mine, other = mine_ref[...].astype(F32), other_ref[...].astype(F32)
    halves = []
    for core in range(2):
        rows = slice(core * z.chunk, (core + 1) * z.chunk)
        a, b = mine[:, rows], other[:, rows]
        by_core = jnp.where(first, a, b), jnp.where(first, b, a)
        chunks = [by_core[device % 2][z.ring.index(device // 2)] for device in z.order]
        halves.append(jnp.concatenate(chunks, axis=0))
    one_ref[...] = jnp.concatenate([half[z.early : z.early + z.late] for half in halves], axis=0)
    early = jnp.concatenate([half[: z.early] for half in halves], axis=0)
    two_ref[...] = early[: z.tap_rows]
    low_ref[...] = early[z.tap_rows :]


def vmem(*shape, dtype=F32):
    return pltpu.VMEM(shape, dtype)


class Pulled:
    def __init__(self, source, buffer, semaphore):
        self.buffer, self.shape, self.waits = buffer, buffer.shape, True
        self.copy = pltpu.make_async_copy(source, buffer, semaphore)
        self.copy.start()

    def __getitem__(self, at):
        if self.waits:
            self.copy.wait()
            self.waits = False
        return self.buffer[at]


class Pushed:
    def __init__(self, target, buffer, semaphore):
        self.buffer, self.shape, self.started = buffer, buffer.shape, False
        self.copy = pltpu.make_async_copy(buffer, target, semaphore)

    def __getitem__(self, at):
        return self.buffer[at]

    def __setitem__(self, at, value):
        self.buffer[at] = value

    def send(self):
        if not self.started:
            self.copy.start()
            self.started = True


def push(ref):
    if isinstance(ref, Pushed):
        ref.send()


def call(body, outs, scratch=(), scalars=0, fetch=0, name=None):
    def run(*operands):
        first = len(operands) - fetch
        far = [len(out) == 3 for out in outs]
        fetched = operands[first:]
        sent = [out for out in outs if len(out) == 3]
        ends = (first, fetch, len(outs), fetch, len(sent), len(scratch), 1, 1)

        def kernel(*refs):
            groups, at = [], 0
            for count in ends:
                groups.append(refs[at : at + count])
                at += count
            here, there, results, in_buffers, out_buffers, rest, (in_sems,), (out_sems,) = groups
            pulled = [Pulled(ref, in_buffers[k], in_sems.at[k]) for k, ref in enumerate(there)]
            made, pushed = [], []
            for ref, is_far in zip(results, far):
                if is_far:
                    k = len(pushed)
                    pushed.append(Pushed(ref, out_buffers[k], out_sems.at[k]))
                    ref = pushed[k]
                made.append(ref)
            body(*here, *pulled, *made, *rest)
            for ref in pushed:
                ref.send()
            for ref in pushed:
                ref.copy.wait()

        spec = pl.BlockSpec(memory_space=pltpu.VMEM)
        small = pl.BlockSpec(memory_space=pltpu.SMEM)
        apart = pl.BlockSpec(memory_space=pltpu.HBM)
        return pl.pallas_call(
            kernel,
            out_shape=[
                pltpu.HBM(out[0], out[1]) if is_far else jax.ShapeDtypeStruct(out[0], out[1])
                for out, is_far in zip(outs, far)
            ],
            in_specs=[small] * scalars + [spec] * (first - scalars) + [apart] * fetch,
            out_specs=[apart if is_far else spec for is_far in far],
            scratch_shapes=[pltpu.VMEM(x.shape, x.dtype) for x in fetched]
            + [pltpu.VMEM(out[0], out[1]) for out in sent]
            + list(scratch)
            + [pltpu.SemaphoreType.DMA((max(1, fetch),)), pltpu.SemaphoreType.DMA((max(1, len(sent)),))],
            compiler_params=pltpu.CompilerParams(vmem_limit_bytes=24 * 1024 * 1024),
            name=name,
        )(*operands[:first], *[pltpu.with_memory_space_constraint(x, pltpu.HBM) for x in fetched])

    return run


def array(*shape, dtype=F32):
    return shape, dtype


def far(*shape, dtype=F32):
    return shape, dtype, True


def exchange(x, groups):
    return lax.all_to_all(x, "tile", split_axis=0, concat_axis=0, tiled=True, axis_index_groups=groups)


def deal(others, z):
    got = []
    for k, (shift, core) in enumerate(z.parts[1:]):
        pairs = [
            (s * z.devices + t, (s + shift) % z.samples * z.devices + (t ^ core))
            for s in range(z.samples)
            for t in range(z.devices)
        ]
        got.append(lax.ppermute(others[k], ("dp", "tile"), pairs))
    return got


def local(inputs, cotangent, w_first, w_second, w_down, edge_owner, corner_owner, neighbour_tile, seam_rotation):
    tiles_in, cot = inputs[0], cotangent[0]
    tiles, side, _, chan = tiles_in.shape
    z = Sizes(tiles, side, chan, lax.axis_size("tile"), lax.axis_size("dp"))
    scale = float(z.samples * z.devices * z.pixels) ** -0.5
    me = lax.axis_index("tile").astype(I32).reshape(1)
    sample = lax.axis_index("dp").astype(I32).reshape(1)
    half = side // 2
    down_pixels = half * half * tiles
    sent = array(z.devices, z.pair, chan, dtype=BF16)
    sent_far = far(z.devices, z.pair, chan, dtype=BF16)
    field, field16 = array(z.pixels, chan), array(z.pixels, chan, dtype=BF16)
    field16_far = far(z.pixels, chan, dtype=BF16)
    columns = array(z.column * side, 3 * chan, dtype=BF16)
    wide_columns = vmem(z.column * side, 3 * chan, dtype=BF16)
    strip = array(z.column * (side + 2), chan, dtype=BF16)
    turned = array(9 * chan, chan, dtype=BF16)
    wide = vmem((side + 2) * z.line, 3 * chan, dtype=BF16)
    side_columns = (vmem(z.column * side, chan), vmem(z.column * side, chan))
    flat = vmem(z.pixels, chan)
    taps = vmem(9 * chan, chan)
    bind = functools.partial
    tables = (edge_owner.T, corner_owner.T, neighbour_tile.T, seam_rotation.T)
    others = len(z.parts) - 1
    everyone = [list(z.order)]
    same_core = [[2 * chip + core for chip in z.ring] for core in range(2)]

    (send,) = call(bind(pack_kernel, z), [sent_far], scalars=1, fetch=5, name="pack")(me, *tables, tiles_in)
    got = exchange(send, everyone)
    cot_rows = cot.transpose(1, 0, 2, 3).reshape(down_pixels, chan)
    index, back_second, turned_first, turned_second = call(
        bind(side_kernel, z),
        [
            array(24, max(z.sent, z.cells_up), dtype=I32),
            field,
            turned,
            turned,
        ],
        scalars=1,
        name="aside",
    )(me, *tables, cot_rows, w_down, w_first, w_second)
    send, hidden, strip_first = call(
        bind(first_kernel, z), [sent, field16, strip], (wide_columns,) + side_columns, name="first"
    )(got, index, tiles_in, w_first)
    got = exchange(send, everyone)
    slope_in, columns_first = call(bind(again_kernel, z), [field, columns], side_columns, name="again")(
        strip_first, w_first
    )
    send, slope_second, hidden_second, strip_second = call(
        bind(second_kernel, z), [sent_far, field16, field16, strip], (wide_columns,) + side_columns + (flat,), name="second"
    )(got, index, hidden, w_second, turned_second, back_second)
    got = exchange(send, everyone)
    (inner,) = call(bind(inner_kernel, z), [field], (wide,), name="inner")(slope_second, turned_second)
    features, early_own, *early_other = call(
        bind(early_kernel, z, scale),
        [array(down_pixels, chan, dtype=BF16), array(z.early, chan)] + [array(z.early, chan, dtype=BF16)] * others,
        (taps, vmem(2 * z.samples * z.early, chan), flat, vmem(down_pixels, 4 * chan, dtype=BF16), wide_columns)
        + side_columns,
        scalars=2,
        name="early",
    )(sample, me, slope_second, hidden_second, cot_rows, w_down, strip_second)
    features = features.reshape(half, tiles, half, chan).transpose(1, 0, 2, 3)
    (early,) = call(gain_kernel, [array(z.early, chan)], name="gain")(early_own, *deal(early_other, z))
    slope_first, late_own, *late_other = call(
        bind(slope_kernel, z, scale),
        [field16, array(z.late, chan)] + [array(z.late, chan, dtype=BF16)] * others,
        (taps,),
        scalars=2,
        name="slope",
    )(sample, me, got, index, inner, slope_in, columns_first)
    late_got = deal(late_other, z)
    (send,) = call(bind(last_kernel, z), [sent], (flat,), name="last")(slope_first, turned_first, index)
    (inner,) = call(bind(inner_kernel, z), [field], (wide,), name="inner")(slope_first, turned_first)
    send, inner, features = lax.optimization_barrier((send, inner, features))
    (send,) = call(
        bind(join_kernel, z),
        [array(z.devices, z.pair + z.chunk, chan, dtype=BF16)],
        (vmem(z.devices * z.chunk, chan),),
        name="join",
    )(send, early, late_own, *late_got)
    got = exchange(send, everyone)
    (chunk,) = call(bind(sum_kernel, z), [array(z.devices // 2, 2 * z.chunk, chan, dtype=BF16)], name="sum")(got)
    mine = exchange(chunk, same_core)
    (input_grad,) = call(bind(input_kernel, z), [array(tiles, side, side, chan)], name="input")(got, index, inner)
    other = lax.ppermute(mine, "tile", [(t, t ^ 1) for t in range(z.devices)])
    grad_first, grad_second, grad_down = call(
        bind(spread_kernel, z),
        [array(z.tap_rows, chan), array(z.tap_rows, chan), array(z.down_rows, chan)],
        scalars=1,
        name="spread",
    )(me, mine, other)
    return features[None], input_grad[None], grad_first, grad_second, grad_down


def solution(mesh):
    split = P("dp", "tile", None, None, None)
    return jax.shard_map(
        local,
        mesh=mesh,
        in_specs=(split, split, P(), P(), P(), P(), P(), P(), P()),
        out_specs=(split, split, P("dp", None), P("dp", None), P("dp", None)),
        check_vma=False,
    )
```

```python
import functools
import jax
import jax.numpy as jnp
from jax import lax
from jax.experimental import pallas as pl
from jax.experimental.pallas import tpu as pltpu
from jax.sharding import PartitionSpec as P

F32, BF16, I32 = jnp.float32, jnp.bfloat16, jnp.int32
LANES = 128
ORDERS = {
    16: (9, 7, 8, 12, 5, 4, 0, 13, 10, 15, 6, 2, 11, 3, 1, 14),
    8: (5, 2, 0, 6, 1, 7, 3, 4),
}


def order_of(count):
    return ORDERS.get(count, tuple(range(count)))


class Sizes:
    def __init__(self, tiles, side, chan, devices, samples):
        self.tiles, self.side, self.chan = tiles, side, chan
        self.devices, self.samples = devices, samples
        self.slots = max(2, 4 * tiles // devices + 1)
        self.pair = -(-self.slots * (side + 1) // 16) * 16
        self.sent = devices * self.pair
        self.line = tiles * side
        self.pixels = side * self.line
        self.column = (side + 2) * tiles
        self.cells = 2 * self.line + 2 * self.column
        self.cells_up = -(-self.cells // (2 * LANES)) * 2 * LANES
        self.cells_read = -(-self.cells // LANES) * LANES
        self.tap_rows = 9 * chan // samples
        self.down_rows = 4 * chan // samples
        self.late = self.tap_rows // 2
        self.early = (self.tap_rows + self.down_rows) // 2
        self.chunk = -(-(self.early + self.late) // (16 * devices)) * 16
        self.parts = [(s, c) for s in range(samples) for c in range(2)]
        self.order = order_of(devices)
        self.place = tuple(self.order.index(device) for device in range(devices))
        self.ring = order_of(devices // 2)
        self.slot_rows = -(-self.slots // 8) * 8


def iota(shape, dim):
    return lax.broadcasted_iota(I32, shape, dim)


def mm(a, b):
    return jnp.dot(a.astype(BF16), b.astype(BF16), preferred_element_type=F32)


def mm_t(a, b):
    return lax.dot_general(a, b, (((0,), (0,)), ((), ())), preferred_element_type=F32)


def flag(cond):
    return jnp.where(cond, 1.0, 0.0).astype(BF16)


def pick_rows(index, width):
    rows = index.shape[0]
    lane = iota((rows, LANES), 1)
    return jnp.concatenate([flag(index == lane + at) for at in range(0, width, LANES)], axis=1)


def gather(index, source):
    half, chan = source.shape[0] // 2, source.shape[1]
    source = source.astype(BF16)
    right = index >= half
    wide = mm(pick_rows(jnp.where(right, index - half, index), half), jnp.concatenate([source[:half], source[half:]], axis=1))
    return jnp.where(right, wide[:, chan:], wide[:, :chan])


def pick_columns(index, height):
    shape = (height, index.shape[1])
    return flag(jnp.broadcast_to(index, shape) == iota(shape, 0))


def row_first(x):
    tiles, side, _, chan = x.shape
    x = x.astype(F32)
    return jnp.stack([x[:, r].reshape(tiles * side, chan) for r in range(side)], axis=0)


def relabel(values, table):
    if table == tuple(range(len(table))):
        return values
    new = jnp.zeros_like(values)
    for old, label in enumerate(table):
        new = jnp.where(values == old, label, new)
    return new


def sender_index(me, owners, local_ids, turns, z):
    requests = z.devices * z.tiles
    row8 = iota((8, requests), 0)
    matched = owners == me
    code = jnp.where(matched, local_ids * 16 + turns * 4 + (row8 & 3) + 1, 0).astype(F32)
    found = jnp.where(matched, 1.0, 0.0)

    def both(values):
        edge = jnp.sum(values[:4], axis=0, keepdims=True)
        corner = jnp.sum(values[4:], axis=0, keepdims=True)
        shape = (z.slot_rows, requests)
        return jnp.concatenate([jnp.broadcast_to(edge, shape), jnp.broadcast_to(corner, shape)], axis=0)

    column = iota((1, 1, requests), 2)
    cube = (z.devices, z.tiles, requests)
    earlier = (iota(cube, 0) == lax.div(column, z.tiles)) & (iota(cube, 1) < lax.rem(column, z.tiles))
    rank = mm(both(found), flag(earlier).reshape(requests, requests))
    slot = iota((2 * z.slot_rows, requests), 0)
    slot = jnp.where(slot < z.slot_rows, slot, slot - z.slot_rows)
    placed = jnp.where(slot.astype(F32) == rank, both(code), 0.0)
    row = iota((1, z.sent), 1)
    device, at = relabel(lax.div(row, z.pair), z.order), lax.rem(row, z.pair)
    cube = (z.devices, z.tiles, z.sent)
    rows = mm(placed, flag(iota(cube, 0) == device.reshape(1, 1, z.sent)).reshape(requests, z.sent))
    edges = z.slots * z.side
    is_edge = at < edges
    wanted = jnp.where(is_edge, lax.div(at, z.side), at - edges + z.slot_rows)
    wanted = jnp.where(at < edges + z.slots, wanted, -1)
    here = iota((2 * z.slot_rows, z.sent), 0) == wanted
    code = jnp.sum(jnp.where(here, rows, 0.0), axis=0, keepdims=True).astype(I32) - 1
    along = lax.rem(at, z.side)
    source, turn, towards = code >> 4, (code >> 2) & 3, code & 3
    end = z.side - 1
    i_edge = jnp.where(towards == 0, end, jnp.where(towards == 2, 0, along))
    j_edge = jnp.where(towards == 1, 0, jnp.where(towards == 3, end, along))
    i_corner = jnp.where((towards == 0) | (towards == 3), end, 0)
    j_corner = jnp.where(towards >= 2, end, 0)
    i = jnp.where(is_edge, i_edge, i_corner)
    j = jnp.where(is_edge, j_edge, j_corner)
    row = jnp.where(turn == 0, i, jnp.where(turn == 1, j, jnp.where(turn == 2, end - i, end - j)))
    col = jnp.where(turn == 0, j, jnp.where(turn == 1, end - i, jnp.where(turn == 2, end - j, i)))
    return jnp.where(code >= 0, row * z.line + source * z.side + col, -1)


def receiver_index(own, z):
    lane = iota((z.tiles, LANES), 1)
    lower = flag(iota((z.tiles, z.tiles), 1) < iota((z.tiles, z.tiles), 0))
    values = jnp.zeros((z.tiles, LANES), F32)
    for base in (0, 4):
        hits = [jnp.broadcast_to(own[:, base + k : base + k + 1], (z.tiles, LANES)) == lane for k in range(4)]
        named = sum(jnp.where(hit, 1.0, 0.0) for hit in hits)
        before = mm(lower, named)
        for k in range(4):
            rank = jnp.sum(jnp.where(hits[k], before, 0.0), axis=1, keepdims=True)
            values = jnp.where(lane == 2 * base + k, own[:, base + k : base + k + 1].astype(F32), values)
            values = jnp.where(lane == 2 * base + 4 + k, rank, values)
    ones = jnp.ones((LANES, LANES), BF16)

    def spread(tile, own_lane, is_edge, along):
        rows = tile.shape[0]
        lane = iota((rows, LANES), 1)
        here = mm(flag(tile[:, : z.tiles] == iota((rows, z.tiles), 1)), values)
        own = mm(jnp.where(lane == own_lane, here, 0.0), ones).astype(I32)
        rank = mm(jnp.where(lane == own_lane + 4, here, 0.0), ones).astype(I32)
        return own * z.pair + jnp.where(is_edge, rank * z.side + along, z.slots * z.side + rank)

    line = (z.tiles, z.side, LANES)
    tile = iota(line, 0).reshape(z.line, LANES)
    along = iota(line, 1).reshape(z.line, LANES)
    parts = [spread(tile, k, jnp.full(tile.shape, True), along) for k in (0, 2)]
    column = (z.side + 2, z.tiles, LANES)
    row = iota(column, 0).reshape(z.column, LANES)
    tile = iota(column, 1).reshape(z.column, LANES)
    is_edge = (row > 0) & (row <= z.side)
    for edge, top, bottom in ((3, 3, 2), (1, 0, 1)):
        own_lane = jnp.where(is_edge, edge, jnp.where(row == 0, 8 + top, 8 + bottom))
        parts.append(spread(tile, own_lane, is_edge, row - 1))
    parts.append(jnp.full((z.cells_up - z.cells, LANES), -1, I32))
    return jnp.concatenate(parts, axis=0)


def as_column(index):
    return jnp.transpose(jnp.broadcast_to(index.astype(F32), (LANES, index.shape[1]))).astype(I32)


def pack_kernel(z, me_ref, eo_ref, co_ref, ids_ref, turn_ref, x_ref, send_ref):
    owners = jnp.concatenate([eo_ref[...], co_ref[...]], axis=0)
    index = sender_index(me_ref[0], owners, ids_ref[...], turn_ref[...], z)
    pixels = row_first(x_ref[...]).reshape(z.pixels, z.chan)
    send_ref[...] = gather(as_column(index), pixels).astype(BF16).reshape(send_ref.shape)


def side_kernel(
    z, me_ref, eo_ref, co_ref, ids_ref, turn_ref, cot_ref, wd_ref, w1_ref, w2_ref,
    table_ref, back_ref, t1_ref, t2_ref,
):
    me = me_ref[0]
    owners = jnp.concatenate([eo_ref[...], co_ref[...]], axis=0)
    index = sender_index(me, owners, ids_ref[...], turn_ref[...], z)
    table_ref[0:8, : z.sent] = jnp.broadcast_to(index, (8, z.sent))
    shape = (z.tiles, z.devices * z.tiles)
    mine = flag(iota(shape, 1) == iota(shape, 0) + me * z.tiles)
    own = lax.dot_general(
        mine, owners.astype(F32).astype(BF16), (((1,), (1,)), ((), ())), preferred_element_type=F32
    )
    index = receiver_index(relabel(own.astype(I32), z.place), z)
    table_ref[8:16, : z.cells_up] = jnp.transpose(index.astype(F32))[0:8].astype(I32)
    cell = iota((16, z.cells_up), 1) + 1
    digits = jnp.where(iota((16, z.cells_up), 0) < 8, cell >> 4, cell & 15).astype(F32)
    found = mm(digits, pick_rows(index, z.sent))
    table_ref[16:24, : z.sent] = jnp.broadcast_to(found[0:1] * 16.0 + found[8:9] - 1.0, (8, z.sent)).astype(I32)
    chan, half = z.chan, z.side // 2
    for taps, out in ((w1_ref, t1_ref), (w2_ref, t2_ref)):
        for tap in range(9):
            rows = slice(tap * chan, (tap + 1) * chan)
            out[rows, :] = jnp.transpose(taps[rows, :].astype(F32)).astype(BF16)
    cot = cot_ref[...]
    part = half * z.tiles
    for p in range(2):
        for q in range(2):
            tap = wd_ref[(2 * p + q) * chan : (2 * p + q + 1) * chan, :]
            back = lax.dot_general(cot, tap, (((1,), (1,)), ((), ())), preferred_element_type=F32)
            for i in range(half):
                back_ref[pl.ds((2 * i + p) * z.line + q, part, stride=2), :] = back[i * part : (i + 1) * part]


def padded_columns(z, center, arrived, index, west_ref, east_ref, out_ref):
    rims = gather(index, arrived)
    at = 2 * z.line
    strip = jnp.concatenate([rims[: z.line], center, rims[z.line : at], rims[at : at + 2 * z.column]], axis=0)
    fill_columns(z, strip, west_ref, east_ref, out_ref)
    return strip


def fill_columns(z, strip, west_ref, east_ref, out_ref):
    rows = z.column * z.side
    west_ref[pl.ds(0, z.column, stride=z.side), :] = strip[rows : rows + z.column]
    east_ref[pl.ds(z.side - 1, z.column, stride=z.side), :] = strip[rows + z.column :]
    shape = (z.column, z.side, z.chan)
    middle = strip[:rows].reshape(shape)
    place = iota(shape, 1)
    flat = (rows, z.chan)
    left = jnp.where(place == 0, west_ref[...].reshape(shape), pltpu.roll(middle, 1, 1))
    right = jnp.where(place == z.side - 1, east_ref[...].reshape(shape), pltpu.roll(middle, z.side - 1, 1))
    out_ref[:, : z.chan] = left.reshape(flat).astype(BF16)
    out_ref[:, z.chan : 2 * z.chan] = middle.reshape(flat).astype(BF16)
    out_ref[:, 2 * z.chan :] = right.reshape(flat).astype(BF16)


def conv(z, columns_ref, w_ref):
    total = None
    for p in range(3):
        part = jnp.dot(
            columns_ref[p * z.line : p * z.line + z.pixels, :],
            w_ref[3 * p * z.chan : 3 * (p + 1) * z.chan, :],
            preferred_element_type=F32,
        )
        total = part if total is None else total + part
    return total


def silu_slope(v):
    s = 1.0 / (1.0 + jnp.exp(-v))
    return s * (1.0 + v * (1.0 - s))


def first_kernel(z, got_ref, index_ref, x_ref, w_ref, send_ref, hidden_ref, strip_ref, columns_ref, west_ref, east_ref):
    center = row_first(x_ref[...]).reshape(z.pixels, z.chan)
    strip = padded_columns(z, center, got_ref[...].reshape(z.sent, z.chan), as_column(index_ref[8:9, : z.cells_read]), west_ref, east_ref, columns_ref)
    strip_ref[...] = strip.astype(BF16)
    v = conv(z, columns_ref, w_ref)
    hidden = (v / (1.0 + jnp.exp(-v))).astype(BF16)
    send_ref[...] = gather(as_column(index_ref[0:1, : z.sent]), hidden).astype(BF16).reshape(send_ref.shape)
    hidden_ref[...] = hidden


def again_kernel(z, strip_ref, w_ref, slope_ref, columns_ref, west_ref, east_ref):
    fill_columns(z, strip_ref[...].astype(F32), west_ref, east_ref, columns_ref)
    slope_ref[...] = silu_slope(conv(z, columns_ref, w_ref))


def shifted(z, slope):
    cube = slope.reshape(slope.shape[0] // z.side, z.side, z.chan)
    place = iota(cube.shape, 1)
    after = jnp.where(place == z.side - 1, 0.0, pltpu.roll(cube, z.side - 1, 1))
    before = jnp.where(place == 0, 0.0, pltpu.roll(cube, 1, 1))
    return [part.reshape(slope.shape).astype(BF16) for part in (after, cube, before)]


def rims_back(z, slope, turned_ref, slope_ref):
    chan = z.chan
    parts = []
    for p, row in ((0, 0), (2, z.side - 1)):
        wide = jnp.concatenate(shifted(z, slope[row * z.line : (row + 1) * z.line]), axis=1)
        parts.append(jnp.dot(wide, turned_ref[3 * p * chan : 3 * (p + 1) * chan, :], preferred_element_type=F32))
    slope_ref[...] = slope
    blank = jnp.zeros((2 * z.tiles, chan), F32)
    for start, q in ((0, 0), (z.side - 1, 2)):
        line = slope_ref[pl.ds(start, z.side * z.tiles, stride=z.side), :]
        line = jnp.concatenate([blank, line, blank], axis=0).astype(BF16)
        side = None
        for p in range(3):
            part = jnp.dot(
                line[(2 - p) * z.tiles : (2 - p) * z.tiles + z.column],
                turned_ref[(3 * p + q) * chan : (3 * p + q + 1) * chan, :],
                preferred_element_type=F32,
            )
            side = part if side is None else side + part
        parts.append(side)
    parts.append(jnp.zeros((z.cells_up - z.cells, chan), F32))
    return jnp.concatenate(parts, axis=0).astype(BF16)


def inner_back(z, slope, turned_ref, wide_ref):
    chan = z.chan
    zero = jnp.zeros((z.line, 3 * chan), BF16)
    wide_ref[: z.line, :] = zero
    wide_ref[z.line + z.pixels :, :] = zero
    for q, part in enumerate(shifted(z, slope)):
        wide_ref[z.line : z.line + z.pixels, q * chan : (q + 1) * chan] = part
    total = None
    for p in range(3):
        part = jnp.dot(
            wide_ref[(2 - p) * z.line : (2 - p) * z.line + z.pixels, :],
            turned_ref[3 * p * chan : 3 * (p + 1) * chan, :],
            preferred_element_type=F32,
        )
        total = part if total is None else total + part
    return total


def second_kernel(
    z, got_ref, index_ref, hidden_ref, w_ref, turned_ref, back_ref,
    send_ref, slope_ref, out_ref, strip_ref, columns_ref, west_ref, east_ref, scratch_ref,
):
    center = hidden_ref[...].astype(F32)
    strip = padded_columns(z, center, got_ref[...].reshape(z.sent, z.chan), as_column(index_ref[8:9, : z.cells_read]), west_ref, east_ref, columns_ref)
    strip_ref[...] = strip.astype(BF16)
    v = conv(z, columns_ref, w_ref)
    s = 1.0 / (1.0 + jnp.exp(-v))
    out_ref[...] = (v * s).astype(BF16)
    push(out_ref)
    slope = (back_ref[...] * (s * (1.0 + v * (1.0 - s)))).astype(BF16)
    slope_ref[...] = slope
    push(slope_ref)
    rims = rims_back(z, slope.astype(F32), turned_ref, scratch_ref)
    send_ref[...] = gather(as_column(index_ref[16:17, : z.sent]), rims).astype(BF16).reshape(send_ref.shape)


def tap_products(z, columns_ref, slope, scale, total_ref):
    blank = jnp.zeros((2 * z.line, z.chan), BF16)
    padded = jnp.concatenate([blank, slope, blank], axis=0)
    rows = (z.side + 2) * z.line
    wide = jnp.concatenate([padded[(2 - p) * z.line : (2 - p) * z.line + rows] for p in range(3)], axis=1)
    total = mm_t(columns_ref[...], wide) * scale
    for p in range(3):
        total_ref[3 * p * z.chan : 3 * (p + 1) * z.chan, :] = total[:, p * z.chan : (p + 1) * z.chan]


def deal_parts(z, sample_ref, me_ref, source_ref, own_ref, other_refs):
    rows = own_ref.shape[0]
    for k, (shift, core) in enumerate(z.parts):
        whose = lax.rem(sample_ref[0] + shift, z.samples)
        half = jnp.bitwise_xor(me_ref[0] & 1, core)
        part = source_ref[pl.ds((2 * whose + half) * rows, rows), :]
        if k == 0:
            own_ref[...] = part
        else:
            other_refs[k - 1][...] = part.astype(BF16)


def early_kernel(
    z, scale, sample_ref, me_ref, slope_ref, hidden_ref, cot_ref, wd_ref, strip_ref, feature_ref, own_ref, *refs
):
    other_refs, (taps_ref, total_ref, flat_ref, block_ref, columns_ref, west_ref, east_ref) = refs[:-7], refs[-7:]
    chan, half = z.chan, z.side // 2
    part = half * z.tiles
    flat_ref[...] = hidden_ref[...].astype(F32)
    for i in range(half):
        for p in range(2):
            for q in range(2):
                block_ref[i * part : (i + 1) * part, (2 * p + q) * chan : (2 * p + q + 1) * chan] = flat_ref[
                    pl.ds((2 * i + p) * z.line + q, part, stride=2), :
                ].astype(BF16)
    block = block_ref[...]
    feature_ref[...] = jnp.dot(block, wd_ref[...], preferred_element_type=F32).astype(BF16)
    down = mm_t(block, cot_ref[...]) * scale
    fill_columns(z, strip_ref[...].astype(F32), west_ref, east_ref, columns_ref)
    tap_products(z, columns_ref, slope_ref[...], scale, taps_ref)
    both = z.tap_rows + z.down_rows
    for s in range(z.samples):
        total_ref[s * both : s * both + z.tap_rows, :] = taps_ref[s * z.tap_rows : (s + 1) * z.tap_rows, :]
        total_ref[s * both + z.tap_rows : (s + 1) * both, :] = down[s * z.down_rows : (s + 1) * z.down_rows]
    deal_parts(z, sample_ref, me_ref, total_ref, own_ref, other_refs)


def inner_kernel(z, slope_ref, turned_ref, inner_ref, wide_ref):
    inner_ref[...] = inner_back(z, slope_ref[...].astype(F32), turned_ref, wide_ref)


def slope_kernel(
    z, scale, sample_ref, me_ref, got_ref, pix_row_ref, inner_ref, slope_in_ref, columns_ref,
    slope_ref, own_ref, *refs,
):
    other_refs, total_ref = refs[:-1], refs[-1]
    back = inner_ref[...] + mm(pick_columns(pix_row_ref[0:1, : z.sent], z.pixels), got_ref[...].reshape(z.sent, z.chan))
    slope = (back * slope_in_ref[...]).astype(BF16)
    slope_ref[...] = slope
    tap_products(z, columns_ref, slope, scale, total_ref)
    deal_parts(z, sample_ref, me_ref, total_ref, own_ref, other_refs)


def last_kernel(z, slope_ref, turned_ref, index_ref, send_ref, scratch_ref):
    rims = rims_back(z, slope_ref[...].astype(F32), turned_ref, scratch_ref)
    send_ref[...] = gather(as_column(index_ref[16:17, : z.sent]), rims).astype(BF16).reshape(send_ref.shape)


def gain_kernel(own_ref, *refs):
    others, out_ref = refs[:-1], refs[-1]
    total = own_ref[...]
    for other in others:
        total = total + other[...].astype(F32)
    out_ref[...] = total


def join_kernel(z, rim_ref, early_ref, late_ref, *refs):
    others, (send_ref, total_ref) = refs[:-2], refs[-2:]
    late = late_ref[...]
    for other in others:
        late = late + other[...].astype(F32)
    total_ref[: z.early, :] = early_ref[...]
    total_ref[z.early : z.early + z.late, :] = late
    spare = z.devices * z.chunk - z.early - z.late
    if spare:
        total_ref[z.early + z.late :, :] = jnp.zeros((spare, z.chan), F32)
    send_ref[:, : z.pair, :] = rim_ref[...]
    send_ref[:, z.pair :, :] = total_ref[...].astype(BF16).reshape(z.devices, z.chunk, z.chan)


def sum_kernel(z, got_ref, out_ref):
    sums = []
    for core in range(2):
        first, *rest = [z.place[device] for device in range(core, z.devices, 2)]
        total = got_ref[first, z.pair :, :].astype(F32)
        for k in rest:
            total = total + got_ref[k, z.pair :, :].astype(F32)
        sums.append(total.astype(BF16))
    for k in range(z.devices // 2):
        for core in range(2):
            out_ref[k, core * z.chunk : (core + 1) * z.chunk, :] = sums[core]


def input_kernel(z, got_ref, pix_row_ref, inner_ref, out_ref):
    arrived = got_ref[:, : z.pair, :].reshape(z.sent, z.chan)
    total = inner_ref[...] + mm(pick_columns(pix_row_ref[0:1, : z.sent], z.pixels), arrived)
    for r in range(z.side):
        out_ref[:, r] = total[r * z.line : (r + 1) * z.line].reshape(z.tiles, z.side, z.chan)


def spread_kernel(z, me_ref, mine_ref, other_ref, one_ref, two_ref, low_ref):
    first = (me_ref[0] & 1) == 0
    mine, other = mine_ref[...].astype(F32), other_ref[...].astype(F32)
    halves = []
    for core in range(2):
        rows = slice(core * z.chunk, (core + 1) * z.chunk)
        a, b = mine[:, rows], other[:, rows]
        by_core = jnp.where(first, a, b), jnp.where(first, b, a)
        chunks = [by_core[device % 2][z.ring.index(device // 2)] for device in z.order]
        halves.append(jnp.concatenate(chunks, axis=0))
    one_ref[...] = jnp.concatenate([half[z.early : z.early + z.late] for half in halves], axis=0)
    push(one_ref)
    early = jnp.concatenate([half[: z.early] for half in halves], axis=0)
    two_ref[...] = early[: z.tap_rows]
    push(two_ref)
    low_ref[...] = early[z.tap_rows :]
    push(low_ref)


def vmem(*shape, dtype=F32):
    return pltpu.VMEM(shape, dtype)


class Pulled:
    def __init__(self, source, buffer, semaphore):
        self.buffer, self.shape, self.waits = buffer, buffer.shape, True
        self.copy = pltpu.make_async_copy(source, buffer, semaphore)
        self.copy.start()

    def __getitem__(self, at):
        if self.waits:
            self.copy.wait()
            self.waits = False
        return self.buffer[at]


class Pushed:
    def __init__(self, target, buffer, semaphore):
        self.buffer, self.shape, self.started = buffer, buffer.shape, False
        self.copy = pltpu.make_async_copy(buffer, target, semaphore)

    def __getitem__(self, at):
        return self.buffer[at]

    def __setitem__(self, at, value):
        self.buffer[at] = value

    def send(self):
        if not self.started:
            self.copy.start()
            self.started = True


def push(ref):
    if isinstance(ref, Pushed):
        ref.send()


def call(body, outs, scratch=(), scalars=0, fetch=0, name=None):
    def run(*operands):
        first = len(operands) - fetch
        far = [len(out) == 3 for out in outs]
        fetched = operands[first:]
        sent = [out for out in outs if len(out) == 3]
        ends = (first, fetch, len(outs), fetch, len(sent), len(scratch), 1, 1)

        def kernel(*refs):
            groups, at = [], 0
            for count in ends:
                groups.append(refs[at : at + count])
                at += count
            here, there, results, in_buffers, out_buffers, rest, (in_sems,), (out_sems,) = groups
            pulled = [Pulled(ref, in_buffers[k], in_sems.at[k]) for k, ref in enumerate(there)]
            made, pushed = [], []
            for ref, is_far in zip(results, far):
                if is_far:
                    k = len(pushed)
                    pushed.append(Pushed(ref, out_buffers[k], out_sems.at[k]))
                    ref = pushed[k]
                made.append(ref)
            body(*here, *pulled, *made, *rest)
            for ref in pushed:
                ref.send()
            for ref in pushed:
                ref.copy.wait()

        spec = pl.BlockSpec(memory_space=pltpu.VMEM)
        small = pl.BlockSpec(memory_space=pltpu.SMEM)
        apart = pl.BlockSpec(memory_space=pltpu.HBM)
        return pl.pallas_call(
            kernel,
            out_shape=[
                pltpu.HBM(out[0], out[1]) if is_far else jax.ShapeDtypeStruct(out[0], out[1])
                for out, is_far in zip(outs, far)
            ],
            in_specs=[small] * scalars + [spec] * (first - scalars) + [apart] * fetch,
            out_specs=[apart if is_far else spec for is_far in far],
            scratch_shapes=[pltpu.VMEM(x.shape, x.dtype) for x in fetched]
            + [pltpu.VMEM(out[0], out[1]) for out in sent]
            + list(scratch)
            + [pltpu.SemaphoreType.DMA((max(1, fetch),)), pltpu.SemaphoreType.DMA((max(1, len(sent)),))],
            compiler_params=pltpu.CompilerParams(vmem_limit_bytes=24 * 1024 * 1024),
            name=name,
        )(*operands[:first], *[pltpu.with_memory_space_constraint(x, pltpu.HBM) for x in fetched])

    return run


def array(*shape, dtype=F32):
    return shape, dtype


def far(*shape, dtype=F32):
    return shape, dtype, True


def exchange(x, groups):
    return lax.all_to_all(x, "tile", split_axis=0, concat_axis=0, tiled=True, axis_index_groups=groups)


def deal(others, z):
    got = []
    for k, (shift, core) in enumerate(z.parts[1:]):
        pairs = [
            (s * z.devices + t, (s + shift) % z.samples * z.devices + (t ^ core))
            for s in range(z.samples)
            for t in range(z.devices)
        ]
        got.append(lax.ppermute(others[k], ("dp", "tile"), pairs))
    return got


def local(inputs, cotangent, w_first, w_second, w_down, edge_owner, corner_owner, neighbour_tile, seam_rotation):
    tiles_in, cot = inputs[0], cotangent[0]
    tiles, side, _, chan = tiles_in.shape
    z = Sizes(tiles, side, chan, lax.axis_size("tile"), lax.axis_size("dp"))
    scale = float(z.samples * z.devices * z.pixels) ** -0.5
    me = lax.axis_index("tile").astype(I32).reshape(1)
    sample = lax.axis_index("dp").astype(I32).reshape(1)
    half = side // 2
    down_pixels = half * half * tiles
    sent = array(z.devices, z.pair, chan, dtype=BF16)
    sent_far = far(z.devices, z.pair, chan, dtype=BF16)
    field, field16 = array(z.pixels, chan), array(z.pixels, chan, dtype=BF16)
    field16_far = far(z.pixels, chan, dtype=BF16)
    columns = array(z.column * side, 3 * chan, dtype=BF16)
    wide_columns = vmem(z.column * side, 3 * chan, dtype=BF16)
    strip = array(z.column * (side + 2), chan, dtype=BF16)
    turned = array(9 * chan, chan, dtype=BF16)
    wide = vmem((side + 2) * z.line, 3 * chan, dtype=BF16)
    side_columns = (vmem(z.column * side, chan), vmem(z.column * side, chan))
    flat = vmem(z.pixels, chan)
    taps = vmem(9 * chan, chan)
    bind = functools.partial
    tables = (edge_owner.T, corner_owner.T, neighbour_tile.T, seam_rotation.T)
    others = len(z.parts) - 1
    everyone = [list(z.order)]
    same_core = [[2 * chip + core for chip in z.ring] for core in range(2)]

    (send,) = call(bind(pack_kernel, z), [sent_far], scalars=1, fetch=5, name="pack")(me, *tables, tiles_in)
    got = exchange(send, everyone)
    cot_rows = cot.transpose(1, 0, 2, 3).reshape(down_pixels, chan)
    index, back_second, turned_first, turned_second = call(
        bind(side_kernel, z),
        [
            array(24, max(z.sent, z.cells_up), dtype=I32),
            field,
            turned,
            turned,
        ],
        scalars=1,
        name="aside",
    )(me, *tables, cot_rows, w_down, w_first, w_second)
    send, hidden, strip_first = call(
        bind(first_kernel, z), [sent, field16, strip], (wide_columns,) + side_columns, name="first"
    )(got, index, tiles_in, w_first)
    got = exchange(send, everyone)
    slope_in, columns_first = call(bind(again_kernel, z), [field, columns], side_columns, name="again")(
        strip_first, w_first
    )
    send, slope_second, hidden_second, strip_second = call(
        bind(second_kernel, z), [sent_far, field16, field16, strip], (wide_columns,) + side_columns + (flat,), name="second"
    )(got, index, hidden, w_second, turned_second, back_second)
    got = exchange(send, everyone)
    (inner,) = call(bind(inner_kernel, z), [field], (wide,), name="inner")(slope_second, turned_second)
    features, early_own, *early_other = call(
        bind(early_kernel, z, scale),
        [array(down_pixels, chan, dtype=BF16), array(z.early, chan)] + [array(z.early, chan, dtype=BF16)] * others,
        (taps, vmem(2 * z.samples * z.early, chan), flat, vmem(down_pixels, 4 * chan, dtype=BF16), wide_columns)
        + side_columns,
        scalars=2,
        name="early",
    )(sample, me, slope_second, hidden_second, cot_rows, w_down, strip_second)
    features = features.reshape(half, tiles, half, chan).transpose(1, 0, 2, 3)
    (early,) = call(gain_kernel, [array(z.early, chan)], name="gain")(early_own, *deal(early_other, z))
    slope_first, late_own, *late_other = call(
        bind(slope_kernel, z, scale),
        [field16, array(z.late, chan)] + [array(z.late, chan, dtype=BF16)] * others,
        (taps,),
        scalars=2,
        name="slope",
    )(sample, me, got, index, inner, slope_in, columns_first)
    late_got = deal(late_other, z)
    (send,) = call(bind(last_kernel, z), [sent], (flat,), name="last")(slope_first, turned_first, index)
    (inner,) = call(bind(inner_kernel, z), [field], (wide,), name="inner")(slope_first, turned_first)
    send, inner, features = lax.optimization_barrier((send, inner, features))
    (send,) = call(
        bind(join_kernel, z),
        [array(z.devices, z.pair + z.chunk, chan, dtype=BF16)],
        (vmem(z.devices * z.chunk, chan),),
        name="join",
    )(send, early, late_own, *late_got)
    got = exchange(send, everyone)
    (chunk,) = call(bind(sum_kernel, z), [array(z.devices // 2, 2 * z.chunk, chan, dtype=BF16)], name="sum")(got)
    mine = exchange(chunk, same_core)
    (input_grad,) = call(bind(input_kernel, z), [array(tiles, side, side, chan)], name="input")(got, index, inner)
    other = lax.ppermute(mine, "tile", [(t, t ^ 1) for t in range(z.devices)])
    grad_first, grad_second, grad_down = call(
        bind(spread_kernel, z),
        [far(z.tap_rows, chan), far(z.tap_rows, chan), far(z.down_rows, chan)],
        scalars=1,
        name="spread",
    )(me, mine, other)
    return features[None], input_grad[None], grad_first, grad_second, grad_down


def solution(mesh):
    split = P("dp", "tile", None, None, None)
    return jax.shard_map(
        local,
        mesh=mesh,
        in_specs=(split, split, P(), P(), P(), P(), P(), P(), P()),
        out_specs=(split, split, P("dp", None), P("dp", None), P("dp", None)),
        check_vma=False,
    )
```
